32 devices in a mesh: group: 2 (over x), branch: 8 (over z, y), expert: 2 (over core).
Axes of the slice: x: 2, y: 2, z: 4, core: 2. Of those that a mesh axis runs over, the one named last changes fastest.
Arguments:
- latent_cache: bfloat16 [16, 2048, 512], P(('group', 'branch'), 'expert'), parts along dimension 0, may hold values from -4 to 4
- rope_cache: bfloat16 [16, 256, 512], P(('group', 'branch'), 'expert'), parts along dimension 0, may hold values from -4 to 4
- q_latent: bfloat16 [256, 2, 128, 512], P(('group', 'branch', 'expert')), parts along dimension 0, may hold values from -4.8 to 4.8
- q_rope: bfloat16 [256, 2, 8192], P(('group', 'branch', 'expert')), parts along dimension 0, may hold values from -192 to 192
- new_latent: bfloat16 [256, 2, 512], P(('group', 'branch', 'expert')), parts along dimension 0, may hold values from -4 to 4
- new_rope: bfloat16 [256, 2, 64], P(('group', 'branch', 'expert')), parts along dimension 0, may hold values from -4.2 to 4.2
- branch_slot: int32 [256], P(('group', 'branch', 'expert')), parts along dimension 0, may hold values from 0 to 7, as said below
- moe_input: bfloat16 [256, 2, 7168], P(('group', 'branch', 'expert')), parts along dimension 0, may hold values from -6 to 6
- routes: int32 [256, 2, 8], P(('group', 'branch', 'expert')), parts along dimension 0, may hold values from 0 to 255, as said below
- route_gate: float32 [256, 2, 8], P(('group', 'branch', 'expert')), parts along dimension 0, may hold values from 0.05 to 0.6
- w_gate: bfloat16 [16, 7168, 128], P(('branch', 'expert')), may hold values from -0.0625 to 0.0625
- w_up: bfloat16 [16, 7168, 128], P(('branch', 'expert')), may hold values from -0.0625 to 0.0625
- w_down: bfloat16 [16, 128, 7168], P(('branch', 'expert')), may hold values from -0.1875 to 0.1875
Outputs:
- attended: bfloat16 [256, 2, 128, 512], P(('group', 'branch', 'expert')), parts along dimension 0
- moe_out: bfloat16 [256, 2, 7168], P(('group', 'branch', 'expert')), parts along dimension 0
The draws below stay inside these ranges and needn't reach their ends.
There are 2 independent parts, one for each index of `group`. The reference program is written for one: setup_inputs(seed, part) draws one part's arguments, and reference() takes and returns one part's arrays. A program takes and returns all parts, laid end to end along the dimension named above; an argument that names none is the same for every part. Nothing has to cross between parts.
Inputs may be any that keep to these rules, and one draw needn't show every extreme that they name: `branch_slot`: among the 8 tokens of one device every number from 0 to 7 stands exactly once. `routes`: each row (a token at a step) names 8 different experts, at most one of them below 2; within the 16 rows of one device no expert below 2 is named more than 2 times, and some one exactly 2 times.
All inputs are finite; a program needn't handle non-finite values.
Results may differ from the reference program's by a relative error of at most 0.0057.
Values may be sent and summed in bfloat16 or wider, within the bound.
No kernel may reach another device: no remote copies, remote signals or barrier semaphores. Data moves between devices by JAX's collectives and lax.ppermute only.
A program may use at most 192 MiB of HBM per device.

```python
import math
import jax
import jax.numpy as jnp
from jax import lax

D = 7168
HEADS = 128
LAT = 512
ROPE = 64
ALL_EXPERTS = 256
EXP_HID = 1024
SHARDS = 8
TOPK = 8
STEPS = 2
BRANCHES = 16
BLOCK = 8
LEN = 2048
OUTLINES = 8
TOKENS = 128
EXPERTS = 2
CAP = 2


def draw_branch_slot(key, part):
    devices = TOKENS // BLOCK
    scores = jax.random.randint(jax.random.fold_in(key, 11), (devices, BLOCK), 0, 1 << 20)
    scores = scores * BLOCK + jnp.arange(BLOCK, dtype=jnp.int32)[None, :]
    return jnp.argsort(scores, axis=1).astype(jnp.int32).reshape(TOKENS)


def draw_routes(key, part):
    devices = TOKENS // BLOCK
    row_count = STEPS * BLOCK
    others = ALL_EXPERTS - EXPERTS
    keys = jax.random.split(jax.random.fold_in(key, 37), 5)
    scores = jax.random.randint(keys[0], (devices, row_count, others), 0, 1 << 20)
    scores = scores * others + jnp.arange(others, dtype=jnp.int32)[None, None, :]
    unused, picks = lax.top_k(scores, TOPK)
    picks = (picks % others + EXPERTS).astype(jnp.int32)
    order_scores = jax.random.randint(keys[1], (devices, EXPERTS), 0, 1 << 20) * EXPERTS + jnp.arange(EXPERTS, dtype=jnp.int32)[None, :]
    expert_order = jnp.argsort(order_scores, axis=1).astype(jnp.int32)
    row_scores = jax.random.randint(keys[2], (devices, row_count), 0, 1 << 20) * row_count + jnp.arange(row_count, dtype=jnp.int32)[None, :]
    row_order = jnp.argsort(row_scores, axis=1).astype(jnp.int32)
    rank = jnp.argsort(row_order, axis=1).astype(jnp.int32)
    pair = rank // CAP
    kept = (pair < EXPERTS) & ((rank < CAP) | (jax.random.randint(keys[3], (devices, row_count), 0, 8) < 7))
    computed = jnp.take_along_axis(expert_order, jnp.minimum(pair, EXPERTS - 1), axis=1)
    where_slot = jax.random.randint(keys[4], (devices, row_count), 0, TOPK)
    column = jnp.arange(TOPK, dtype=jnp.int32)[None, None, :]
    replace = kept[:, :, None] & (column == where_slot[:, :, None])
    chosen = jnp.where(replace, computed[:, :, None], picks)
    return chosen.reshape(TOKENS, STEPS, TOPK).astype(jnp.int32)


def shared_draws(key, part):
    keys = jax.random.split(jax.random.fold_in(key, 23), 5)
    rope = jnp.clip(jax.random.normal(keys[0], (OUTLINES, LEN, ROPE), jnp.float32), -4.0, 4.0)
    rope_new = jnp.clip(jax.random.normal(keys[1], (TOKENS, STEPS, ROPE), jnp.float32), -4.0, 4.0)
    latent_new = jnp.clip(jax.random.normal(keys[2], (TOKENS, STEPS, LAT), jnp.float32), -4.0, 4.0)
    query_rope = jnp.clip(jax.random.normal(keys[3], (TOKENS, STEPS, HEADS, ROPE), jnp.float32), -4.0, 4.0)
    query_lat = jnp.clip(jax.random.normal(keys[4], (TOKENS, STEPS, HEADS, LAT), jnp.float32), -4.0, 4.0)
    query_lat = query_lat + 0.2 * latent_new[:, :, None, :]
    return (rope, rope_new, latent_new, query_rope, query_lat)


def draw_rope_cache(key, part):
    return shared_draws(key, part)[0].reshape(OUTLINES, LEN // 8, 8 * ROPE).astype(jnp.bfloat16)


def draw_new_rope(key, part):
    return shared_draws(key, part)[1].astype(jnp.bfloat16)


def draw_new_latent(key, part):
    return shared_draws(key, part)[2].astype(jnp.bfloat16)


def draw_q_rope(key, part):
    return shared_draws(key, part)[3].reshape(TOKENS, STEPS, HEADS * ROPE).astype(jnp.bfloat16)


def draw_q_latent(key, part):
    return shared_draws(key, part)[4].astype(jnp.bfloat16)


def steps_of(key, dims, pieces, low, largest):
    level = 1.0
    for dim, blocks in pieces:
        heights = jax.random.uniform(jax.random.fold_in(jax.random.fold_in(key, 6), dim), (blocks,), jnp.float32, low / len(pieces), largest / len(pieces))
        level = level * jnp.repeat(jnp.exp(heights), dims[dim] // blocks).reshape((-1,) + (1,) * (len(dims) - 1 - dim))
    return level


def normal_values(rng, dims, scale, limit, shards=(), held_as=jnp.bfloat16):
    gain = steps_of(rng, dims, shards, -0.22, 0.18) if shards else 1.0
    drawn = jax.random.normal(rng, dims, jnp.float32) * scale * gain
    return jnp.minimum(jnp.maximum(drawn, -limit), limit).astype(held_as)


def setup_inputs(seed: int = 0, part: int = 0) -> dict:
    key_list = jax.random.split(jax.random.key(seed), 14)
    part_splits = jax.random.split(jax.random.fold_in(key_list[13], part), 14)
    return {
        "latent_cache": normal_values(part_splits[0], (OUTLINES, LEN, LAT), 1.0, 4.0, ((0, 8), (1, 2))),
        "rope_cache": draw_rope_cache(jax.random.fold_in(jax.random.fold_in(key_list[13], part), 71), part),
        "q_latent": draw_q_latent(jax.random.fold_in(jax.random.fold_in(key_list[13], part), 71), part),
        "q_rope": draw_q_rope(jax.random.fold_in(jax.random.fold_in(key_list[13], part), 71), part),
        "new_latent": draw_new_latent(jax.random.fold_in(jax.random.fold_in(key_list[13], part), 71), part),
        "new_rope": draw_new_rope(jax.random.fold_in(jax.random.fold_in(key_list[13], part), 71), part),
        "branch_slot": draw_branch_slot(jax.random.fold_in(jax.random.fold_in(key_list[13], part), 71), part),
        "moe_input": normal_values(part_splits[7], (TOKENS, STEPS, D), 1.0, 6.0, ((0, 16),)),
        "routes": draw_routes(jax.random.fold_in(jax.random.fold_in(key_list[13], part), 71), part),
        "route_gate": jnp.clip(jnp.exp(math.log(0.6) - 2.4849067 * jax.random.uniform(part_splits[9], (TOKENS, STEPS, TOPK), jnp.float32) ** steps_of(part_splits[9], (TOKENS, STEPS, TOPK), ((0, 16),), -0.2, 0.2)), 0.05, 0.6),
        "w_gate": normal_values(key_list[10], (EXPERTS * SHARDS, D, EXP_HID // SHARDS), D ** -0.5, 0.0625, ((0, 16),)),
        "w_up": normal_values(key_list[11], (EXPERTS * SHARDS, D, EXP_HID // SHARDS), D ** -0.5, 0.0625, ((0, 16),)),
        "w_down": normal_values(key_list[12], (EXPERTS * SHARDS, EXP_HID // SHARDS, D), EXP_HID ** -0.5, 0.1875, ((0, 16),)),
    }


softmax_scale = 192.0 ** -0.5


def cache_partial(query_lat, query_rope, keys_lat, keys_rope):
    highest = lax.Precision.HIGHEST
    scores = jnp.einsum("tshc,pc->tshp", query_lat, keys_lat, precision=highest)
    scores = scores + jnp.einsum("tshr,pr->tshp", query_rope, keys_rope, precision=highest)
    scores = scores * softmax_scale
    cache_peak = jnp.max(scores, axis=-1)
    exponent = jnp.exp(scores - cache_peak[..., None])
    totals = jnp.sum(exponent, axis=-1)
    weights = lax.optimization_barrier(exponent.astype(jnp.bfloat16)).astype(jnp.float32)
    summed = jnp.einsum("tshp,pc->tshc", weights, keys_lat, precision=highest)
    return cache_peak, totals, summed


def expert_ffn(packed):
    arrived, gate_matrix, up_matrix, down_matrix = packed
    highest = lax.Precision.HIGHEST
    inputs = arrived.astype(jnp.float32)
    gate_value = jnp.einsum("rd,jdh->jrh", inputs, gate_matrix.astype(jnp.float32), precision=highest)
    lifted = jnp.einsum("rd,jdh->jrh", inputs, up_matrix.astype(jnp.float32), precision=highest)
    hidden = lax.optimization_barrier((jax.nn.silu(gate_value) * lifted).astype(jnp.bfloat16)).astype(jnp.float32)
    parts = jnp.einsum("jrh,jhd->jrd", hidden, down_matrix.astype(jnp.float32), precision=highest)
    parts = lax.optimization_barrier(parts.astype(jnp.bfloat16)).astype(jnp.float32)
    return jnp.sum(parts, axis=0)


def reference(latent_cache, rope_cache, q_latent, q_rope, new_latent, new_rope, branch_slot, moe_input, routes, route_gate, w_gate, w_up, w_down):
    highest = lax.Precision.HIGHEST
    token_ids = jnp.arange(TOKENS, dtype=jnp.int32)
    outline = (BLOCK * (token_ids // (BRANCHES * BLOCK)) + branch_slot).astype(jnp.int32)
    members = jnp.argsort(outline, stable=True).astype(jnp.int32).reshape(OUTLINES, BRANCHES)
    query_rope_all = q_rope.reshape(TOKENS, STEPS, HEADS, ROPE)
    rope_keys = rope_cache.reshape(OUTLINES, LEN, ROPE)

    def per_outline(outline_index):
        chosen = members[outline_index]
        query_lat = jnp.take(q_latent, chosen, axis=0).astype(jnp.float32)
        query_rope = jnp.take(query_rope_all, chosen, axis=0).astype(jnp.float32)
        keys_lat = latent_cache[outline_index].astype(jnp.float32)
        keys_rope = rope_keys[outline_index].astype(jnp.float32)
        return cache_partial(query_lat, query_rope, keys_lat, keys_rope)

    cache_peak, totals, summed = lax.map(per_outline, jnp.arange(OUTLINES, dtype=jnp.int32))
    position_of = jnp.zeros((TOKENS,), jnp.int32).at[members.reshape(-1)].set(token_ids)
    cache_peak = jnp.take(cache_peak.reshape((TOKENS,) + cache_peak.shape[2:]), position_of, axis=0)
    totals = jnp.take(totals.reshape((TOKENS,) + totals.shape[2:]), position_of, axis=0)
    summed = jnp.take(summed.reshape((TOKENS,) + summed.shape[2:]), position_of, axis=0)
    cache_out = lax.optimization_barrier((summed / totals[..., None]).astype(jnp.bfloat16)).astype(jnp.float32)
    cache_lse = cache_peak + jnp.log(totals)

    latent_own = new_latent.astype(jnp.float32)
    own_scores = jnp.einsum("tshc,tjc->tshj", q_latent.astype(jnp.float32), latent_own, precision=highest)
    own_scores = own_scores + jnp.einsum("tshr,tjr->tshj", query_rope_all.astype(jnp.float32), new_rope.astype(jnp.float32), precision=highest)
    own_scores = own_scores * softmax_scale
    causal = (jnp.arange(STEPS)[None, :] <= jnp.arange(STEPS)[:, None])[None, :, None, :]
    own_peak = jnp.max(jnp.where(causal, own_scores, -1e30), axis=-1)
    own_weight = jnp.where(causal, jnp.exp(own_scores - own_peak[..., None]), 0.0)
    own_total = jnp.sum(own_weight, axis=-1)
    own_sum = jnp.einsum("tshj,tjc->tshc", own_weight, latent_own, precision=highest)
    top_value = jnp.maximum(cache_lse, own_peak)
    factor = jnp.exp(cache_lse - top_value)
    own_factor = jnp.exp(own_peak - top_value)
    numerator = factor[..., None] * cache_out + own_factor[..., None] * own_sum
    denominator = factor + own_factor * own_total
    attended = (numerator / denominator[..., None]).astype(jnp.bfloat16)

    devices = TOKENS // BLOCK
    per_device = STEPS * BLOCK * TOPK
    slot_total = EXPERTS * devices * CAP
    flat_routes = routes.reshape(devices, per_device).astype(jnp.int32)
    inside = flat_routes < EXPERTS
    onehot = (flat_routes[:, :, None] == jnp.arange(EXPERTS, dtype=jnp.int32)[None, None, :]).astype(jnp.int32)
    position = jnp.sum((jnp.cumsum(onehot, axis=1) - onehot) * onehot, axis=2)
    slot_index = flat_routes * (devices * CAP) + jnp.arange(devices, dtype=jnp.int32)[:, None] * CAP + position
    slot_index = jnp.where(inside, slot_index, slot_total).reshape(-1).astype(jnp.int32)
    rows_flat = moe_input.reshape(TOKENS * STEPS, D)
    source = jnp.repeat(rows_flat, TOPK, axis=0)
    buffer = jnp.zeros((slot_total, D), jnp.bfloat16).at[slot_index].set(source, mode="drop")
    hid_block = EXP_HID // SHARDS
    outputs = lax.map(expert_ffn, (buffer.reshape(EXPERTS, devices * CAP, D),
                                   w_gate.reshape(EXPERTS, SHARDS, D, hid_block),
                                   w_up.reshape(EXPERTS, SHARDS, D, hid_block),
                                   w_down.reshape(EXPERTS, SHARDS, hid_block, D)))
    safe_index = jnp.minimum(slot_index, slot_total - 1).astype(jnp.int32)
    picked = jnp.take(outputs.reshape(-1, D), safe_index, axis=0).reshape(TOKENS * STEPS, TOPK, D)
    gate_used = jnp.where(inside.reshape(TOKENS * STEPS, TOPK), route_gate.reshape(TOKENS * STEPS, TOPK), 0.0)
    combined = jnp.sum(gate_used[:, :, None] * picked, axis=1)
    moe_out = combined.astype(jnp.bfloat16).reshape(TOKENS, STEPS, D)
    return attended, moe_out
```

```python
import functools

import jax
import jax.numpy as jnp
from jax import lax
from jax.experimental import pallas as pl
from jax.experimental.pallas import tpu as pltpu
from jax.sharding import PartitionSpec as P

SHARDS = 8
CAP = 2
LANES = 128
PAD = 16

softmax_scale = 192.0 ** (-0.5)
log2e = 1.4426950408889634


def swapped(x, axis, bit):
    return lax.ppermute(x, axis, [(i, i ^ 1 << bit) for i in range(lax.axis_size(axis))])


def line_hop(x, block, moves):
    pairs = []
    for base in range(0, lax.axis_size("branch"), block):
        for low in range(2):
            pairs += [(base + 2 * i + low, base + 2 * j + low) for i, j in moves]
    return lax.ppermute(x, "branch", pairs)


def pack_cache_kernel(lat_ref, rope_ref, out_ref, sems):
    rows = lat_ref.shape[0]
    first = pltpu.make_async_copy(lat_ref, out_ref.at[pl.ds(0, rows)], sems.at[0])
    second = pltpu.make_async_copy(
        rope_ref, out_ref.at[pl.ds(rows, rope_ref.shape[0])], sems.at[1]
    )
    first.start()
    second.start()
    first.wait()
    second.wait()


def pack_cache(lat, rope):
    return pl.pallas_call(
        pack_cache_kernel,
        out_shape=jax.ShapeDtypeStruct((lat.shape[0] + rope.shape[0], lat.shape[1]), lat.dtype),
        in_specs=[pl.BlockSpec(memory_space=pl.ANY)] * 2,
        out_specs=pl.BlockSpec(memory_space=pl.ANY),
        scratch_shapes=[pltpu.SemaphoreType.DMA((2,))],
        cost_estimate=pl.CostEstimate(flops=0, bytes_accessed=2 * 2 * lat.size, transcendentals=0),
        name="pack_cache",
    )(lat, rope)


def pack_queries_kernel(stay_row, leave_row, q_ref, rope_ref, new_ref, stay_ref, leave_ref, sems):
    slots = stay_ref.shape[0]
    copies = []
    for out, rows, group in ((leave_ref, leave_row, 0), (stay_ref, stay_row, 1)):
        for slot in range(slots):
            start = 0
            for part, source in enumerate((q_ref, rope_ref, new_ref)):
                count = source.shape[1]
                copies.append(
                    pltpu.make_async_copy(
                        source.at[rows[slot]],
                        out.at[slot, pl.ds(start, count)],
                        sems.at[group, slot, part],
                    )
                )
                start += count
    for copy in copies:
        copy.start()
    for copy in copies:
        copy.wait()


def pack_queries(stay_row, leave_row, q_lat, q_rope, new):
    slots = stay_row.shape[0]
    rows = q_lat.shape[1] + q_rope.shape[1] + new.shape[1]
    shape = jax.ShapeDtypeStruct((slots, rows, q_lat.shape[2]), q_lat.dtype)
    return pl.pallas_call(
        pack_queries_kernel,
        out_shape=(shape, shape),
        in_specs=[pl.BlockSpec(memory_space=pltpu.SMEM)] * 2
        + [pl.BlockSpec(memory_space=pl.ANY)] * 3,
        out_specs=(pl.BlockSpec(memory_space=pl.ANY),) * 2,
        scratch_shapes=[pltpu.SemaphoreType.DMA((2, slots, 3))],
        cost_estimate=pl.CostEstimate(flops=0, bytes_accessed=4 * q_lat.size, transcendentals=0),
        name="pack_queries",
    )(stay_row, leave_row, q_lat, q_rope, new)


def spread_matrix(raw_rows, width):
    per_row = width // (LANES // 2)
    blocks = width // LANES
    shape = (raw_rows * per_row, raw_rows * blocks)
    row = lax.broadcasted_iota(jnp.int32, shape, 0)
    column = lax.broadcasted_iota(jnp.int32, shape, 1)
    wanted = ((row % per_row) // 2) * raw_rows + row // per_row
    return (column == wanted).astype(jnp.bfloat16)


def spread(matrix, raw):
    blocks = raw.shape[1] // LANES
    stacked = jnp.concatenate(
        [raw[:, b * LANES : (b + 1) * LANES] for b in range(blocks)], axis=0
    )
    rows = jnp.dot(matrix, stacked, preferred_element_type=jnp.float32)
    row = lax.broadcasted_iota(jnp.int32, rows.shape, 0)
    lane = lax.broadcasted_iota(jnp.int32, rows.shape, 1)
    return jnp.where(row % 2 == lane // (LANES // 2), rows, 0.0)


def build_attend(heads, steps, width, half, rope_rows, raw_group):
    q_rows = heads * steps
    token_rope = q_rows // 8

    def one_token(q_ref, keys):
        lat = q_ref[0:q_rows, :]
        matrix = spread_matrix(raw_group, width)
        pieces = []
        for start in range(0, token_rope, raw_group):
            part = spread(matrix, q_ref[q_rows + start : q_rows + start + raw_group, :])
            pieces.append(part + pltpu.roll(part, LANES // 2, 1))
        rope = pieces[0] if len(pieces) == 1 else jnp.concatenate(pieces, axis=0)
        rope = rope.astype(jnp.bfloat16)
        query = jnp.concatenate([lat, rope], axis=1)
        contract = (((1,), (1,)), ((), ()))
        scores = lax.dot_general(query, keys[...], contract, preferred_element_type=jnp.float32)
        peak = jnp.max(scores, axis=1, keepdims=True)
        base = q_rows + token_rope
        fresh = q_ref[base : base + PAD, :]
        fresh_rope = q_ref[base + PAD : base + 2 * PAD, 0:LANES]
        own = lax.dot_general(lat, fresh, contract, preferred_element_type=jnp.float32)
        own = own + lax.dot_general(rope, fresh_rope, contract, preferred_element_type=jnp.float32)
        factor = softmax_scale * log2e
        weights = jnp.exp2(scores * factor - peak * factor)
        total = jnp.sum(weights, axis=1, keepdims=True)
        summed = jnp.dot(
            weights.astype(jnp.bfloat16), keys[:, 0:width], preferred_element_type=jnp.float32
        )
        row_step = lax.broadcasted_iota(jnp.int32, (q_rows, 1), 0) // heads
        columns = [
            jnp.where(row_step >= j, own[:, j : j + 1], -1e30) for j in range(steps)
        ]
        top = peak
        for column in columns:
            top = jnp.maximum(top, column)
        share = jnp.exp2((peak - top) * factor)
        numerator = summed * share
        denominator = total * share
        fresh32 = fresh.astype(jnp.float32)
        for j, column in enumerate(columns):
            weight = jnp.where(row_step >= j, jnp.exp2((column - top) * factor), 0.0)
            numerator = numerator + weight * fresh32[j : j + 1, :]
            denominator = denominator + weight
        return (numerator / denominator).astype(jnp.bfloat16)

    def load_keys(caches, keys, sems):
        copies = []
        for i, cache in enumerate(caches):
            copies.append(
                pltpu.make_async_copy(
                    cache.at[pl.ds(0, half)],
                    keys.at[pl.ds(i * half, half), pl.ds(0, width)],
                    sems.at[i],
                )
            )
        for copy in copies:
            copy.start()
        return copies

    def spread_keys(rope_scratch, keys):
        matrix = spread_matrix(raw_group, width)
        grown = raw_group * width // (LANES // 2)
        for i in range(2):
            for start in range(0, rope_rows, raw_group):
                part = spread(matrix, rope_scratch[i, start : start + raw_group, :])
                first = i * half + start * (width // (LANES // 2))
                keys[first : first + grown, width : width + LANES] = part.astype(jnp.bfloat16)

    def kernel(kinds, n_arrived, has_placed, *refs):
        refs = list(refs)
        index = refs.pop(0)
        queries = [refs.pop(0) for _ in kinds]
        caches = [refs.pop(0) for _ in range(2)]
        arrived = [refs.pop(0) for _ in range(n_arrived)]
        if has_placed:
            refs.pop(0)
        gives = [refs.pop(0) for kind in kinds if kind == "give"]
        placed = refs.pop(0) if ("keep" in kinds or n_arrived) else None
        keys, rope_scratch, result, sems, place_sems = refs
        copies = load_keys(caches, keys, sems)
        rope_copies = []
        for i in range(2):
            copy = pltpu.make_async_copy(
                caches[i].at[pl.ds(half, rope_rows)], rope_scratch.at[i], sems.at[2 + i]
            )
            copy.start()
            rope_copies.append(copy)
        placing = []
        for i, source in enumerate(arrived):
            copy = pltpu.make_async_copy(source, placed.at[index[1 + i]], place_sems.at[1 + i])
            copy.start()
            placing.append(copy)
        for copy in rope_copies:
            copy.wait()
        spread_keys(rope_scratch, keys)
        for copy in copies:
            copy.wait()
        for kind, query in zip(kinds, queries):
            value = one_token(query.at[0], keys)
            if kind == "give":
                gives.pop(0)[...] = value
            else:
                result[...] = value
                copy = pltpu.make_async_copy(result, placed.at[index[0]], place_sems.at[0])
                copy.start()
                placing.append(copy)
        for copy in placing:
            copy.wait()

    def call(index, kinds, slot, packed, caches, arrived, placed, count):
        n_tok = len(kinds)
        rows = packed[0].shape[1]
        any_spec = pl.BlockSpec(memory_space=pl.ANY)
        in_specs = [pl.BlockSpec(memory_space=pltpu.SMEM)]
        in_specs += [
            pl.BlockSpec((1, rows, width), lambda i: (slot, 0, 0)) for _ in range(n_tok)
        ]
        in_specs += [any_spec] * (2 + len(arrived))
        operands = [index, *packed, *caches, *arrived]
        has_placed = placed is not None
        out_shape, out_specs, alias = [], [], {}
        for kind in kinds:
            if kind == "give":
                out_shape.append(jax.ShapeDtypeStruct((q_rows, width), jnp.bfloat16))
                out_specs.append(pl.BlockSpec((q_rows, width), lambda i: (0, 0)))
        if "keep" in kinds or arrived:
            out_shape.append(jax.ShapeDtypeStruct((count, q_rows, width), jnp.bfloat16))
            out_specs.append(any_spec)
            if has_placed:
                alias = {len(operands): len(out_shape) - 1}
        if has_placed:
            in_specs.append(any_spec)
            operands.append(placed)
        all_rows = 2 * half
        return pl.pallas_call(
            functools.partial(kernel, kinds, len(arrived), has_placed),
            grid=(1,),
            out_shape=tuple(out_shape),
            in_specs=in_specs,
            out_specs=tuple(out_specs),
            scratch_shapes=[
                pltpu.VMEM((all_rows, width + LANES), jnp.bfloat16),
                pltpu.VMEM((2, rope_rows, width), jnp.bfloat16),
                pltpu.VMEM((q_rows, width), jnp.bfloat16),
                pltpu.SemaphoreType.DMA((4,)),
                pltpu.SemaphoreType.DMA((1 + max(1, len(arrived)),)),
            ],
            input_output_aliases=alias,
            cost_estimate=pl.CostEstimate(
                flops=2 * n_tok * q_rows * all_rows * (2 * width + LANES),
                bytes_accessed=2 * all_rows * (width + LANES) + 4 * n_tok * q_rows * width,
                transcendentals=n_tok * q_rows * all_rows,
            ),
            compiler_params=pltpu.CompilerParams(vmem_limit_bytes=32 * 1024 * 1024),
            name="attend_" + "_".join(kinds),
        )(*operands)

    return call


def place_kernel(index, source, before, placed, sem):
    copy = pltpu.make_async_copy(source, placed.at[index[0]], sem)
    copy.start()
    copy.wait()


def place(index, source, placed):
    return pl.pallas_call(
        place_kernel,
        out_shape=jax.ShapeDtypeStruct(placed.shape, placed.dtype),
        in_specs=[pl.BlockSpec(memory_space=pltpu.SMEM)]
        + [pl.BlockSpec(memory_space=pl.ANY)] * 2,
        out_specs=pl.BlockSpec(memory_space=pl.ANY),
        scratch_shapes=[pltpu.SemaphoreType.DMA],
        input_output_aliases={2: 0},
        name="place",
    )(index, source, placed)


def dispatch_kernel(experts, block_ref, routes_ref, gate_ref, tokens_ref, out_ref, share_ref):
    block = block_ref[0]
    routes = routes_ref[...]
    gates = gate_ref[...]
    rows = routes.shape[0]
    down = lax.broadcasted_iota(jnp.int32, (rows, rows), 0)
    across = lax.broadcasted_iota(jnp.int32, (rows, rows), 1)
    same = (down == across).astype(jnp.float32)
    slots = experts * CAP
    slot_row = lax.broadcasted_iota(jnp.int32, (slots, rows), 0)
    slot_column = lax.broadcasted_iota(jnp.int32, (rows, slots), 1)
    placing = jnp.zeros((slots, rows), jnp.float32)
    share = jnp.zeros((rows, slots), jnp.float32)
    for k in range(experts):
        expert = lax.rem(block + k, experts)
        hit = routes == expert
        has = jnp.sum(hit.astype(jnp.float32), axis=1, keepdims=True)
        weight = jnp.sum(jnp.where(hit, gates, 0.0), axis=1, keepdims=True)
        has_row = jnp.sum(has * same, axis=0, keepdims=True)
        before_row = jnp.sum(jnp.where(down < across, has, 0.0), axis=0, keepdims=True)
        before = jnp.sum(jnp.where(across < down, has_row, 0.0), axis=1, keepdims=True)
        for c in range(CAP):
            slot = k * CAP + c
            placing += jnp.where((slot_row == slot) & (before_row == c), has_row, 0.0)
            share += jnp.where((slot_column == slot) & (before == c), weight, 0.0)
    out_ref[...] = jnp.dot(
        placing.astype(jnp.bfloat16), tokens_ref[...], preferred_element_type=jnp.float32
    ).astype(jnp.bfloat16)
    share_ref[...] = share


def dispatch(block, routes, gates, tokens, experts):
    slots = experts * CAP
    return pl.pallas_call(
        functools.partial(dispatch_kernel, experts),
        out_shape=(
            jax.ShapeDtypeStruct((slots, tokens.shape[1]), tokens.dtype),
            jax.ShapeDtypeStruct((tokens.shape[0], slots), jnp.float32),
        ),
        in_specs=[pl.BlockSpec(memory_space=pltpu.SMEM)]
        + [pl.BlockSpec(memory_space=pltpu.VMEM)] * 3,
        out_specs=(pl.BlockSpec(memory_space=pltpu.VMEM),) * 2,
        cost_estimate=pl.CostEstimate(
            flops=2 * slots * tokens.size, bytes_accessed=3 * tokens.size, transcendentals=0
        ),
        name="dispatch",
    )(block, routes, gates, tokens)


def on_device(
    latent_cache,
    rope_cache,
    q_latent,
    q_rope,
    new_latent,
    new_rope,
    branch_slot,
    moe_input,
    routes,
    route_gate,
    w_gate,
    w_up,
    w_down,
):
    tok_rows, step_count, head_count, width = q_latent.shape
    rope_width = new_rope.shape[-1]
    line = tok_rows // 2
    q_rows = step_count * head_count
    half = latent_cache.shape[1]
    rope_rows = rope_cache.shape[1]
    branch = lax.axis_index("branch")
    own = branch % tok_rows
    low = own % 2
    high = own // 2
    middle = jnp.logical_and(high > 0, high < line - 1)

    outer = [(i, i ^ 1) for i in range(line)]
    inner = [(i, i + 1) for i in range(1, line - 1, 2)]
    inner = inner + [(j, i) for i, j in inner]
    outward = [(i, i ^ 1) for i in range(1, line - 1)]
    own_cache = pack_cache(latent_cache[0], rope_cache[0])
    cache_a = line_hop(own_cache, tok_rows, outer)
    first_b = line_hop(own_cache, tok_rows, inner)
    second_b = line_hop(first_b, tok_rows, outward)
    first_c = line_hop(cache_a, tok_rows, inner)
    second_c = line_hop(first_c, tok_rows, outward)
    cache_b = jnp.where(middle, first_b, second_b)
    cache_c = jnp.where(middle, first_c, second_c)
    caches = [own_cache, cache_a, cache_b, cache_c]
    caches = [(cache, swapped(cache, "expert", 0)) for cache in caches]

    nearer = jnp.where(high < line // 2, line // 2, line // 2 - 1)
    farther = jnp.where(high < line // 2, line - 1, 0)
    order = jnp.stack([high, high ^ 1, nearer, farther])
    row_of = jnp.sum(
        jnp.where(
            branch_slot[None, :] == jnp.arange(tok_rows, dtype=jnp.int32)[:, None],
            jnp.arange(tok_rows, dtype=jnp.int32)[None, :],
            0,
        ),
        axis=1,
    )
    stay_row = row_of[2 * order + low]
    leave_row = row_of[2 * order + 1 - low]

    q_lat = q_latent.reshape(tok_rows, q_rows, width)
    rope_raw = q_rope.reshape(tok_rows, q_rows * rope_width // width, width)
    fresh = jnp.concatenate(
        [
            jnp.pad(new_latent, ((0, 0), (0, PAD - step_count), (0, 0))),
            jnp.pad(new_rope, ((0, 0), (0, PAD - step_count), (0, width - rope_width))),
        ],
        axis=1,
    )
    stay, leave = pack_queries(stay_row, leave_row, q_lat, rope_raw, fresh)
    guest = swapped(leave, "branch", 0)

    attend = build_attend(head_count, step_count, width, half, rope_rows, 32)
    placed = None
    waiting = []
    for slot in range(line):
        index = jnp.stack([stay_row[slot]] + [leave_row[s] for s, _ in waiting])
        arrived = [value for _, value in waiting]
        if slot < line - 1:
            given, placed = attend(
                index,
                ("give", "keep"),
                slot,
                (guest, stay),
                caches[slot],
                arrived,
                placed,
                tok_rows,
            )
        else:
            (given,) = attend(index, ("give",), slot, (guest,), caches[slot], [], None, tok_rows)
            (placed,) = attend(
                index, ("keep",), slot, (stay,), caches[slot], arrived, placed, tok_rows
            )
        waiting = [(slot, swapped(given, "branch", 0))]
    placed = place(leave_row[line - 1 :], waiting[0][1], placed)
    attended = placed.reshape(tok_rows, step_count, head_count, width)

    model_width = moe_input.shape[-1]
    tok_total = tok_rows * step_count
    device = branch * lax.axis_size("expert") + lax.axis_index("expert")
    experts = lax.axis_size("branch") * lax.axis_size("expert") // SHARDS
    cores = lax.axis_size("expert")
    shard_branches = SHARDS // cores
    block = device // SHARDS
    outgoing, share = dispatch(
        block[None],
        routes.reshape(tok_total, -1),
        route_gate.reshape(tok_total, -1),
        moe_input.reshape(tok_total, model_width),
        experts,
    )

    def to_block(x, shift):
        count = lax.axis_size("branch")
        return lax.ppermute(
            x, "branch", [(i, (i + shift * shard_branches) % count) for i in range(count)]
        )

    rows = [outgoing[:CAP]]
    for k in range(1, experts):
        rows.append(to_block(outgoing[k * CAP : (k + 1) * CAP], k))
    rows = jnp.concatenate(rows, axis=0)
    bits = [("branch", b) for b in reversed(range(shard_branches.bit_length() - 1))]
    bits += [("expert", b) for b in reversed(range(cores.bit_length() - 1))]
    for axis, bit in bits:
        rows = jnp.concatenate([rows, swapped(rows, axis, bit)], axis=0)
    gate_value = jnp.dot(rows, w_gate[0], preferred_element_type=jnp.float32)
    lifted = jnp.dot(rows, w_up[0], preferred_element_type=jnp.float32)
    hidden = (jax.nn.silu(gate_value) * lifted).astype(jnp.bfloat16)
    parts = jnp.dot(hidden, w_down[0], preferred_element_type=jnp.float32)
    for axis, bit in reversed(bits):
        count = parts.shape[0] // 2
        parts = parts[:count] + swapped(
            parts[count:].astype(jnp.bfloat16), axis, bit
        ).astype(jnp.float32)
    sums = [parts[:CAP]]
    for k in range(1, experts):
        sums.append(to_block(parts[k * CAP : (k + 1) * CAP], -k))
    sums = jnp.concatenate(sums, axis=0)
    combined = jnp.sum(share[:, :, None] * sums[None, :, :], axis=1)
    moe_out = combined.astype(jnp.bfloat16).reshape(tok_rows, step_count, model_width)
    return (attended, moe_out)


def solution(mesh):
    return jax.shard_map(
        on_device,
        mesh=mesh,
        in_specs=(
            P(("group", "branch"), "expert", None),
            P(("group", "branch"), "expert", None),
            P(("group", "branch", "expert"), None, None, None),
            P(("group", "branch", "expert"), None, None),
            P(("group", "branch", "expert"), None, None),
            P(("group", "branch", "expert"), None, None),
            P(("group", "branch", "expert")),
            P(("group", "branch", "expert"), None, None),
            P(("group", "branch", "expert"), None, None),
            P(("group", "branch", "expert"), None, None),
            P(("branch", "expert"), None, None),
            P(("branch", "expert"), None, None),
            P(("branch", "expert"), None, None),
        ),
        out_specs=(
            P(("group", "branch", "expert"), None, None, None),
            P(("group", "branch", "expert"), None, None),
        ),
        check_vma=False,
    )
```

```python
import functools

import jax
import jax.numpy as jnp
from jax import lax
from jax.experimental import pallas as pl
from jax.experimental.pallas import tpu as pltpu
from jax.sharding import PartitionSpec as P

SHARDS = 8
CAP = 2
LANES = 128
PAD = 16

softmax_scale = 192.0 ** (-0.5)
log2e = 1.4426950408889634


def swapped(x, axis, bit):
    return lax.ppermute(x, axis, [(i, i ^ 1 << bit) for i in range(lax.axis_size(axis))])


def line_hop(x, block, moves):
    pairs = []
    for base in range(0, lax.axis_size("branch"), block):
        for low in range(2):
            pairs += [(base + 2 * i + low, base + 2 * j + low) for i, j in moves]
    return lax.ppermute(x, "branch", pairs)


def pack_cache_kernel(lat_ref, rope_ref, out_ref):
    rows = lat_ref.shape[0]
    out_ref[0:rows, :] = lat_ref[...]
    out_ref[rows:, :] = rope_ref[...]


def pack_cache(lat, rope):
    return pl.pallas_call(
        pack_cache_kernel,
        out_shape=jax.ShapeDtypeStruct((lat.shape[0] + rope.shape[0], lat.shape[1]), lat.dtype),
        in_specs=[pl.BlockSpec(memory_space=pltpu.VMEM)] * 2,
        out_specs=pl.BlockSpec(memory_space=pltpu.VMEM),
        cost_estimate=pl.CostEstimate(flops=0, bytes_accessed=2 * 2 * lat.size, transcendentals=0),
        compiler_params=pltpu.CompilerParams(vmem_limit_bytes=16 * 1024 * 1024),
        name="pack_cache",
    )(lat, rope)


def row_for(slot, parity, slot_ref, own_ref):
    count = slot_ref.shape[0]
    line = count // 2
    own = own_ref[0]
    high = lax.div(own, 2)
    low = lax.rem(own, 2)
    mine = high
    pair = high + 1 - 2 * lax.rem(high, 2)
    first_half = high < line // 2
    nearer = jnp.where(first_half, line // 2, line // 2 - 1)
    farther = jnp.where(first_half, line - 1, 0)
    position = mine
    for number, place_there in ((1, pair), (2, nearer), (3, farther)):
        position = jnp.where(slot == number, place_there, position)
    wanted = 2 * position + (low if parity == 0 else 1 - low)
    row = jnp.int32(0)
    for r in range(1, count):
        row = row + jnp.where(slot_ref[r] == wanted, r, 0)
    return row


def pack_leaving_kernel(slot_ref, own_ref, q_ref, rope_ref, new_ref, out_ref):
    start = 0
    for source in (q_ref, rope_ref, new_ref):
        count = source.shape[1]
        out_ref[0, start : start + count, :] = source[0]
        start += count


def pack_leaving(branch_slot, own, q_lat, q_rope, new):
    slots = branch_slot.shape[0] // 2
    sources = (q_lat, q_rope, new)
    rows = sum(x.shape[1] for x in sources)
    width = q_lat.shape[2]

    def chosen(i, slot_ref, own_ref):
        return (row_for(i, 1, slot_ref, own_ref), 0, 0)

    return pl.pallas_call(
        pack_leaving_kernel,
        out_shape=jax.ShapeDtypeStruct((slots, rows, width), q_lat.dtype),
        grid_spec=pltpu.PrefetchScalarGridSpec(
            num_scalar_prefetch=2,
            grid=(slots,),
            in_specs=[pl.BlockSpec((1, x.shape[1], width), chosen) for x in sources],
            out_specs=pl.BlockSpec((1, rows, width), lambda i, *_: (i, 0, 0)),
        ),
        cost_estimate=pl.CostEstimate(
            flops=0, bytes_accessed=4 * slots * rows * width, transcendentals=0
        ),
        name="pack_leaving",
    )(branch_slot, own, *sources)


def spread_matrix(raw_rows, width):
    per_row = width // (LANES // 2)
    blocks = width // LANES
    shape = (raw_rows * per_row, raw_rows * blocks)
    row = lax.broadcasted_iota(jnp.int32, shape, 0)
    column = lax.broadcasted_iota(jnp.int32, shape, 1)
    wanted = ((row % per_row) // 2) * raw_rows + row // per_row
    return (column == wanted).astype(jnp.bfloat16)


def spread(matrix, raw):
    blocks = raw.shape[1] // LANES
    stacked = jnp.concatenate(
        [raw[:, b * LANES : (b + 1) * LANES] for b in range(blocks)], axis=0
    )
    rows = jnp.dot(matrix, stacked, preferred_element_type=jnp.float32)
    row = lax.broadcasted_iota(jnp.int32, rows.shape, 0)
    lane = lax.broadcasted_iota(jnp.int32, rows.shape, 1)
    return jnp.where(row % 2 == lane // (LANES // 2), rows, 0.0)


def build_attend(heads, steps, width, half, rope_rows, raw_group):
    q_rows = heads * steps
    token_rope = q_rows // 8

    def one_token(lat, raw_rope, fresh_all, keys):
        matrix = spread_matrix(raw_group, width)
        pieces = []
        for start in range(0, token_rope, raw_group):
            part = spread(matrix, raw_rope[start : start + raw_group, :])
            pieces.append(part + pltpu.roll(part, LANES // 2, 1))
        rope = pieces[0] if len(pieces) == 1 else jnp.concatenate(pieces, axis=0)
        rope = rope.astype(jnp.bfloat16)
        query = jnp.concatenate([lat, rope], axis=1)
        contract = (((1,), (1,)), ((), ()))
        scores = lax.dot_general(query, keys[...], contract, preferred_element_type=jnp.float32)
        peak = jnp.max(scores, axis=1, keepdims=True)
        fresh = fresh_all[0:PAD, :]
        fresh_rope = fresh_all[PAD : 2 * PAD, 0:LANES]
        own = lax.dot_general(lat, fresh, contract, preferred_element_type=jnp.float32)
        own = own + lax.dot_general(rope, fresh_rope, contract, preferred_element_type=jnp.float32)
        factor = softmax_scale * log2e
        weights = jnp.exp2(scores * factor - peak * factor)
        total = jnp.sum(weights, axis=1, keepdims=True)
        summed = jnp.dot(
            weights.astype(jnp.bfloat16), keys[:, 0:width], preferred_element_type=jnp.float32
        )
        row_step = lax.broadcasted_iota(jnp.int32, (q_rows, 1), 0) // heads
        columns = [
            jnp.where(row_step >= j, own[:, j : j + 1], -1e30) for j in range(steps)
        ]
        top = peak
        for column in columns:
            top = jnp.maximum(top, column)
        share = jnp.exp2((peak - top) * factor)
        numerator = summed * share
        denominator = total * share
        fresh32 = fresh.astype(jnp.float32)
        for j, column in enumerate(columns):
            weight = jnp.where(row_step >= j, jnp.exp2((column - top) * factor), 0.0)
            numerator = numerator + weight * fresh32[j : j + 1, :]
            denominator = denominator + weight
        return (numerator / denominator).astype(jnp.bfloat16)

    def load_keys(caches, keys, sems):
        copies = []
        for i, cache in enumerate(caches):
            copies.append(
                pltpu.make_async_copy(
                    cache.at[pl.ds(0, half)],
                    keys.at[pl.ds(i * half, half), pl.ds(0, width)],
                    sems.at[i],
                )
            )
        for copy in copies:
            copy.start()
        return copies

    def spread_keys(rope_scratch, keys):
        matrix = spread_matrix(raw_group, width)
        grown = raw_group * width // (LANES // 2)
        for i in range(2):
            for start in range(0, rope_rows, raw_group):
                part = spread(matrix, rope_scratch[i, start : start + raw_group, :])
                first = i * half + start * (width // (LANES // 2))
                keys[first : first + grown, width : width + LANES] = part.astype(jnp.bfloat16)

    def kernel(slot, kinds, given_slots, has_placed, *refs):
        refs = list(refs)
        slot_ref, own_ref = refs.pop(0), refs.pop(0)
        queries = []
        for kind in kinds:
            if kind == "give":
                queries.append(refs.pop(0))
            else:
                queries.append([refs.pop(0) for _ in range(3)])
        caches = [refs.pop(0) for _ in range(2)]
        arrived = [refs.pop(0) for _ in given_slots]
        if has_placed:
            refs.pop(0)
        gives = [refs.pop(0) for kind in kinds if kind == "give"]
        placed = refs.pop(0) if ("keep" in kinds or given_slots) else None
        keys, rope_scratch, result, sems, place_sems = refs
        copies = load_keys(caches, keys, sems)
        rope_copies = []
        for i in range(2):
            copy = pltpu.make_async_copy(
                caches[i].at[pl.ds(half, rope_rows)], rope_scratch.at[i], sems.at[2 + i]
            )
            copy.start()
            rope_copies.append(copy)
        placing = []
        for i, (number, source) in enumerate(zip(given_slots, arrived)):
            copy = pltpu.make_async_copy(
                source, placed.at[row_for(number, 1, slot_ref, own_ref)], place_sems.at[1 + i]
            )
            copy.start()
            placing.append(copy)
        for copy in rope_copies:
            copy.wait()
        spread_keys(rope_scratch, keys)
        for copy in copies:
            copy.wait()
        for kind, query in zip(kinds, queries):
            if kind == "give":
                packed = query.at[0]
                middle = q_rows + token_rope
                value = one_token(
                    packed[0:q_rows, :],
                    packed[q_rows:middle, :],
                    packed[middle : middle + 2 * PAD, :],
                    keys,
                )
                gives.pop(0)[...] = value
            else:
                value = one_token(query[0][0], query[1][0], query[2][0], keys)
                result[...] = value
                copy = pltpu.make_async_copy(
                    result, placed.at[row_for(slot, 0, slot_ref, own_ref)], place_sems.at[0]
                )
                copy.start()
                placing.append(copy)
        for copy in placing:
            copy.wait()

    def call(scalars, kinds, slot, guest, stay, caches, arrived, placed):
        count = scalars[0].shape[0]
        n_tok = len(kinds)
        any_spec = pl.BlockSpec(memory_space=pl.ANY)

        def chosen(i, slot_ref, own_ref):
            return (row_for(slot, 0, slot_ref, own_ref), 0, 0)

        in_specs, operands = [], []
        for kind in kinds:
            if kind == "give":
                in_specs.append(
                    pl.BlockSpec((1, guest.shape[1], width), lambda i, *_: (slot, 0, 0))
                )
                operands.append(guest)
            else:
                in_specs += [pl.BlockSpec((1, x.shape[1], width), chosen) for x in stay]
                operands += stay
        given_slots = tuple(number for number, _ in arrived)
        in_specs += [any_spec] * (2 + len(arrived))
        operands += [*caches, *(value for _, value in arrived)]
        has_placed = placed is not None
        out_shape, out_specs, alias = [], [], {}
        for kind in kinds:
            if kind == "give":
                out_shape.append(jax.ShapeDtypeStruct((q_rows, width), jnp.bfloat16))
                out_specs.append(pl.BlockSpec((q_rows, width), lambda i, *_: (0, 0)))
        if "keep" in kinds or arrived:
            out_shape.append(jax.ShapeDtypeStruct((count, q_rows, width), jnp.bfloat16))
            out_specs.append(any_spec)
            if has_placed:
                alias = {2 + len(operands): len(out_shape) - 1}
        if has_placed:
            in_specs.append(any_spec)
            operands.append(placed)
        all_rows = 2 * half
        return pl.pallas_call(
            functools.partial(kernel, slot, kinds, given_slots, has_placed),
            out_shape=tuple(out_shape),
            grid_spec=pltpu.PrefetchScalarGridSpec(
                num_scalar_prefetch=2,
                grid=(1,),
                in_specs=in_specs,
                out_specs=tuple(out_specs),
                scratch_shapes=[
                    pltpu.VMEM((all_rows, width + LANES), jnp.bfloat16),
                    pltpu.VMEM((2, rope_rows, width), jnp.bfloat16),
                    pltpu.VMEM((q_rows, width), jnp.bfloat16),
                    pltpu.SemaphoreType.DMA((4,)),
                    pltpu.SemaphoreType.DMA((1 + max(1, len(arrived)),)),
                ],
            ),
            input_output_aliases=alias,
            cost_estimate=pl.CostEstimate(
                flops=2 * n_tok * q_rows * all_rows * (2 * width + LANES),
                bytes_accessed=2 * all_rows * (width + LANES) + 4 * n_tok * q_rows * width,
                transcendentals=n_tok * q_rows * all_rows,
            ),
            compiler_params=pltpu.CompilerParams(vmem_limit_bytes=32 * 1024 * 1024),
            name="attend_" + "_".join(kinds),
        )(*scalars, *operands)

    return call


def place_kernel(slot_ref, own_ref, source_ref, before, placed_ref):
    placed_ref[0] = source_ref[...]


def place(scalars, slot, source, placed):
    def chosen(i, slot_ref, own_ref):
        return (row_for(slot, 1, slot_ref, own_ref), 0, 0)

    return pl.pallas_call(
        place_kernel,
        out_shape=jax.ShapeDtypeStruct(placed.shape, placed.dtype),
        grid_spec=pltpu.PrefetchScalarGridSpec(
            num_scalar_prefetch=2,
            grid=(1,),
            in_specs=[
                pl.BlockSpec(source.shape, lambda i, *_: (0, 0)),
                pl.BlockSpec(memory_space=pl.ANY),
            ],
            out_specs=pl.BlockSpec((1,) + source.shape, chosen),
        ),
        input_output_aliases={3: 0},
        name="place",
    )(*scalars, source, placed)


def dispatch_kernel(experts, block_ref, routes_ref, gate_ref, tokens_ref, out_ref, share_ref):
    block = block_ref[0]
    routes = routes_ref[...]
    gates = gate_ref[...]
    rows = routes.shape[0]
    down = lax.broadcasted_iota(jnp.int32, (rows, rows), 0)
    across = lax.broadcasted_iota(jnp.int32, (rows, rows), 1)
    same = (down == across).astype(jnp.float32)
    slots = experts * CAP
    slot_row = lax.broadcasted_iota(jnp.int32, (slots, rows), 0)
    slot_column = lax.broadcasted_iota(jnp.int32, (rows, slots), 1)
    placing = jnp.zeros((slots, rows), jnp.float32)
    share = jnp.zeros((rows, slots), jnp.float32)
    for k in range(experts):
        expert = lax.rem(block + k, experts)
        hit = routes == expert
        has = jnp.sum(hit.astype(jnp.float32), axis=1, keepdims=True)
        weight = jnp.sum(jnp.where(hit, gates, 0.0), axis=1, keepdims=True)
        has_row = jnp.sum(has * same, axis=0, keepdims=True)
        before_row = jnp.sum(jnp.where(down < across, has, 0.0), axis=0, keepdims=True)
        before = jnp.sum(jnp.where(across < down, has_row, 0.0), axis=1, keepdims=True)
        for c in range(CAP):
            slot = k * CAP + c
            placing += jnp.where((slot_row == slot) & (before_row == c), has_row, 0.0)
            share += jnp.where((slot_column == slot) & (before == c), weight, 0.0)
    out_ref[...] = jnp.dot(
        placing.astype(jnp.bfloat16), tokens_ref[...], preferred_element_type=jnp.float32
    ).astype(jnp.bfloat16)
    share_ref[...] = share


def dispatch(block, routes, gates, tokens, experts):
    slots = experts * CAP
    return pl.pallas_call(
        functools.partial(dispatch_kernel, experts),
        out_shape=(
            jax.ShapeDtypeStruct((slots, tokens.shape[1]), tokens.dtype),
            jax.ShapeDtypeStruct((tokens.shape[0], slots), jnp.float32),
        ),
        in_specs=[pl.BlockSpec(memory_space=pltpu.SMEM)]
        + [pl.BlockSpec(memory_space=pltpu.VMEM)] * 3,
        out_specs=(pl.BlockSpec(memory_space=pltpu.VMEM),) * 2,
        cost_estimate=pl.CostEstimate(
            flops=2 * slots * tokens.size, bytes_accessed=3 * tokens.size, transcendentals=0
        ),
        name="dispatch",
    )(block, routes, gates, tokens)


def on_device(
    latent_cache,
    rope_cache,
    q_latent,
    q_rope,
    new_latent,
    new_rope,
    branch_slot,
    moe_input,
    routes,
    route_gate,
    w_gate,
    w_up,
    w_down,
):
    tok_rows, step_count, head_count, width = q_latent.shape
    rope_width = new_rope.shape[-1]
    line = tok_rows // 2
    q_rows = step_count * head_count
    half = latent_cache.shape[1]
    rope_rows = rope_cache.shape[1]
    branch = lax.axis_index("branch")
    own = branch % tok_rows
    low = own % 2
    high = own // 2
    middle = jnp.logical_and(high > 0, high < line - 1)

    outer = [(i, i ^ 1) for i in range(line)]
    inner = [(i, i + 1) for i in range(1, line - 1, 2)]
    inner = inner + [(j, i) for i, j in inner]
    outward = [(i, i ^ 1) for i in range(1, line - 1)]
    own_cache = pack_cache(latent_cache[0], rope_cache[0])
    cache_a = line_hop(own_cache, tok_rows, outer)
    first_b = line_hop(own_cache, tok_rows, inner)
    second_b = line_hop(first_b, tok_rows, outward)
    first_c = line_hop(cache_a, tok_rows, inner)
    second_c = line_hop(first_c, tok_rows, outward)
    cache_b = jnp.where(middle, first_b, second_b)
    cache_c = jnp.where(middle, first_c, second_c)
    caches = [own_cache, cache_a, cache_b, cache_c]
    caches = [(cache, swapped(cache, "expert", 0)) for cache in caches]

    q_lat = q_latent.reshape(tok_rows, q_rows, width)
    rope_raw = q_rope.reshape(tok_rows, q_rows * rope_width // width, width)
    fresh = jnp.concatenate(
        [
            jnp.pad(new_latent, ((0, 0), (0, PAD - step_count), (0, 0))),
            jnp.pad(new_rope, ((0, 0), (0, PAD - step_count), (0, width - rope_width))),
        ],
        axis=1,
    )
    scalars = (branch_slot, own[None])
    stay = (q_lat, rope_raw, fresh)
    leave = pack_leaving(*scalars, *stay)
    guest = swapped(leave, "branch", 0)

    attend = build_attend(head_count, step_count, width, half, rope_rows, 32)
    placed = None
    waiting = []
    for slot in range(line):
        kinds = [("give", "keep")] if slot < line - 1 else [("give",), ("keep",)]
        given = None
        for kind in kinds:
            keeps = "keep" in kind
            results = attend(
                scalars,
                kind,
                slot,
                guest,
                stay,
                caches[slot],
                waiting if keeps else [],
                placed if keeps else None,
            )
            if "give" in kind:
                given = results[0]
            if keeps:
                placed = results[-1]
        waiting = [(slot, swapped(given, "branch", 0))]
    placed = place(scalars, line - 1, waiting[0][1], placed)
    attended = placed.reshape(tok_rows, step_count, head_count, width)

    model_width = moe_input.shape[-1]
    tok_total = tok_rows * step_count
    device = branch * lax.axis_size("expert") + lax.axis_index("expert")
    experts = lax.axis_size("branch") * lax.axis_size("expert") // SHARDS
    cores = lax.axis_size("expert")
    shard_branches = SHARDS // cores
    block = device // SHARDS
    outgoing, share = dispatch(
        block[None],
        routes.reshape(tok_total, -1),
        route_gate.reshape(tok_total, -1),
        moe_input.reshape(tok_total, model_width),
        experts,
    )

    around = shard_branches // 2

    def along(x, shift, flip):
        count = lax.axis_size("branch")
        there = [
            ((i // shard_branches + shift) % experts) * shard_branches
            + ((i % shard_branches) ^ (flip * 2))
            for i in range(count)
        ]
        return lax.ppermute(x, "branch", list(enumerate(there)))

    ways = [(k, m) for k in range(experts) for m in range(around)]
    rows = []
    for k, m in ways:
        piece = outgoing[k * CAP : (k + 1) * CAP]
        rows.append(piece if (k, m) == (0, 0) else along(piece, k, m))
    rows = jnp.concatenate(rows, axis=0)
    bits = [("branch", 0)] + [("expert", b) for b in reversed(range(cores.bit_length() - 1))]
    for axis, bit in bits:
        rows = jnp.concatenate([rows, swapped(rows, axis, bit)], axis=0)
    gate_value = jnp.dot(rows, w_gate[0], preferred_element_type=jnp.float32)
    lifted = jnp.dot(rows, w_up[0], preferred_element_type=jnp.float32)
    hidden = (jax.nn.silu(gate_value) * lifted).astype(jnp.bfloat16)
    parts = jnp.dot(hidden, w_down[0], preferred_element_type=jnp.float32)
    for axis, bit in reversed(bits):
        count = parts.shape[0] // 2
        parts = parts[:count] + swapped(
            parts[count:].astype(jnp.bfloat16), axis, bit
        ).astype(jnp.float32)
    sums = [0.0] * experts
    for number, (k, m) in enumerate(ways):
        piece = parts[number * CAP : (number + 1) * CAP]
        if (k, m) != (0, 0):
            piece = along(piece.astype(jnp.bfloat16), -k, m).astype(jnp.float32)
        sums[k] = sums[k] + piece
    sums = jnp.concatenate(sums, axis=0)
    combined = jnp.sum(share[:, :, None] * sums[None, :, :], axis=1)
    moe_out = combined.astype(jnp.bfloat16).reshape(tok_rows, step_count, model_width)
    return (attended, moe_out)


def solution(mesh):
    return jax.shard_map(
        on_device,
        mesh=mesh,
        in_specs=(
            P(("group", "branch"), "expert", None),
            P(("group", "branch"), "expert", None),
            P(("group", "branch", "expert"), None, None, None),
            P(("group", "branch", "expert"), None, None),
            P(("group", "branch", "expert"), None, None),
            P(("group", "branch", "expert"), None, None),
            P(("group", "branch", "expert")),
            P(("group", "branch", "expert"), None, None),
            P(("group", "branch", "expert"), None, None),
            P(("group", "branch", "expert"), None, None),
            P(("branch", "expert"), None, None),
            P(("branch", "expert"), None, None),
            P(("branch", "expert"), None, None),
        ),
        out_specs=(
            P(("group", "branch", "expert"), None, None, None),
            P(("group", "branch", "expert"), None, None),
        ),
        check_vma=False,
    )
```

```python
import functools

import jax
import jax.numpy as jnp
from jax import lax
from jax.experimental import pallas as pl
from jax.experimental.pallas import tpu as pltpu
from jax.sharding import PartitionSpec as P

SHARDS = 8
CAP = 2
LANES = 128
PAD = 16

SMALL = pl.CostEstimate(flops=0, bytes_accessed=1024, transcendentals=0)

softmax_scale = 192.0 ** (-0.5)
log2e = 1.4426950408889634


def after(x, *earlier):
    return lax.optimization_barrier((x, *earlier))[0]


def swapped(x, axis, bit):
    return lax.ppermute(x, axis, [(i, i ^ 1 << bit) for i in range(lax.axis_size(axis))])


def line_hop(x, block, moves):
    pairs = []
    for base in range(0, lax.axis_size("branch"), block):
        for low in range(2):
            pairs += [(base + 2 * i + low, base + 2 * j + low) for i, j in moves]
    return lax.ppermute(x, "branch", pairs)


def pack_cache_kernel(lat_ref, rope_ref, out_ref):
    rows = lat_ref.shape[0]
    out_ref[0:rows, :] = lat_ref[...]
    out_ref[rows:, :] = rope_ref[...]


def pack_cache(lat, rope):
    return pl.pallas_call(
        pack_cache_kernel,
        out_shape=jax.ShapeDtypeStruct((lat.shape[0] + rope.shape[0], lat.shape[1]), lat.dtype),
        in_specs=[pl.BlockSpec(memory_space=pltpu.VMEM)] * 2,
        out_specs=pl.BlockSpec(memory_space=pltpu.VMEM),
        cost_estimate=SMALL,
        compiler_params=pltpu.CompilerParams(vmem_limit_bytes=16 * 1024 * 1024),
        name="pack_cache",
    )(lat, rope)


def row_for(slot, parity, slot_ref, own_ref):
    count = slot_ref.shape[0]
    line = count // 2
    own = own_ref[0]
    high = lax.div(own, 2)
    low = lax.rem(own, 2)
    mine = high
    pair = high + 1 - 2 * lax.rem(high, 2)
    first_half = high < line // 2
    nearer = jnp.where(first_half, line // 2, line // 2 - 1)
    farther = jnp.where(first_half, line - 1, 0)
    position = mine
    for number, place_there in ((1, pair), (2, nearer), (3, farther)):
        position = jnp.where(slot == number, place_there, position)
    wanted = 2 * position + (low if parity == 0 else 1 - low)
    row = jnp.int32(0)
    for r in range(1, count):
        row = row + jnp.where(slot_ref[r] == wanted, r, 0)
    return row


def pack_leaving_kernel(slot_ref, own_ref, q_ref, rope_ref, new_ref, out_ref, sems):
    copies = []
    for slot in range(out_ref.shape[0]):
        row = row_for(slot, 1, slot_ref, own_ref)
        start = 0
        for part, source in enumerate((q_ref, rope_ref, new_ref)):
            count = source.shape[1]
            copy = pltpu.make_async_copy(
                source.at[row], out_ref.at[slot, pl.ds(start, count)], sems.at[slot, part]
            )
            copy.start()
            copies.append(copy)
            start += count
    for copy in copies:
        copy.wait()


def pack_leaving(branch_slot, own, q_lat, q_rope, new):
    slots = branch_slot.shape[0] // 2
    sources = (q_lat, q_rope, new)
    rows = sum(x.shape[1] for x in sources)
    return pl.pallas_call(
        pack_leaving_kernel,
        out_shape=jax.ShapeDtypeStruct((slots, rows, q_lat.shape[2]), q_lat.dtype),
        in_specs=[pl.BlockSpec(memory_space=pltpu.SMEM)] * 2
        + [pl.BlockSpec(memory_space=pl.ANY)] * 3,
        out_specs=pl.BlockSpec(memory_space=pltpu.VMEM),
        scratch_shapes=[pltpu.SemaphoreType.DMA((slots, 3))],
        cost_estimate=SMALL,
        compiler_params=pltpu.CompilerParams(vmem_limit_bytes=16 * 1024 * 1024),
        name="pack_leaving",
    )(branch_slot, own, *sources)


def spread_matrix(raw_rows, width):
    per_row = width // (LANES // 2)
    blocks = width // LANES
    shape = (raw_rows * per_row, raw_rows * blocks)
    row = lax.broadcasted_iota(jnp.int32, shape, 0)
    column = lax.broadcasted_iota(jnp.int32, shape, 1)
    wanted = ((row % per_row) // 2) * raw_rows + row // per_row
    return (column == wanted).astype(jnp.bfloat16)


def spread(matrix, raw):
    blocks = raw.shape[1] // LANES
    stacked = jnp.concatenate(
        [raw[:, b * LANES : (b + 1) * LANES] for b in range(blocks)], axis=0
    )
    rows = jnp.dot(matrix, stacked, preferred_element_type=jnp.float32)
    row = lax.broadcasted_iota(jnp.int32, rows.shape, 0)
    lane = lax.broadcasted_iota(jnp.int32, rows.shape, 1)
    return jnp.where(row % 2 == lane // (LANES // 2), rows, 0.0)


def build_attend(heads, steps, width, half, rope_rows, raw_group, chunk):
    q_rows = heads * steps
    token_rope = q_rows // 8

    factor = softmax_scale * log2e
    contract = (((1,), (1,)), ((), ()))

    def put_query(queries, number, lat, raw_rope, matrix):
        first = number * q_rows
        queries[first : first + q_rows, 0:width] = lat
        grown = raw_group * width // (LANES // 2)
        for i, start in enumerate(range(0, token_rope, raw_group)):
            part = spread(matrix, raw_rope[start : start + raw_group, :])
            part = part + pltpu.roll(part, LANES // 2, 1)
            row = first + i * grown
            queries[row : row + grown, width : width + LANES] = part.astype(jnp.bfloat16)

    def merge_own(query, fresh_all, peak, total, summed):
        fresh = fresh_all[0:PAD, :]
        fresh_rope = fresh_all[PAD : 2 * PAD, 0:LANES]
        own = lax.dot_general(
            query[:, 0:width], fresh, contract, preferred_element_type=jnp.float32
        )
        own = own + lax.dot_general(
            query[:, width:], fresh_rope, contract, preferred_element_type=jnp.float32
        )
        row_step = lax.broadcasted_iota(jnp.int32, (q_rows, 1), 0) // heads
        columns = [jnp.where(row_step >= j, own[:, j : j + 1], -1e30) for j in range(steps)]
        top = peak
        for column in columns:
            top = jnp.maximum(top, column)
        share = jnp.exp2((peak - top) * factor)
        parts = [
            jnp.where(row_step >= j, jnp.exp2((column - top) * factor), 0.0)
            for j, column in enumerate(columns)
        ]
        denominator = total * share
        for part in parts:
            denominator = denominator + part
        inverse = 1.0 / denominator
        fresh32 = fresh.astype(jnp.float32)
        value = summed * (share * inverse)
        for j, part in enumerate(parts):
            value = value + (part * inverse) * fresh32[j : j + 1, :]
        return value.astype(jnp.bfloat16)

    def load_keys(caches, keys, sems):
        copies = []
        for i, cache in enumerate(caches):
            copies.append(
                pltpu.make_async_copy(
                    cache.at[pl.ds(0, half)],
                    keys.at[pl.ds(i * half, half), pl.ds(0, width)],
                    sems.at[i],
                )
            )
        for copy in copies:
            copy.start()
        return copies

    def spread_keys(i, rope_scratch, keys, matrix):
        grown = raw_group * width // (LANES // 2)
        for start in range(0, rope_rows, raw_group):
            part = spread(matrix, rope_scratch[i, start : start + raw_group, :])
            first = i * half + start * (width // (LANES // 2))
            keys[first : first + grown, width : width + LANES] = part.astype(jnp.bfloat16)

    def kernel(slot, kinds, given_slots, has_placed, *refs):
        refs = list(refs)
        slot_ref, own_ref = refs.pop(0), refs.pop(0)
        queries = []
        for kind in kinds:
            if kind == "give":
                queries.append(refs.pop(0))
            else:
                queries.append([refs.pop(0) for _ in range(3)])
        caches = [refs.pop(0) for _ in range(2)]
        arrived = [refs.pop(0) for _ in given_slots]
        if has_placed:
            refs.pop(0)
        gives = [refs.pop(0) for kind in kinds if kind == "give"]
        placed = refs.pop(0) if ("keep" in kinds or given_slots) else None
        keys, rope_scratch, query_all, scores, summed, result, sems, place_sems = refs
        copies = load_keys(caches, keys, sems)
        rope_copies = []
        for i in range(2):
            copy = pltpu.make_async_copy(
                caches[i].at[pl.ds(half, rope_rows)], rope_scratch.at[i], sems.at[2 + i]
            )
            copy.start()
            rope_copies.append(copy)
        placing = []
        for i, (number, source) in enumerate(zip(given_slots, arrived)):
            copy = pltpu.make_async_copy(
                source, placed.at[row_for(number, 1, slot_ref, own_ref)], place_sems.at[1 + i]
            )
            copy.start()
            placing.append(copy)
        matrix = spread_matrix(raw_group, width)
        fresh_parts = []
        for number, (kind, query) in enumerate(zip(kinds, queries)):
            if kind == "give":
                middle = q_rows + token_rope
                packed = query.at[0]
                lat, raw = packed[0:q_rows, :], packed[q_rows:middle, :]
                fresh_parts.append(packed[middle : middle + 2 * PAD, :])
            else:
                lat, raw = query[0][0], query[1][0]
                fresh_parts.append(query[2][0])
            put_query(query_all, number, lat, raw, matrix)
        peak = None
        for i in range(2):
            rope_copies[i].wait()
            spread_keys(i, rope_scratch, keys, matrix)
            copies[i].wait()
            for start in range(i * half, (i + 1) * half, chunk):
                part = lax.dot_general(
                    query_all[...],
                    keys[start : start + chunk, :],
                    contract,
                    preferred_element_type=jnp.float32,
                )
                scores[:, start : start + chunk] = part
                high = jnp.max(part, axis=1, keepdims=True)
                peak = high if peak is None else jnp.maximum(peak, high)
        scaled = peak * factor
        total = None
        for start in range(0, 2 * half, chunk):
            weights = jnp.exp2(scores[:, start : start + chunk] * factor - scaled)
            part = jnp.sum(weights, axis=1, keepdims=True)
            value = jnp.dot(
                weights.astype(jnp.bfloat16),
                keys[start : start + chunk, 0:width],
                preferred_element_type=jnp.float32,
            )
            if start == 0:
                total = part
                summed[...] = value
            else:
                total = total + part
                summed[...] += value
        for number, kind in enumerate(kinds):
            rows = slice(number * q_rows, (number + 1) * q_rows)
            value = merge_own(
                query_all[rows, :], fresh_parts[number], peak[rows], total[rows], summed[rows, :]
            )
            if kind == "give":
                gives.pop(0)[...] = value
            else:
                result[...] = value
                copy = pltpu.make_async_copy(
                    result, placed.at[row_for(slot, 0, slot_ref, own_ref)], place_sems.at[0]
                )
                copy.start()
                placing.append(copy)
        for copy in placing:
            copy.wait()

    def call(scalars, kinds, slot, guest, stay, caches, arrived, placed):
        count = scalars[0].shape[0]
        n_tok = len(kinds)
        any_spec = pl.BlockSpec(memory_space=pl.ANY)

        def chosen(i, slot_ref, own_ref):
            return (row_for(slot, 0, slot_ref, own_ref), 0, 0)

        in_specs, operands = [], []
        for kind in kinds:
            if kind == "give":
                in_specs.append(
                    pl.BlockSpec((1, guest.shape[1], width), lambda i, *_: (slot, 0, 0))
                )
                operands.append(guest)
            else:
                in_specs += [pl.BlockSpec((1, x.shape[1], width), chosen) for x in stay]
                operands += stay
        given_slots = tuple(number for number, _ in arrived)
        in_specs += [any_spec] * 2
        in_specs += [pl.BlockSpec((q_rows, width), lambda i, *_: (0, 0)) for _ in arrived]
        operands += [*caches, *(value for _, value in arrived)]
        has_placed = placed is not None
        out_shape, out_specs, alias = [], [], {}
        for kind in kinds:
            if kind == "give":
                out_shape.append(jax.ShapeDtypeStruct((q_rows, width), jnp.bfloat16))
                out_specs.append(pl.BlockSpec((q_rows, width), lambda i, *_: (0, 0)))
        if "keep" in kinds or arrived:
            out_shape.append(jax.ShapeDtypeStruct((count, q_rows, width), jnp.bfloat16))
            out_specs.append(any_spec)
            if has_placed:
                alias = {2 + len(operands): len(out_shape) - 1}
        if has_placed:
            in_specs.append(any_spec)
            operands.append(placed)
        all_rows = 2 * half
        return pl.pallas_call(
            functools.partial(kernel, slot, kinds, given_slots, has_placed),
            out_shape=tuple(out_shape),
            grid_spec=pltpu.PrefetchScalarGridSpec(
                num_scalar_prefetch=2,
                grid=(1,),
                in_specs=in_specs,
                out_specs=tuple(out_specs),
                scratch_shapes=[
                    pltpu.VMEM((all_rows, width + LANES), jnp.bfloat16),
                    pltpu.VMEM((2, rope_rows, width), jnp.bfloat16),
                    pltpu.VMEM((n_tok * q_rows, width + LANES), jnp.bfloat16),
                    pltpu.VMEM((n_tok * q_rows, all_rows), jnp.float32),
                    pltpu.VMEM((n_tok * q_rows, width), jnp.float32),
                    pltpu.VMEM((q_rows, width), jnp.bfloat16),
                    pltpu.SemaphoreType.DMA((4,)),
                    pltpu.SemaphoreType.DMA((1 + max(1, len(arrived)),)),
                ],
            ),
            input_output_aliases=alias,
            cost_estimate=SMALL,
            compiler_params=pltpu.CompilerParams(vmem_limit_bytes=32 * 1024 * 1024),
            name="attend_" + "_".join(kinds),
        )(*scalars, *operands)

    return call


def place_kernel(slot_ref, own_ref, source_ref, before, placed_ref):
    placed_ref[0] = source_ref[...]


def place(scalars, slot, source, placed):
    def chosen(i, slot_ref, own_ref):
        return (row_for(slot, 1, slot_ref, own_ref), 0, 0)

    return pl.pallas_call(
        place_kernel,
        out_shape=jax.ShapeDtypeStruct(placed.shape, placed.dtype),
        grid_spec=pltpu.PrefetchScalarGridSpec(
            num_scalar_prefetch=2,
            grid=(1,),
            in_specs=[
                pl.BlockSpec(source.shape, lambda i, *_: (0, 0)),
                pl.BlockSpec(memory_space=pl.ANY),
            ],
            out_specs=pl.BlockSpec((1,) + source.shape, chosen),
        ),
        input_output_aliases={3: 0},
        name="place",
    )(*scalars, source, placed)


def dispatch_kernel(experts, block_ref, routes_ref, gate_ref, tokens_ref, out_ref, share_ref):
    block = block_ref[0]
    routes = routes_ref[...]
    gates = gate_ref[...]
    rows = routes.shape[0]
    down = lax.broadcasted_iota(jnp.int32, (rows, rows), 0)
    across = lax.broadcasted_iota(jnp.int32, (rows, rows), 1)
    same = (down == across).astype(jnp.float32)
    slots = experts * CAP
    slot_row = lax.broadcasted_iota(jnp.int32, (slots, rows), 0)
    slot_column = lax.broadcasted_iota(jnp.int32, (rows, slots), 1)
    placing = jnp.zeros((slots, rows), jnp.float32)
    share = jnp.zeros((rows, slots), jnp.float32)
    for k in range(experts):
        expert = lax.rem(block + k, experts)
        hit = routes == expert
        has = jnp.sum(hit.astype(jnp.float32), axis=1, keepdims=True)
        weight = jnp.sum(jnp.where(hit, gates, 0.0), axis=1, keepdims=True)
        has_row = jnp.sum(has * same, axis=0, keepdims=True)
        before_row = jnp.sum(jnp.where(down < across, has, 0.0), axis=0, keepdims=True)
        before = jnp.sum(jnp.where(across < down, has_row, 0.0), axis=1, keepdims=True)
        for c in range(CAP):
            slot = k * CAP + c
            placing += jnp.where((slot_row == slot) & (before_row == c), has_row, 0.0)
            share += jnp.where((slot_column == slot) & (before == c), weight, 0.0)
    out_ref[...] = jnp.dot(
        placing.astype(jnp.bfloat16), tokens_ref[...], preferred_element_type=jnp.float32
    ).astype(jnp.bfloat16)
    share_ref[...] = share


def dispatch(block, routes, gates, tokens, experts):
    slots = experts * CAP
    return pl.pallas_call(
        functools.partial(dispatch_kernel, experts),
        out_shape=(
            jax.ShapeDtypeStruct((slots, tokens.shape[1]), tokens.dtype),
            jax.ShapeDtypeStruct((tokens.shape[0], slots), jnp.float32),
        ),
        in_specs=[pl.BlockSpec(memory_space=pltpu.SMEM)]
        + [pl.BlockSpec(memory_space=pltpu.VMEM)] * 3,
        out_specs=(pl.BlockSpec(memory_space=pltpu.VMEM),) * 2,
        cost_estimate=SMALL,
        name="dispatch",
    )(block, routes, gates, tokens)


def experts_kernel(mine_ref, theirs_ref, gate_ref, up_ref, down_ref, keep_ref, send_ref):
    rows = jnp.concatenate([mine_ref[...], theirs_ref[...]], axis=0)
    gate = jnp.dot(rows, gate_ref[0], preferred_element_type=jnp.float32)
    lifted = jnp.dot(rows, up_ref[0], preferred_element_type=jnp.float32)
    hidden = (gate / (1.0 + jnp.exp(-gate)) * lifted).astype(jnp.bfloat16)
    parts = jnp.dot(hidden, down_ref[0], preferred_element_type=jnp.float32)
    count = mine_ref.shape[0]
    keep_ref[...] = parts[:count]
    send_ref[...] = parts[count:].astype(jnp.bfloat16)


def run_experts(mine, theirs, w_gate, w_up, w_down):
    return pl.pallas_call(
        experts_kernel,
        out_shape=(
            jax.ShapeDtypeStruct(mine.shape, jnp.float32),
            jax.ShapeDtypeStruct(mine.shape, jnp.bfloat16),
        ),
        cost_estimate=SMALL,
        compiler_params=pltpu.CompilerParams(vmem_limit_bytes=32 * 1024 * 1024),
        name="experts",
    )(mine, theirs, w_gate, w_up, w_down)


def halve_kernel(sum_ref, arrived_ref, keep_ref, send_ref):
    count = keep_ref.shape[0]
    total = sum_ref[...] + arrived_ref[...].astype(jnp.float32)
    keep_ref[...] = total[:count]
    send_ref[...] = total[count:].astype(jnp.bfloat16)


def halve(kept, arrived):
    shape = (kept.shape[0] // 2, kept.shape[1])
    return pl.pallas_call(
        halve_kernel,
        out_shape=(
            jax.ShapeDtypeStruct(shape, jnp.float32),
            jax.ShapeDtypeStruct(shape, jnp.bfloat16),
        ),
        cost_estimate=SMALL,
        compiler_params=pltpu.CompilerParams(vmem_limit_bytes=16 * 1024 * 1024),
        name="halve",
    )(kept, arrived)


def on_device(
    latent_cache,
    rope_cache,
    q_latent,
    q_rope,
    new_latent,
    new_rope,
    branch_slot,
    moe_input,
    routes,
    route_gate,
    w_gate,
    w_up,
    w_down,
):
    tok_rows, step_count, head_count, width = q_latent.shape
    rope_width = new_rope.shape[-1]
    line = tok_rows // 2
    q_rows = step_count * head_count
    half = latent_cache.shape[1]
    rope_rows = rope_cache.shape[1]
    branch = lax.axis_index("branch")
    own = branch % tok_rows
    low = own % 2
    high = own // 2
    middle = jnp.logical_and(high > 0, high < line - 1)

    outer = [(i, i ^ 1) for i in range(line)]
    inner = [(i, i + 1) for i in range(1, line - 1, 2)]
    inner = inner + [(j, i) for i, j in inner]
    outward = [(i, i ^ 1) for i in range(1, line - 1)]
    own_cache = pack_cache(latent_cache[0], rope_cache[0])
    cache_a = line_hop(own_cache, tok_rows, outer)
    first_b = line_hop(own_cache, tok_rows, inner)
    second_b = line_hop(first_b, tok_rows, outward)
    first_c = line_hop(cache_a, tok_rows, inner)
    second_c = line_hop(first_c, tok_rows, outward)

    q_lat = q_latent.reshape(tok_rows, q_rows, width)
    rope_raw = q_rope.reshape(tok_rows, q_rows * rope_width // width, width)
    fresh = jnp.concatenate(
        [
            jnp.pad(new_latent, ((0, 0), (0, PAD - step_count), (0, 0))),
            jnp.pad(new_rope, ((0, 0), (0, PAD - step_count), (0, width - rope_width))),
        ],
        axis=1,
    )
    scalars = (branch_slot, own[None])
    stay = (q_lat, rope_raw, fresh)

    attend = build_attend(head_count, step_count, width, half, rope_rows, 32, half // 2)
    model_width = moe_input.shape[-1]
    tok_total = tok_rows * step_count
    device = branch * lax.axis_size("expert") + lax.axis_index("expert")
    experts = lax.axis_size("branch") * lax.axis_size("expert") // SHARDS
    cores = lax.axis_size("expert")
    shard_branches = SHARDS // cores
    block = device // SHARDS
    outgoing, share = dispatch(
        after(block[None], own_cache),
        routes.reshape(tok_total, -1),
        route_gate.reshape(tok_total, -1),
        moe_input.reshape(tok_total, model_width),
        experts,
    )

    around = shard_branches // 2

    def along(x, shift, flip):
        count = lax.axis_size("branch")
        there = [
            ((i // shard_branches + shift) % experts) * shard_branches
            + ((i % shard_branches) ^ (flip * 2))
            for i in range(count)
        ]
        return lax.ppermute(x, "branch", list(enumerate(there)))

    beside = swapped(outgoing, "branch", 0)
    leave = pack_leaving(branch_slot, after(own[None], beside), *stay)
    guest = swapped(leave, "branch", 0)
    ways = [(k, m) for k in range(experts) for m in range(around)]
    pieces = []
    for k, m in ways:
        piece = jnp.concatenate([x[k * CAP : (k + 1) * CAP] for x in (outgoing, beside)], axis=0)
        pieces.append(piece if (k, m) == (0, 0) else along(piece, k, m))

    def attend_slot(slot, cache, kinds, waiting, placed):
        keeps = "keep" in kinds
        results = attend(
            scalars,
            kinds,
            slot,
            guest,
            stay,
            cache,
            waiting if keeps else [],
            placed if keeps else None,
        )
        given = results[0] if "give" in kinds else None
        return given, (results[-1] if keeps else placed)

    def both_halves(cache):
        return cache, swapped(cache, "expert", 0)

    guest = after(guest, cache_a, first_b)
    both = ("give", "keep")
    given_0, placed = attend_slot(0, both_halves(own_cache), both, [], None)
    back_0 = swapped(given_0, "branch", 0)
    given_1, placed = attend_slot(1, both_halves(cache_a), both, [], placed)
    back_1 = swapped(given_1, "branch", 0)


    first_c, second_b, given_1, *pieces = lax.optimization_barrier(
        (first_c, second_b, given_1, *pieces)
    )
    rows = jnp.concatenate([x[:CAP] for x in pieces] + [x[CAP:] for x in pieces], axis=0)
    cache_b = jnp.where(middle, first_b, second_b)
    kept, sent = run_experts(rows, swapped(rows, "expert", 0), w_gate, w_up, w_down)
    kept, sent = halve(kept, swapped(sent, "expert", 0))
    given_2, placed = attend_slot(2, both_halves(cache_b), both, [(0, back_0)], placed)
    back_2 = swapped(given_2, "branch", 0)

    second_c, given_2, kept, sent = lax.optimization_barrier((second_c, given_2, kept, sent))
    cache_c = both_halves(jnp.where(middle, first_c, second_c))
    given_3, _ = attend_slot(3, cache_c, ("give",), [], None)
    back_3 = swapped(given_3, "branch", 0)
    _, placed = attend_slot(3, cache_c, ("keep",), [(1, back_1), (2, back_2)], placed)
    placed = place(scalars, 3, back_3, placed)
    attended = placed.reshape(tok_rows, step_count, head_count, width)

    parts = kept + swapped(sent, "branch", 0).astype(jnp.float32)
    parts = after(parts, given_3)
    sums = [0.0] * experts
    for number, (k, m) in enumerate(ways):
        piece = parts[number * CAP : (number + 1) * CAP]
        if (k, m) != (0, 0):
            piece = along(piece.astype(jnp.bfloat16), -k, m).astype(jnp.float32)
        sums[k] = sums[k] + piece
    sums = jnp.concatenate(sums, axis=0)
    combined = jnp.sum(share[:, :, None] * sums[None, :, :], axis=1)
    moe_out = combined.astype(jnp.bfloat16).reshape(tok_rows, step_count, model_width)
    return (attended, moe_out)


def solution(mesh):
    return jax.shard_map(
        on_device,
        mesh=mesh,
        in_specs=(
            P(("group", "branch"), "expert", None),
            P(("group", "branch"), "expert", None),
            P(("group", "branch", "expert"), None, None, None),
            P(("group", "branch", "expert"), None, None),
            P(("group", "branch", "expert"), None, None),
            P(("group", "branch", "expert"), None, None),
            P(("group", "branch", "expert")),
            P(("group", "branch", "expert"), None, None),
            P(("group", "branch", "expert"), None, None),
            P(("group", "branch", "expert"), None, None),
            P(("branch", "expert"), None, None),
            P(("branch", "expert"), None, None),
            P(("branch", "expert"), None, None),
        ),
        out_specs=(
            P(("group", "branch", "expert"), None, None, None),
            P(("group", "branch", "expert"), None, None),
        ),
        check_vma=False,
    )
```

```python
import functools

import jax
import jax.numpy as jnp
from jax import lax
from jax.experimental import pallas as pl
from jax.experimental.pallas import tpu as pltpu
from jax.sharding import PartitionSpec as P

SHARDS = 8
CAP = 2
LANES = 128
PAD = 16

SMALL = pl.CostEstimate(flops=0, bytes_accessed=1024, transcendentals=0)

softmax_scale = 192.0 ** (-0.5)
log2e = 1.4426950408889634


def after(x, *earlier):
    return lax.optimization_barrier((x, *earlier))[0]


def swapped(x, axis, bit):
    return lax.ppermute(x, axis, [(i, i ^ 1 << bit) for i in range(lax.axis_size(axis))])


def line_hop(x, block, moves):
    pairs = []
    for base in range(0, lax.axis_size("branch"), block):
        for low in range(2):
            pairs += [(base + 2 * i + low, base + 2 * j + low) for i, j in moves]
    return lax.ppermute(x, "branch", pairs)


def pack_cache_kernel(lat_ref, rope_ref, out_ref, sems):
    rows = lat_ref.shape[0]
    copies = [
        pltpu.make_async_copy(lat_ref, out_ref.at[pl.ds(0, rows)], sems.at[0]),
        pltpu.make_async_copy(rope_ref, out_ref.at[pl.ds(rows, rope_ref.shape[0])], sems.at[1]),
    ]
    for copy in copies:
        copy.start()
    for copy in copies:
        copy.wait()


def pack_cache(lat, rope):
    return pl.pallas_call(
        pack_cache_kernel,
        out_shape=jax.ShapeDtypeStruct((lat.shape[0] + rope.shape[0], lat.shape[1]), lat.dtype),
        in_specs=[pl.BlockSpec(memory_space=pl.ANY)] * 2,
        out_specs=pl.BlockSpec(memory_space=pltpu.VMEM),
        scratch_shapes=[pltpu.SemaphoreType.DMA((2,))],
        cost_estimate=SMALL,
        compiler_params=pltpu.CompilerParams(vmem_limit_bytes=4 * 1024 * 1024),
        name="pack_cache",
    )(lat, rope)


def row_for(slot, parity, slot_ref, own_ref):
    count = slot_ref.shape[0]
    line = count // 2
    own = own_ref[0]
    high = lax.div(own, 2)
    low = lax.rem(own, 2)
    mine = high
    pair = high + 1 - 2 * lax.rem(high, 2)
    first_half = high < line // 2
    nearer = jnp.where(first_half, line // 2, line // 2 - 1)
    farther = jnp.where(first_half, line - 1, 0)
    position = mine
    for number, place_there in ((1, pair), (2, nearer), (3, farther)):
        position = jnp.where(slot == number, place_there, position)
    wanted = 2 * position + (low if parity == 0 else 1 - low)
    row = jnp.int32(0)
    for r in range(1, count):
        row = row + jnp.where(slot_ref[r] == wanted, r, 0)
    return row


def pack_leaving_kernel(slot_ref, own_ref, q_ref, rope_ref, new_ref, out_ref, sems):
    copies = []
    for slot in range(out_ref.shape[0]):
        row = row_for(slot, 1, slot_ref, own_ref)
        start = 0
        for part, source in enumerate((q_ref, rope_ref, new_ref)):
            count = source.shape[1]
            copy = pltpu.make_async_copy(
                source.at[row], out_ref.at[slot, pl.ds(start, count)], sems.at[slot, part]
            )
            copy.start()
            copies.append(copy)
            start += count
    for copy in copies:
        copy.wait()


def pack_leaving(branch_slot, own, q_lat, q_rope, new):
    slots = branch_slot.shape[0] // 2
    sources = (q_lat, q_rope, new)
    rows = sum(x.shape[1] for x in sources)
    return pl.pallas_call(
        pack_leaving_kernel,
        out_shape=jax.ShapeDtypeStruct((slots, rows, q_lat.shape[2]), q_lat.dtype),
        in_specs=[pl.BlockSpec(memory_space=pltpu.SMEM)] * 2
        + [pl.BlockSpec(memory_space=pl.ANY)] * 3,
        out_specs=pl.BlockSpec(memory_space=pltpu.VMEM),
        scratch_shapes=[pltpu.SemaphoreType.DMA((slots, 3))],
        cost_estimate=SMALL,
        compiler_params=pltpu.CompilerParams(vmem_limit_bytes=4 * 1024 * 1024),
        name="pack_leaving",
    )(branch_slot, own, *sources)


def spread_matrix(raw_rows, width):
    per_row = width // (LANES // 2)
    blocks = width // LANES
    shape = (raw_rows * per_row, raw_rows * blocks)
    row = lax.broadcasted_iota(jnp.int32, shape, 0)
    column = lax.broadcasted_iota(jnp.int32, shape, 1)
    wanted = ((row % per_row) // 2) * raw_rows + row // per_row
    return (column == wanted).astype(jnp.bfloat16)


def spread(matrix, raw):
    blocks = raw.shape[1] // LANES
    stacked = jnp.concatenate(
        [raw[:, b * LANES : (b + 1) * LANES] for b in range(blocks)], axis=0
    )
    rows = jnp.dot(matrix, stacked, preferred_element_type=jnp.float32)
    row = lax.broadcasted_iota(jnp.int32, rows.shape, 0)
    lane = lax.broadcasted_iota(jnp.int32, rows.shape, 1)
    return jnp.where(row % 2 == lane // (LANES // 2), rows, 0.0)


def build_attend(heads, steps, width, half, rope_rows, raw_group, chunk):
    q_rows = heads * steps
    token_rope = q_rows // 8

    factor = softmax_scale * log2e
    contract = (((1,), (1,)), ((), ()))

    def put_query(queries, number, lat, raw_rope, matrix):
        first = number * q_rows
        queries[first : first + q_rows, 0:width] = lat
        grown = raw_group * width // (LANES // 2)
        for i, start in enumerate(range(0, token_rope, raw_group)):
            part = spread(matrix, raw_rope[start : start + raw_group, :])
            part = part + pltpu.roll(part, LANES // 2, 1)
            row = first + i * grown
            queries[row : row + grown, width : width + LANES] = part.astype(jnp.bfloat16)

    def merge_own(query, fresh_all, peak, total, summed):
        fresh = fresh_all[0:PAD, :]
        fresh_rope = fresh_all[PAD : 2 * PAD, 0:LANES]
        own = lax.dot_general(
            query[:, 0:width], fresh, contract, preferred_element_type=jnp.float32
        )
        own = own + lax.dot_general(
            query[:, width:], fresh_rope, contract, preferred_element_type=jnp.float32
        )
        row_step = lax.broadcasted_iota(jnp.int32, (q_rows, 1), 0) // heads
        columns = [jnp.where(row_step >= j, own[:, j : j + 1], -1e30) for j in range(steps)]
        top = peak
        for column in columns:
            top = jnp.maximum(top, column)
        share = jnp.exp2((peak - top) * factor)
        parts = [
            jnp.where(row_step >= j, jnp.exp2((column - top) * factor), 0.0)
            for j, column in enumerate(columns)
        ]
        denominator = total * share
        for part in parts:
            denominator = denominator + part
        inverse = 1.0 / denominator
        fresh32 = fresh.astype(jnp.float32)
        value = summed * (share * inverse)
        for j, part in enumerate(parts):
            value = value + (part * inverse) * fresh32[j : j + 1, :]
        return value.astype(jnp.bfloat16)

    def spread_keys(cache, rope_keys, matrix):
        grown = raw_group * width // (LANES // 2)
        for start in range(0, rope_rows, raw_group):
            part = spread(matrix, cache[half + start : half + start + raw_group, :])
            first = start * (width // (LANES // 2))
            rope_keys[first : first + grown, :] = part.astype(jnp.bfloat16)

    def kernel(slot, kinds, given_slots, has_placed, *refs):
        refs = list(refs)
        slot_ref, own_ref = refs.pop(0), refs.pop(0)
        guest = refs.pop(0) if "give" in kinds else None
        stay = [refs.pop(0) for _ in range(3)] if "keep" in kinds else None
        caches = [refs.pop(0) for _ in range(2)]
        arrived = [refs.pop(0) for _ in given_slots]
        if has_placed:
            refs.pop(0)
        give = refs.pop(0) if "give" in kinds else None
        placed = refs.pop(0) if ("keep" in kinds or given_slots) else None
        rope_keys, query_all, scores, summed, result, place_sems = refs
        placing = []
        for i, (number, source) in enumerate(zip(given_slots, arrived)):
            copy = pltpu.make_async_copy(
                source, placed.at[row_for(number, 1, slot_ref, own_ref)], place_sems.at[1 + i]
            )
            copy.start()
            placing.append(copy)
        kept_row = row_for(slot, 0, slot_ref, own_ref)
        matrix = spread_matrix(raw_group, width)
        fresh_parts = []
        for number, kind in enumerate(kinds):
            if kind == "give":
                middle = q_rows + token_rope
                lat, raw = guest[slot, 0:q_rows, :], guest[slot, q_rows:middle, :]
                fresh_parts.append(guest[slot, middle : middle + 2 * PAD, :])
            else:
                lat, raw = stay[0][kept_row], stay[1][kept_row]
                fresh_parts.append(stay[2][kept_row])
            put_query(query_all, number, lat, raw, matrix)
        peak = None
        for i, cache in enumerate(caches):
            spread_keys(cache, rope_keys, matrix)
            for start in range(0, half, chunk):
                part = lax.dot_general(
                    query_all[:, 0:width],
                    cache[start : start + chunk, :],
                    contract,
                    preferred_element_type=jnp.float32,
                )
                part = part + lax.dot_general(
                    query_all[:, width:],
                    rope_keys[start : start + chunk, :],
                    contract,
                    preferred_element_type=jnp.float32,
                )
                scores[:, i * half + start : i * half + start + chunk] = part
                high = jnp.max(part, axis=1, keepdims=True)
                peak = high if peak is None else jnp.maximum(peak, high)
        scaled = peak * factor
        total = None
        for start in range(0, 2 * half, chunk):
            weights = jnp.exp2(scores[:, start : start + chunk] * factor - scaled)
            part = jnp.sum(weights, axis=1, keepdims=True)
            value = jnp.dot(
                weights.astype(jnp.bfloat16),
                caches[start // half][start % half : start % half + chunk, :],
                preferred_element_type=jnp.float32,
            )
            if start == 0:
                total = part
                summed[...] = value
            else:
                total = total + part
                summed[...] += value
        for number, kind in enumerate(kinds):
            rows = slice(number * q_rows, (number + 1) * q_rows)
            value = merge_own(
                query_all[rows, :], fresh_parts[number], peak[rows], total[rows], summed[rows, :]
            )
            if kind == "give":
                give[...] = value
            else:
                result[...] = value
                copy = pltpu.make_async_copy(result, placed.at[kept_row], place_sems.at[0])
                copy.start()
                placing.append(copy)
        for copy in placing:
            copy.wait()

    def call(scalars, kinds, slot, guest, stay, caches, arrived, placed):
        count = scalars[0].shape[0]
        n_tok = len(kinds)
        operands = [*scalars]
        if "give" in kinds:
            operands.append(guest)
        if "keep" in kinds:
            operands += stay
        given_slots = tuple(number for number, _ in arrived)
        operands += [*caches, *(value for _, value in arrived)]
        in_specs = [pl.BlockSpec(memory_space=pltpu.SMEM)] * len(scalars)
        in_specs += [pl.BlockSpec(memory_space=pltpu.VMEM)] * (len(operands) - len(scalars))
        out_shape, out_specs, alias = [], [], {}
        if "give" in kinds:
            out_shape.append(jax.ShapeDtypeStruct((q_rows, width), jnp.bfloat16))
            out_specs.append(pl.BlockSpec(memory_space=pltpu.VMEM))
        if "keep" in kinds or arrived:
            out_shape.append(jax.ShapeDtypeStruct((count, q_rows, width), jnp.bfloat16))
            out_specs.append(pl.BlockSpec(memory_space=pl.ANY))
        has_placed = placed is not None
        if has_placed:
            alias = {len(operands): len(out_shape) - 1}
            in_specs.append(pl.BlockSpec(memory_space=pl.ANY))
            operands.append(placed)
        return pl.pallas_call(
            functools.partial(kernel, slot, kinds, given_slots, has_placed),
            out_shape=tuple(out_shape),
            in_specs=in_specs,
            out_specs=tuple(out_specs),
            scratch_shapes=[
                pltpu.VMEM((half, LANES), jnp.bfloat16),
                pltpu.VMEM((n_tok * q_rows, width + LANES), jnp.bfloat16),
                pltpu.VMEM((n_tok * q_rows, 2 * half), jnp.float32),
                pltpu.VMEM((n_tok * q_rows, width), jnp.float32),
                pltpu.VMEM((q_rows, width), jnp.bfloat16),
                pltpu.SemaphoreType.DMA((1 + max(1, len(arrived)),)),
            ],
            input_output_aliases=alias,
            cost_estimate=SMALL,
            compiler_params=pltpu.CompilerParams(vmem_limit_bytes=20 * 1024 * 1024),
            name="attend_" + "_".join(kinds),
        )(*operands)

    return call


def place_kernel(slot, slot_ref, own_ref, source_ref, before, placed_ref, sem):
    row = row_for(slot, 1, slot_ref, own_ref)
    copy = pltpu.make_async_copy(source_ref, placed_ref.at[row], sem)
    copy.start()
    copy.wait()


def place(scalars, slot, source, placed):
    return pl.pallas_call(
        functools.partial(place_kernel, slot),
        out_shape=jax.ShapeDtypeStruct(placed.shape, placed.dtype),
        in_specs=[pl.BlockSpec(memory_space=pltpu.SMEM)] * 2
        + [pl.BlockSpec(memory_space=pltpu.VMEM), pl.BlockSpec(memory_space=pl.ANY)],
        out_specs=pl.BlockSpec(memory_space=pl.ANY),
        scratch_shapes=[pltpu.SemaphoreType.DMA],
        input_output_aliases={3: 0},
        cost_estimate=SMALL,
        compiler_params=pltpu.CompilerParams(vmem_limit_bytes=4 * 1024 * 1024),
        name="place",
    )(*scalars, source, placed)


def dispatch_kernel(experts, block_ref, routes_ref, gate_ref, tokens_ref, out_ref, share_ref):
    block = block_ref[0]
    routes = routes_ref[...]
    gates = gate_ref[...]
    rows = routes.shape[0]
    down = lax.broadcasted_iota(jnp.int32, (rows, rows), 0)
    across = lax.broadcasted_iota(jnp.int32, (rows, rows), 1)
    same = (down == across).astype(jnp.float32)
    slots = experts * CAP
    slot_row = lax.broadcasted_iota(jnp.int32, (slots, rows), 0)
    slot_column = lax.broadcasted_iota(jnp.int32, (rows, slots), 1)
    placing = jnp.zeros((slots, rows), jnp.float32)
    share = jnp.zeros((rows, slots), jnp.float32)
    for k in range(experts):
        expert = lax.rem(block + k, experts)
        hit = routes == expert
        has = jnp.sum(hit.astype(jnp.float32), axis=1, keepdims=True)
        weight = jnp.sum(jnp.where(hit, gates, 0.0), axis=1, keepdims=True)
        has_row = jnp.sum(has * same, axis=0, keepdims=True)
        before_row = jnp.sum(jnp.where(down < across, has, 0.0), axis=0, keepdims=True)
        before = jnp.sum(jnp.where(across < down, has_row, 0.0), axis=1, keepdims=True)
        for c in range(CAP):
            slot = k * CAP + c
            placing += jnp.where((slot_row == slot) & (before_row == c), has_row, 0.0)
            share += jnp.where((slot_column == slot) & (before == c), weight, 0.0)
    out_ref[...] = jnp.dot(
        placing.astype(jnp.bfloat16), tokens_ref[...], preferred_element_type=jnp.float32
    ).astype(jnp.bfloat16)
    share_ref[...] = share


def dispatch(block, routes, gates, tokens, experts):
    slots = experts * CAP
    return pl.pallas_call(
        functools.partial(dispatch_kernel, experts),
        out_shape=(
            jax.ShapeDtypeStruct((slots, tokens.shape[1]), tokens.dtype),
            jax.ShapeDtypeStruct((tokens.shape[0], slots), jnp.float32),
        ),
        in_specs=[pl.BlockSpec(memory_space=pltpu.SMEM)]
        + [pl.BlockSpec(memory_space=pltpu.VMEM)] * 3,
        out_specs=(pl.BlockSpec(memory_space=pltpu.VMEM),) * 2,
        cost_estimate=SMALL,
        compiler_params=pltpu.CompilerParams(vmem_limit_bytes=8 * 1024 * 1024),
        name="dispatch",
    )(block, routes, gates, tokens)


def moved_rows(pieces, places, rows):
    total = None
    for piece, places_of_piece in zip(pieces, places):
        shape = (rows, piece.shape[0])
        row = lax.broadcasted_iota(jnp.int32, shape, 0)
        column = lax.broadcasted_iota(jnp.int32, shape, 1)
        chosen = jnp.zeros(shape, jnp.float32)
        for source, there in places_of_piece:
            chosen += ((row == there) & (column == source)).astype(jnp.float32)
        part = jnp.dot(
            chosen.astype(jnp.bfloat16), piece[...], preferred_element_type=jnp.float32
        )
        total = part if total is None else total + part
    return total.astype(jnp.bfloat16)


def move_kernel(count, plans, *refs):
    for plan, out_ref in zip(plans, refs[count:]):
        used = [i for i in range(count) if plan[i]]
        out_ref[...] = moved_rows(
            [refs[i] for i in used], [plan[i] for i in used], out_ref.shape[0]
        )


def move_rows(arrays, plans, rows, name):
    width = arrays[0].shape[1]
    return pl.pallas_call(
        functools.partial(move_kernel, len(arrays), plans),
        out_shape=tuple(jax.ShapeDtypeStruct((rows, width), jnp.bfloat16) for _ in plans),
        in_specs=[pl.BlockSpec(memory_space=pltpu.VMEM)] * len(arrays),
        out_specs=tuple(pl.BlockSpec(memory_space=pltpu.VMEM) for _ in plans),
        cost_estimate=SMALL,
        compiler_params=pltpu.CompilerParams(vmem_limit_bytes=8 * 1024 * 1024),
        name=name,
    )(*arrays)


def experts_kernel(mine_ref, theirs_ref, gate_hbm, up_hbm, down_hbm, keep_ref, send_ref, *scratch):
    gate_ref, up_ref, down_ref, sems = scratch
    copies = [
        pltpu.make_async_copy(source.at[0], there, sems.at[i])
        for i, (source, there) in enumerate(
            ((gate_hbm, gate_ref), (up_hbm, up_ref), (down_hbm, down_ref))
        )
    ]
    for copy in copies:
        copy.start()
    rows = jnp.concatenate([mine_ref[...], theirs_ref[...]], axis=0)
    copies[0].wait()
    gate = jnp.dot(rows, gate_ref[...], preferred_element_type=jnp.float32)
    copies[1].wait()
    lifted = jnp.dot(rows, up_ref[...], preferred_element_type=jnp.float32)
    hidden = (gate / (1.0 + jnp.exp(-gate)) * lifted).astype(jnp.bfloat16)
    copies[2].wait()
    parts = jnp.dot(hidden, down_ref[...], preferred_element_type=jnp.float32)
    count = mine_ref.shape[0]
    keep_ref[...] = parts[:count]
    send_ref[...] = parts[count:].astype(jnp.bfloat16)


def run_experts(mine, theirs, w_gate, w_up, w_down):
    return pl.pallas_call(
        experts_kernel,
        out_shape=(
            jax.ShapeDtypeStruct(mine.shape, jnp.float32),
            jax.ShapeDtypeStruct(mine.shape, jnp.bfloat16),
        ),
        in_specs=[pl.BlockSpec(memory_space=pltpu.VMEM)] * 2
        + [pl.BlockSpec(memory_space=pl.ANY)] * 3,
        out_specs=(pl.BlockSpec(memory_space=pltpu.VMEM),) * 2,
        scratch_shapes=[
            pltpu.VMEM(w_gate.shape[1:], w_gate.dtype),
            pltpu.VMEM(w_up.shape[1:], w_up.dtype),
            pltpu.VMEM(w_down.shape[1:], w_down.dtype),
            pltpu.SemaphoreType.DMA((3,)),
        ],
        cost_estimate=SMALL,
        compiler_params=pltpu.CompilerParams(vmem_limit_bytes=16 * 1024 * 1024),
        name="experts",
    )(mine, theirs, w_gate, w_up, w_down)


def halve_kernel(sum_ref, arrived_ref, keep_ref, send_ref):
    count = keep_ref.shape[0]
    total = sum_ref[...] + arrived_ref[...].astype(jnp.float32)
    keep_ref[...] = total[:count]
    send_ref[...] = total[count:].astype(jnp.bfloat16)


def halve(kept, arrived):
    shape = (kept.shape[0] // 2, kept.shape[1])
    return pl.pallas_call(
        halve_kernel,
        out_shape=(
            jax.ShapeDtypeStruct(shape, jnp.float32),
            jax.ShapeDtypeStruct(shape, jnp.bfloat16),
        ),
        cost_estimate=SMALL,
        compiler_params=pltpu.CompilerParams(vmem_limit_bytes=8 * 1024 * 1024),
        name="halve",
    )(kept, arrived)


def on_device(
    latent_cache,
    rope_cache,
    q_latent,
    q_rope,
    new_latent,
    new_rope,
    branch_slot,
    moe_input,
    routes,
    route_gate,
    w_gate,
    w_up,
    w_down,
):
    tok_rows, step_count, head_count, width = q_latent.shape
    rope_width = new_rope.shape[-1]
    line = tok_rows // 2
    q_rows = step_count * head_count
    half = latent_cache.shape[1]
    rope_rows = rope_cache.shape[1]
    branch = lax.axis_index("branch")
    own = branch % tok_rows
    low = own % 2
    high = own // 2
    middle = jnp.logical_and(high > 0, high < line - 1)

    outer = [(i, i ^ 1) for i in range(line)]
    inner = [(i, i + 1) for i in range(1, line - 1, 2)]
    inner = inner + [(j, i) for i, j in inner]
    outward = [(i, i ^ 1) for i in range(1, line - 1)]
    own_cache = pack_cache(latent_cache[0], rope_cache[0])
    cache_a = line_hop(own_cache, tok_rows, outer)
    first_b = line_hop(own_cache, tok_rows, inner)
    second_b = line_hop(first_b, tok_rows, outward)
    first_c = line_hop(cache_a, tok_rows, inner)
    second_c = line_hop(first_c, tok_rows, outward)

    q_lat = q_latent.reshape(tok_rows, q_rows, width)
    rope_raw = q_rope.reshape(tok_rows, q_rows * rope_width // width, width)
    fresh = jnp.concatenate(
        [
            jnp.pad(new_latent, ((0, 0), (0, PAD - step_count), (0, 0))),
            jnp.pad(new_rope, ((0, 0), (0, PAD - step_count), (0, width - rope_width))),
        ],
        axis=1,
    )
    scalars = (branch_slot, own[None])
    stay = (q_lat, rope_raw, fresh)

    leave = pack_leaving(branch_slot, after(own[None], own_cache), *stay)
    guest = swapped(leave, "branch", 0)
    attend = build_attend(head_count, step_count, width, half, rope_rows, 32, half // 2)
    model_width = moe_input.shape[-1]
    tok_total = tok_rows * step_count
    device = branch * lax.axis_size("expert") + lax.axis_index("expert")
    experts = lax.axis_size("branch") * lax.axis_size("expert") // SHARDS
    cores = lax.axis_size("expert")
    shard_branches = SHARDS // cores
    block = device // SHARDS
    outgoing, share = dispatch(
        after(block[None], leave),
        routes.reshape(tok_total, -1),
        route_gate.reshape(tok_total, -1),
        moe_input.reshape(tok_total, model_width),
        experts,
    )

    around = shard_branches // 2

    def along(x, shift, flip):
        count = lax.axis_size("branch")
        there = [
            ((i // shard_branches + shift) % experts) * shard_branches
            + ((i % shard_branches) ^ (flip * 2))
            for i in range(count)
        ]
        return lax.ppermute(x, "branch", list(enumerate(there)))

    beside = swapped(outgoing, "branch", 0)
    pair = tuple(
        tuple(tuple((k * CAP + c, i * CAP + c) for c in range(CAP)) for i in range(2))
        for k in range(experts)
    )
    ways = [(k, m) for k in range(experts) for m in range(around)]

    def attend_slot(slot, cache, kinds, waiting, placed):
        keeps = "keep" in kinds
        results = attend(
            scalars,
            kinds,
            slot,
            guest,
            stay,
            cache,
            waiting if keeps else [],
            placed if keeps else None,
        )
        given = results[0] if "give" in kinds else None
        return given, (results[-1] if keeps else placed)

    def both_halves(cache):
        return cache, swapped(cache, "expert", 0)

    guest = after(guest, cache_a, first_b)
    both = ("give", "keep")
    given_0, placed = attend_slot(0, both_halves(own_cache), both, [], None)
    back_0 = swapped(given_0, "branch", 0)
    by_expert = move_rows((outgoing, after(beside, given_0)), pair, 2 * CAP, "pair_rows")
    pieces = [by_expert[k] if (k, m) == (0, 0) else along(by_expert[k], k, m) for k, m in ways]
    given_1, placed = attend_slot(1, both_halves(cache_a), both, [], placed)
    back_1 = swapped(given_1, "branch", 0)


    first_c, second_b, given_1, *pieces = lax.optimization_barrier(
        (first_c, second_b, given_1, *pieces)
    )
    count = len(ways) * CAP
    stacked = tuple(
        tuple((i * CAP + c, i * count + w * CAP + c) for i in range(2) for c in range(CAP))
        for w in range(len(ways))
    )
    (rows,) = move_rows(tuple(pieces), (stacked,), 2 * count, "stack_rows")
    cache_b = jnp.where(middle, first_b, second_b)
    kept, sent = run_experts(rows, swapped(rows, "expert", 0), w_gate, w_up, w_down)
    kept, sent = halve(kept, swapped(sent, "expert", 0))
    given_2, placed = attend_slot(2, both_halves(cache_b), both, [(0, back_0), (1, back_1)], placed)
    back_2 = swapped(given_2, "branch", 0)

    second_c, back_2, kept, sent = lax.optimization_barrier((second_c, back_2, kept, sent))
    cache_c = both_halves(jnp.where(middle, first_c, second_c))
    parts = kept + swapped(sent, "branch", 0).astype(jnp.float32)
    homeward = [
        parts[w * CAP : (w + 1) * CAP].astype(jnp.float32 if way == (0, 0) else jnp.bfloat16)
        for w, way in enumerate(ways)
    ]
    guest, *homeward = lax.optimization_barrier((guest, *homeward))
    given_3, _ = attend_slot(3, cache_c, ("give",), [], None)
    homeward = [after(x, given_3) for x in homeward]
    back_3 = swapped(given_3, "branch", 0)
    _, placed = attend_slot(3, cache_c, ("keep",), [(2, back_2)], placed)
    placed = place(scalars, 3, back_3, placed)
    attended = placed.reshape(tok_rows, step_count, head_count, width)

    sums = [0.0] * experts
    for (k, m), piece in zip(ways, homeward):
        if (k, m) != (0, 0):
            piece = along(piece, -k, m).astype(jnp.float32)
        sums[k] = sums[k] + piece
    sums = jnp.concatenate(sums, axis=0)
    combined = jnp.sum(share[:, :, None] * sums[None, :, :], axis=1)
    moe_out = combined.astype(jnp.bfloat16).reshape(tok_rows, step_count, model_width)
    return (attended, moe_out)


def solution(mesh):
    return jax.shard_map(
        on_device,
        mesh=mesh,
        in_specs=(
            P(("group", "branch"), "expert", None),
            P(("group", "branch"), "expert", None),
            P(("group", "branch", "expert"), None, None, None),
            P(("group", "branch", "expert"), None, None),
            P(("group", "branch", "expert"), None, None),
            P(("group", "branch", "expert"), None, None),
            P(("group", "branch", "expert")),
            P(("group", "branch", "expert"), None, None),
            P(("group", "branch", "expert"), None, None),
            P(("group", "branch", "expert"), None, None),
            P(("branch", "expert"), None, None),
            P(("branch", "expert"), None, None),
            P(("branch", "expert"), None, None),
        ),
        out_specs=(
            P(("group", "branch", "expert"), None, None, None),
            P(("group", "branch", "expert"), None, None),
        ),
        check_vma=False,
    )
```

```python
import functools

import jax
import jax.numpy as jnp
from jax import lax
from jax.experimental import pallas as pl
from jax.experimental.pallas import tpu as pltpu
from jax.sharding import PartitionSpec as P

SHARDS = 8
CAP = 2
LANES = 128
PAD = 16

SMALL = pl.CostEstimate(flops=0, bytes_accessed=1024, transcendentals=0)

softmax_scale = 192.0 ** (-0.5)
log2e = 1.4426950408889634


def after(x, *earlier):
    return lax.optimization_barrier((x, *earlier))[0]


def swapped(x, axis, bit):
    return lax.ppermute(x, axis, [(i, i ^ 1 << bit) for i in range(lax.axis_size(axis))])


def line_hop(x, block, moves):
    pairs = []
    for base in range(0, lax.axis_size("branch"), block):
        for low in range(2):
            pairs += [(base + 2 * i + low, base + 2 * j + low) for i, j in moves]
    return lax.ppermute(x, "branch", pairs)


def pack_cache_kernel(lat_ref, rope_ref, out_ref, sems):
    rows = lat_ref.shape[0]
    copies = [
        pltpu.make_async_copy(lat_ref, out_ref.at[pl.ds(0, rows)], sems.at[0]),
        pltpu.make_async_copy(rope_ref, out_ref.at[pl.ds(rows, rope_ref.shape[0])], sems.at[1]),
    ]
    for copy in copies:
        copy.start()
    for copy in copies:
        copy.wait()


def pack_cache(lat, rope):
    return pl.pallas_call(
        pack_cache_kernel,
        out_shape=jax.ShapeDtypeStruct((lat.shape[0] + rope.shape[0], lat.shape[1]), lat.dtype),
        in_specs=[pl.BlockSpec(memory_space=pltpu.HBM)] * 2,
        out_specs=pl.BlockSpec(memory_space=pltpu.VMEM),
        scratch_shapes=[pltpu.SemaphoreType.DMA((2,))],
        cost_estimate=SMALL,
        compiler_params=pltpu.CompilerParams(vmem_limit_bytes=4 * 1024 * 1024),
        name="pack_cache",
    )(lat, rope)


def row_for(slot, parity, slot_ref, own_ref):
    count = slot_ref.shape[0]
    line = count // 2
    own = own_ref[0]
    high = lax.div(own, 2)
    low = lax.rem(own, 2)
    mine = high
    pair = high + 1 - 2 * lax.rem(high, 2)
    first_half = high < line // 2
    nearer = jnp.where(first_half, line // 2, line // 2 - 1)
    farther = jnp.where(first_half, line - 1, 0)
    position = mine
    for number, place_there in ((1, pair), (2, nearer), (3, farther)):
        position = jnp.where(slot == number, place_there, position)
    wanted = 2 * position + (low if parity == 0 else 1 - low)
    row = jnp.int32(0)
    for r in range(1, count):
        row = row + jnp.where(slot_ref[r] == wanted, r, 0)
    return row


def pack_leaving_kernel(slot_ref, own_ref, q_ref, rope_ref, new_ref, out_ref, sems):
    copies = []
    for slot in range(out_ref.shape[0]):
        row = row_for(slot, 1, slot_ref, own_ref)
        start = 0
        for part, source in enumerate((q_ref, rope_ref, new_ref)):
            count = source.shape[1]
            copy = pltpu.make_async_copy(
                source.at[row], out_ref.at[slot, pl.ds(start, count)], sems.at[slot, part]
            )
            copy.start()
            copies.append(copy)
            start += count
    for copy in copies:
        copy.wait()


def pack_leaving(branch_slot, own, q_lat, q_rope, new):
    slots = branch_slot.shape[0] // 2
    sources = (q_lat, q_rope, new)
    rows = sum(x.shape[1] for x in sources)
    return pl.pallas_call(
        pack_leaving_kernel,
        out_shape=jax.ShapeDtypeStruct((slots, rows, q_lat.shape[2]), q_lat.dtype),
        in_specs=[pl.BlockSpec(memory_space=pltpu.SMEM)] * 2
        + [pl.BlockSpec(memory_space=pltpu.HBM)] * 3,
        out_specs=pl.BlockSpec(memory_space=pltpu.VMEM),
        scratch_shapes=[pltpu.SemaphoreType.DMA((slots, 3))],
        cost_estimate=SMALL,
        compiler_params=pltpu.CompilerParams(vmem_limit_bytes=4 * 1024 * 1024),
        name="pack_leaving",
    )(branch_slot, own, *sources)


def spread_matrix(raw_rows, width):
    per_row = width // (LANES // 2)
    blocks = width // LANES
    shape = (raw_rows * per_row, raw_rows * blocks)
    row = lax.broadcasted_iota(jnp.int32, shape, 0)
    column = lax.broadcasted_iota(jnp.int32, shape, 1)
    wanted = ((row % per_row) // 2) * raw_rows + row // per_row
    return (column == wanted).astype(jnp.bfloat16)


def spread(matrix, raw):
    blocks = raw.shape[1] // LANES
    stacked = jnp.concatenate(
        [raw[:, b * LANES : (b + 1) * LANES] for b in range(blocks)], axis=0
    )
    rows = jnp.dot(matrix, stacked, preferred_element_type=jnp.float32)
    row = lax.broadcasted_iota(jnp.int32, rows.shape, 0)
    lane = lax.broadcasted_iota(jnp.int32, rows.shape, 1)
    return jnp.where(row % 2 == lane // (LANES // 2), rows, 0.0)


def build_attend(heads, steps, width, half, rope_rows, raw_group, chunk):
    q_rows = heads * steps
    token_rope = q_rows // 8

    factor = softmax_scale * log2e
    contract = (((1,), (1,)), ((), ()))

    def put_query_rope(query_all, number, raw_rope, matrix):
        grown = raw_group * width // (LANES // 2)
        for i, start in enumerate(range(0, token_rope, raw_group)):
            part = spread(matrix, raw_rope[start : start + raw_group, :])
            part = part + pltpu.roll(part, LANES // 2, 1)
            row = number * q_rows + i * grown
            query_all[row : row + grown, width : width + LANES] = part.astype(jnp.bfloat16)

    def merge_own(query, fresh_all, peak, total, summed):
        fresh = fresh_all[0:PAD, :]
        fresh_rope = fresh_all[PAD : 2 * PAD, 0:LANES]
        own = lax.dot_general(
            query[:, 0:width], fresh, contract, preferred_element_type=jnp.float32
        )
        own = own + lax.dot_general(
            query[:, width:], fresh_rope, contract, preferred_element_type=jnp.float32
        )
        row_step = lax.broadcasted_iota(jnp.int32, (q_rows, 1), 0) // heads
        columns = [jnp.where(row_step >= j, own[:, j : j + 1], -1e30) for j in range(steps)]
        top = peak
        for column in columns:
            top = jnp.maximum(top, column)
        share = jnp.exp2((peak - top) * factor)
        parts = [
            jnp.where(row_step >= j, jnp.exp2((column - top) * factor), 0.0)
            for j, column in enumerate(columns)
        ]
        denominator = total * share
        for part in parts:
            denominator = denominator + part
        inverse = 1.0 / denominator
        fresh32 = fresh.astype(jnp.float32)
        value = summed * (share * inverse)
        for j, part in enumerate(parts):
            value = value + (part * inverse) * fresh32[j : j + 1, :]
        return value.astype(jnp.bfloat16)

    def put_key_rope(keys, first, raw_rope, matrix):
        grown = raw_group * width // (LANES // 2)
        for i, start in enumerate(range(0, rope_rows, raw_group)):
            part = spread(matrix, raw_rope[start : start + raw_group, :])
            row = first + i * grown
            keys[row : row + grown, width : width + LANES] = part.astype(jnp.bfloat16)

    def kernel(slot, kinds, given_slots, has_placed, *refs):
        refs = list(refs)
        slot_ref, own_ref = refs.pop(0), refs.pop(0)
        guest = refs.pop(0) if "give" in kinds else None
        stay = [refs.pop(0) for _ in range(3)] if "keep" in kinds else None
        caches = [refs.pop(0) for _ in range(2)]
        arrived = [refs.pop(0) for _ in given_slots]
        if has_placed:
            refs.pop(0)
        give = refs.pop(0) if "give" in kinds else None
        placed = refs.pop(0) if ("keep" in kinds or given_slots) else None
        keys, key_rope, query_all, query_rope, fresh, scores, summed, result, staged, sems = refs
        used = [0]

        def start(source, there):
            copy = pltpu.make_async_copy(source, there, sems.at[used[0]])
            used[0] += 1
            copy.start()
            return copy

        kept_row = row_for(slot, 0, slot_ref, own_ref)
        query_copies, rope_copies = [], []
        middle = q_rows + token_rope
        for number, kind in enumerate(kinds):
            if kind == "give":
                lat = guest.at[slot, pl.ds(0, q_rows)]
                raw = guest.at[slot, pl.ds(q_rows, token_rope)]
                new = guest.at[slot, pl.ds(middle, 2 * PAD)]
            else:
                lat, raw, new = (source.at[kept_row] for source in stay)
            rope_copies.append(start(raw, query_rope.at[number]))
            there = query_all.at[pl.ds(number * q_rows, q_rows), pl.ds(0, width)]
            query_copies.append(start(lat, there))
            query_copies.append(start(new, fresh.at[number]))
        key_copies, key_rope_copies = [], []
        for i, cache in enumerate(caches):
            key_rope_copies.append(start(cache.at[pl.ds(half, rope_rows)], key_rope.at[i]))
            for first in range(0, half, chunk):
                there = keys.at[pl.ds(i * half + first, chunk), pl.ds(0, width)]
                key_copies.append(start(cache.at[pl.ds(first, chunk)], there))
        staging = [start(source, staged.at[i]) for i, source in enumerate(arrived)]
        matrix = spread_matrix(raw_group, width)
        for number, copy in enumerate(rope_copies):
            copy.wait()
            put_query_rope(query_all, number, query_rope.at[number], matrix)
        for i, copy in enumerate(key_rope_copies):
            copy.wait()
            put_key_rope(keys, i * half, key_rope.at[i], matrix)
        for copy in query_copies:
            copy.wait()
        peak = None
        for number, copy in enumerate(key_copies):
            copy.wait()
            first = number * chunk
            part = lax.dot_general(
                query_all[...],
                keys[first : first + chunk, :],
                contract,
                preferred_element_type=jnp.float32,
            )
            scores[:, first : first + chunk] = part
            high = jnp.max(part, axis=1, keepdims=True)
            peak = high if peak is None else jnp.maximum(peak, high)
        placing = []
        for i, (number, copy) in enumerate(zip(given_slots, staging)):
            copy.wait()
            placing.append(
                start(staged.at[i], placed.at[row_for(number, 1, slot_ref, own_ref)])
            )
        scaled = peak * factor
        total = None
        for first in range(0, 2 * half, chunk):
            weights = jnp.exp2(scores[:, first : first + chunk] * factor - scaled)
            part = jnp.sum(weights, axis=1, keepdims=True)
            value = jnp.dot(
                weights.astype(jnp.bfloat16),
                keys[first : first + chunk, 0:width],
                preferred_element_type=jnp.float32,
            )
            if first == 0:
                total = part
                summed[...] = value
            else:
                total = total + part
                summed[...] += value
        for number, kind in enumerate(kinds):
            rows = slice(number * q_rows, (number + 1) * q_rows)
            result[number] = merge_own(
                query_all[rows, :], fresh[number], peak[rows], total[rows], summed[rows, :]
            )
            there = give if kind == "give" else placed.at[kept_row]
            placing.append(start(result.at[number], there))
        for copy in placing:
            copy.wait()

    def call(scalars, kinds, slot, guest, stay, caches, arrived, placed):
        count = scalars[0].shape[0]
        n_tok = len(kinds)
        hbm = pl.BlockSpec(memory_space=pltpu.HBM)
        operands = [*scalars]
        if "give" in kinds:
            operands.append(guest)
        if "keep" in kinds:
            operands += stay
        given_slots = tuple(number for number, _ in arrived)
        operands += [*caches, *(value for _, value in arrived)]
        in_specs = [pl.BlockSpec(memory_space=pltpu.SMEM)] * len(scalars)
        in_specs += [hbm] * (len(operands) - len(scalars))
        out_shape, alias = [], {}
        if "give" in kinds:
            out_shape.append(jax.ShapeDtypeStruct((q_rows, width), jnp.bfloat16))
        if "keep" in kinds or arrived:
            out_shape.append(jax.ShapeDtypeStruct((count, q_rows, width), jnp.bfloat16))
        has_placed = placed is not None
        if has_placed:
            alias = {len(operands): len(out_shape) - 1}
            in_specs.append(hbm)
            operands.append(placed)
        copies = 4 * n_tok + 2 * (1 + half // chunk) + 2 * len(arrived)
        return pl.pallas_call(
            functools.partial(kernel, slot, kinds, given_slots, has_placed),
            out_shape=tuple(out_shape),
            in_specs=in_specs,
            out_specs=(hbm,) * len(out_shape),
            scratch_shapes=[
                pltpu.VMEM((2 * half, width + LANES), jnp.bfloat16),
                pltpu.VMEM((2, rope_rows, width), jnp.bfloat16),
                pltpu.VMEM((n_tok * q_rows, width + LANES), jnp.bfloat16),
                pltpu.VMEM((n_tok, token_rope, width), jnp.bfloat16),
                pltpu.VMEM((n_tok, 2 * PAD, width), jnp.bfloat16),
                pltpu.VMEM((n_tok * q_rows, 2 * half), jnp.float32),
                pltpu.VMEM((n_tok * q_rows, width), jnp.float32),
                pltpu.VMEM((n_tok, q_rows, width), jnp.bfloat16),
                pltpu.VMEM((max(1, len(arrived)), q_rows, width), jnp.bfloat16),
                pltpu.SemaphoreType.DMA((copies,)),
            ],
            input_output_aliases=alias,
            cost_estimate=SMALL,
            compiler_params=pltpu.CompilerParams(vmem_limit_bytes=20 * 1024 * 1024),
            name="attend_" + "_".join(kinds),
        )(*operands)

    return call


def place_kernel(slot, slot_ref, own_ref, source_ref, before, placed_ref, sem):
    row = row_for(slot, 1, slot_ref, own_ref)
    copy = pltpu.make_async_copy(source_ref, placed_ref.at[row], sem)
    copy.start()
    copy.wait()


def place(scalars, slot, source, placed):
    return pl.pallas_call(
        functools.partial(place_kernel, slot),
        out_shape=jax.ShapeDtypeStruct(placed.shape, placed.dtype),
        in_specs=[pl.BlockSpec(memory_space=pltpu.SMEM)] * 2
        + [pl.BlockSpec(memory_space=pltpu.VMEM), pl.BlockSpec(memory_space=pltpu.HBM)],
        out_specs=pl.BlockSpec(memory_space=pltpu.HBM),
        scratch_shapes=[pltpu.SemaphoreType.DMA],
        input_output_aliases={3: 0},
        cost_estimate=SMALL,
        compiler_params=pltpu.CompilerParams(vmem_limit_bytes=4 * 1024 * 1024),
        name="place",
    )(*scalars, source, placed)


def dispatch_kernel(experts, block_ref, routes_ref, gate_ref, tokens_ref, out_ref, share_ref):
    block = block_ref[0]
    routes = routes_ref[...]
    gates = gate_ref[...]
    rows = routes.shape[0]
    down = lax.broadcasted_iota(jnp.int32, (rows, rows), 0)
    across = lax.broadcasted_iota(jnp.int32, (rows, rows), 1)
    same = (down == across).astype(jnp.float32)
    slots = experts * CAP
    slot_row = lax.broadcasted_iota(jnp.int32, (slots, rows), 0)
    slot_column = lax.broadcasted_iota(jnp.int32, (rows, slots), 1)
    placing = jnp.zeros((slots, rows), jnp.float32)
    share = jnp.zeros((rows, slots), jnp.float32)
    for k in range(experts):
        expert = lax.rem(block + k, experts)
        hit = routes == expert
        has = jnp.sum(hit.astype(jnp.float32), axis=1, keepdims=True)
        weight = jnp.sum(jnp.where(hit, gates, 0.0), axis=1, keepdims=True)
        has_row = jnp.sum(has * same, axis=0, keepdims=True)
        before_row = jnp.sum(jnp.where(down < across, has, 0.0), axis=0, keepdims=True)
        before = jnp.sum(jnp.where(across < down, has_row, 0.0), axis=1, keepdims=True)
        for c in range(CAP):
            slot = k * CAP + c
            placing += jnp.where((slot_row == slot) & (before_row == c), has_row, 0.0)
            share += jnp.where((slot_column == slot) & (before == c), weight, 0.0)
    out_ref[...] = jnp.dot(
        placing.astype(jnp.bfloat16), tokens_ref[...], preferred_element_type=jnp.float32
    ).astype(jnp.bfloat16)
    share_ref[...] = share


def dispatch(block, routes, gates, tokens, experts):
    slots = experts * CAP
    return pl.pallas_call(
        functools.partial(dispatch_kernel, experts),
        out_shape=(
            jax.ShapeDtypeStruct((slots, tokens.shape[1]), tokens.dtype),
            jax.ShapeDtypeStruct((tokens.shape[0], slots), jnp.float32),
        ),
        in_specs=[pl.BlockSpec(memory_space=pltpu.SMEM)]
        + [pl.BlockSpec(memory_space=pltpu.VMEM)] * 3,
        out_specs=(pl.BlockSpec(memory_space=pltpu.VMEM),) * 2,
        cost_estimate=SMALL,
        compiler_params=pltpu.CompilerParams(vmem_limit_bytes=8 * 1024 * 1024),
        name="dispatch",
    )(block, routes, gates, tokens)


def moved_rows(pieces, places, rows):
    total = None
    for piece, places_of_piece in zip(pieces, places):
        shape = (rows, piece.shape[0])
        row = lax.broadcasted_iota(jnp.int32, shape, 0)
        column = lax.broadcasted_iota(jnp.int32, shape, 1)
        chosen = jnp.zeros(shape, jnp.float32)
        for source, there in places_of_piece:
            chosen += ((row == there) & (column == source)).astype(jnp.float32)
        part = jnp.dot(
            chosen.astype(jnp.bfloat16), piece[...], preferred_element_type=jnp.float32
        )
        total = part if total is None else total + part
    return total.astype(jnp.bfloat16)


def move_kernel(count, plans, *refs):
    for plan, out_ref in zip(plans, refs[count:]):
        used = [i for i in range(count) if plan[i]]
        out_ref[...] = moved_rows(
            [refs[i] for i in used], [plan[i] for i in used], out_ref.shape[0]
        )


def move_rows(arrays, plans, rows, name):
    width = arrays[0].shape[1]
    return pl.pallas_call(
        functools.partial(move_kernel, len(arrays), plans),
        out_shape=tuple(jax.ShapeDtypeStruct((rows, width), jnp.bfloat16) for _ in plans),
        in_specs=[pl.BlockSpec(memory_space=pltpu.VMEM)] * len(arrays),
        out_specs=tuple(pl.BlockSpec(memory_space=pltpu.VMEM) for _ in plans),
        cost_estimate=SMALL,
        compiler_params=pltpu.CompilerParams(vmem_limit_bytes=8 * 1024 * 1024),
        name=name,
    )(*arrays)


def experts_kernel(mine_ref, theirs_ref, gate_hbm, up_hbm, down_hbm, keep_ref, send_ref, *scratch):
    gate_ref, up_ref, down_ref, sems = scratch
    copies = [
        pltpu.make_async_copy(source.at[0], there, sems.at[i])
        for i, (source, there) in enumerate(
            ((gate_hbm, gate_ref), (up_hbm, up_ref), (down_hbm, down_ref))
        )
    ]
    for copy in copies:
        copy.start()
    rows = jnp.concatenate([mine_ref[...], theirs_ref[...]], axis=0)
    copies[0].wait()
    gate = jnp.dot(rows, gate_ref[...], preferred_element_type=jnp.float32)
    copies[1].wait()
    lifted = jnp.dot(rows, up_ref[...], preferred_element_type=jnp.float32)
    hidden = (gate / (1.0 + jnp.exp(-gate)) * lifted).astype(jnp.bfloat16)
    copies[2].wait()
    parts = jnp.dot(hidden, down_ref[...], preferred_element_type=jnp.float32)
    count = mine_ref.shape[0]
    keep_ref[...] = parts[:count]
    send_ref[...] = parts[count:].astype(jnp.bfloat16)


def run_experts(mine, theirs, w_gate, w_up, w_down):
    return pl.pallas_call(
        experts_kernel,
        out_shape=(
            jax.ShapeDtypeStruct(mine.shape, jnp.float32),
            jax.ShapeDtypeStruct(mine.shape, jnp.bfloat16),
        ),
        in_specs=[pl.BlockSpec(memory_space=pltpu.VMEM)] * 2
        + [pl.BlockSpec(memory_space=pltpu.HBM)] * 3,
        out_specs=(pl.BlockSpec(memory_space=pltpu.VMEM),) * 2,
        scratch_shapes=[
            pltpu.VMEM(w_gate.shape[1:], w_gate.dtype),
            pltpu.VMEM(w_up.shape[1:], w_up.dtype),
            pltpu.VMEM(w_down.shape[1:], w_down.dtype),
            pltpu.SemaphoreType.DMA((3,)),
        ],
        cost_estimate=SMALL,
        compiler_params=pltpu.CompilerParams(vmem_limit_bytes=16 * 1024 * 1024),
        name="experts",
    )(mine, theirs, w_gate, w_up, w_down)


def halve_kernel(sum_ref, arrived_ref, keep_ref, send_ref):
    count = keep_ref.shape[0]
    total = sum_ref[...] + arrived_ref[...].astype(jnp.float32)
    keep_ref[...] = total[:count]
    send_ref[...] = total[count:].astype(jnp.bfloat16)


def halve(kept, arrived):
    shape = (kept.shape[0] // 2, kept.shape[1])
    return pl.pallas_call(
        halve_kernel,
        out_shape=(
            jax.ShapeDtypeStruct(shape, jnp.float32),
            jax.ShapeDtypeStruct(shape, jnp.bfloat16),
        ),
        cost_estimate=SMALL,
        compiler_params=pltpu.CompilerParams(vmem_limit_bytes=8 * 1024 * 1024),
        name="halve",
    )(kept, arrived)


def on_device(
    latent_cache,
    rope_cache,
    q_latent,
    q_rope,
    new_latent,
    new_rope,
    branch_slot,
    moe_input,
    routes,
    route_gate,
    w_gate,
    w_up,
    w_down,
):
    tok_rows, step_count, head_count, width = q_latent.shape
    rope_width = new_rope.shape[-1]
    line = tok_rows // 2
    q_rows = step_count * head_count
    half = latent_cache.shape[1]
    rope_rows = rope_cache.shape[1]
    branch = lax.axis_index("branch")
    own = branch % tok_rows
    low = own % 2
    high = own // 2
    middle = jnp.logical_and(high > 0, high < line - 1)

    outer = [(i, i ^ 1) for i in range(line)]
    inner = [(i, i + 1) for i in range(1, line - 1, 2)]
    inner = inner + [(j, i) for i, j in inner]
    outward = [(i, i ^ 1) for i in range(1, line - 1)]
    own_cache = pack_cache(latent_cache[0], rope_cache[0])
    cache_a = line_hop(own_cache, tok_rows, outer)
    first_b = line_hop(own_cache, tok_rows, inner)

    q_lat = q_latent.reshape(tok_rows, q_rows, width)
    rope_raw = q_rope.reshape(tok_rows, q_rows * rope_width // width, width)
    fresh = jnp.concatenate(
        [
            jnp.pad(new_latent, ((0, 0), (0, PAD - step_count), (0, 0))),
            jnp.pad(new_rope, ((0, 0), (0, PAD - step_count), (0, width - rope_width))),
        ],
        axis=1,
    )
    scalars = (branch_slot, own[None])
    stay = (q_lat, rope_raw, fresh)

    leave = pack_leaving(branch_slot, after(own[None], own_cache), *stay)
    guest = swapped(leave, "branch", 0)
    attend = build_attend(head_count, step_count, width, half, rope_rows, 32, half // 2)
    model_width = moe_input.shape[-1]
    tok_total = tok_rows * step_count
    device = branch * lax.axis_size("expert") + lax.axis_index("expert")
    experts = lax.axis_size("branch") * lax.axis_size("expert") // SHARDS
    cores = lax.axis_size("expert")
    shard_branches = SHARDS // cores
    block = device // SHARDS
    outgoing, share = dispatch(
        after(block[None], leave),
        routes.reshape(tok_total, -1),
        route_gate.reshape(tok_total, -1),
        moe_input.reshape(tok_total, model_width),
        experts,
    )

    around = shard_branches // 2

    def along(x, shift, flip):
        count = lax.axis_size("branch")
        there = [
            ((i // shard_branches + shift) % experts) * shard_branches
            + ((i % shard_branches) ^ (flip * 2))
            for i in range(count)
        ]
        return lax.ppermute(x, "branch", list(enumerate(there)))

    beside = swapped(outgoing, "branch", 0)
    cache_a, first_b, outgoing = lax.optimization_barrier((cache_a, first_b, outgoing))
    second_b = line_hop(first_b, tok_rows, outward)
    first_c = line_hop(cache_a, tok_rows, inner)
    pair = tuple(
        tuple(tuple((k * CAP + c, i * CAP + c) for c in range(CAP)) for i in range(2))
        for k in range(experts)
    )
    ways = [(k, m) for k in range(experts) for m in range(around)]

    def attend_slot(slot, cache, kinds, waiting, placed):
        keeps = "keep" in kinds
        results = attend(
            scalars,
            kinds,
            slot,
            guest,
            stay,
            cache,
            waiting if keeps else [],
            placed if keeps else None,
        )
        given = results[0] if "give" in kinds else None
        return given, (results[-1] if keeps else placed)

    def both_halves(cache):
        return cache, swapped(cache, "expert", 0)

    guest = after(guest, cache_a, first_b)
    both = ("give", "keep")
    given_0, placed = attend_slot(0, both_halves(own_cache), both, [], None)
    back_0 = swapped(given_0, "branch", 0)
    by_expert = move_rows((outgoing, after(beside, given_0)), pair, 2 * CAP, "pair_rows")
    pieces = [by_expert[k] if (k, m) == (0, 0) else along(by_expert[k], k, m) for k, m in ways]
    given_1, placed = attend_slot(1, both_halves(cache_a), both, [], placed)
    back_1 = swapped(given_1, "branch", 0)
    pieces = [after(piece, given_1) for piece in pieces]


    first_c, second_b, given_1, *pieces = lax.optimization_barrier(
        (first_c, second_b, given_1, *pieces)
    )
    second_c = line_hop(first_c, tok_rows, outward)
    count = len(ways) * CAP
    stacked = tuple(
        tuple((i * CAP + c, i * count + w * CAP + c) for i in range(2) for c in range(CAP))
        for w in range(len(ways))
    )
    (rows,) = move_rows(tuple(pieces), (stacked,), 2 * count, "stack_rows")
    cache_b = jnp.where(middle, first_b, second_b)
    theirs = swapped(rows, "expert", 0)
    rows, theirs, back_0, back_1 = lax.optimization_barrier((rows, theirs, back_0, back_1))
    kept, sent = run_experts(rows, theirs, w_gate, w_up, w_down)
    kept, sent = halve(kept, swapped(sent, "expert", 0))
    given_2, placed = attend_slot(2, both_halves(cache_b), both, [], placed)
    back_2 = swapped(given_2, "branch", 0)

    second_c, back_2, kept, sent = lax.optimization_barrier((second_c, back_2, kept, sent))
    cache_c = both_halves(jnp.where(middle, first_c, second_c))
    parts = kept + swapped(sent, "branch", 0).astype(jnp.float32)
    homeward = [
        parts[w * CAP : (w + 1) * CAP].astype(jnp.float32 if way == (0, 0) else jnp.bfloat16)
        for w, way in enumerate(ways)
    ]
    guest, *homeward = lax.optimization_barrier((guest, *homeward))
    given_3, _ = attend_slot(3, cache_c, ("give",), [], None)
    homeward = [after(x, given_3) for x in homeward]
    back_3 = swapped(given_3, "branch", 0)
    _, placed = attend_slot(3, cache_c, ("keep",), [(0, back_0), (1, back_1), (2, back_2)], placed)
    placed = place(scalars, 3, back_3, placed)
    attended = placed.reshape(tok_rows, step_count, head_count, width)

    sums = [0.0] * experts
    for (k, m), piece in zip(ways, homeward):
        if (k, m) != (0, 0):
            piece = along(piece, -k, m).astype(jnp.float32)
        sums[k] = sums[k] + piece
    sums = jnp.concatenate(sums, axis=0)
    combined = jnp.sum(share[:, :, None] * sums[None, :, :], axis=1)
    moe_out = combined.astype(jnp.bfloat16).reshape(tok_rows, step_count, model_width)
    return (attended, moe_out)


def solution(mesh):
    return jax.shard_map(
        on_device,
        mesh=mesh,
        in_specs=(
            P(("group", "branch"), "expert", None),
            P(("group", "branch"), "expert", None),
            P(("group", "branch", "expert"), None, None, None),
            P(("group", "branch", "expert"), None, None),
            P(("group", "branch", "expert"), None, None),
            P(("group", "branch", "expert"), None, None),
            P(("group", "branch", "expert")),
            P(("group", "branch", "expert"), None, None),
            P(("group", "branch", "expert"), None, None),
            P(("group", "branch", "expert"), None, None),
            P(("branch", "expert"), None, None),
            P(("branch", "expert"), None, None),
            P(("branch", "expert"), None, None),
        ),
        out_specs=(
            P(("group", "branch", "expert"), None, None, None),
            P(("group", "branch", "expert"), None, None),
        ),
        check_vma=False,
    )
```

```python
import functools

import jax
import jax.numpy as jnp
from jax import lax
from jax.experimental import pallas as pl
from jax.experimental.pallas import tpu as pltpu
from jax.sharding import PartitionSpec as P

SHARDS = 8
CAP = 2
LANES = 128
PAD = 16

SMALL = pl.CostEstimate(flops=0, bytes_accessed=1024, transcendentals=0)

LARGE = 62 * 1024 * 1024

softmax_scale = 192.0 ** (-0.5)
log2e = 1.4426950408889634


def after(x, *earlier):
    return lax.optimization_barrier((x, *earlier))[0]


def swapped(x, axis, bit):
    return lax.ppermute(x, axis, [(i, i ^ 1 << bit) for i in range(lax.axis_size(axis))])


def line_hop(x, block, moves):
    pairs = []
    for base in range(0, lax.axis_size("branch"), block):
        for low in range(2):
            pairs += [(base + 2 * i + low, base + 2 * j + low) for i, j in moves]
    return lax.ppermute(x, "branch", pairs)


def pack_cache_kernel(lat_ref, rope_ref, out_ref, sems):
    rows = lat_ref.shape[0]
    copies = [
        pltpu.make_async_copy(lat_ref, out_ref.at[pl.ds(0, rows)], sems.at[0]),
        pltpu.make_async_copy(rope_ref, out_ref.at[pl.ds(rows, rope_ref.shape[0])], sems.at[1]),
    ]
    for copy in copies:
        copy.start()
    for copy in copies:
        copy.wait()


def pack_cache(lat, rope):
    return pl.pallas_call(
        pack_cache_kernel,
        out_shape=jax.ShapeDtypeStruct((lat.shape[0] + rope.shape[0], lat.shape[1]), lat.dtype),
        in_specs=[pl.BlockSpec(memory_space=pltpu.HBM)] * 2,
        out_specs=pl.BlockSpec(memory_space=pltpu.VMEM),
        scratch_shapes=[pltpu.SemaphoreType.DMA((2,))],
        cost_estimate=SMALL,
        compiler_params=pltpu.CompilerParams(vmem_limit_bytes=LARGE),
        name="pack_cache",
    )(lat, rope)


def row_for(slot, parity, slot_ref, own_ref):
    count = slot_ref.shape[0]
    line = count // 2
    own = own_ref[0]
    high = lax.div(own, 2)
    low = lax.rem(own, 2)
    mine = high
    pair = high + 1 - 2 * lax.rem(high, 2)
    first_half = high < line // 2
    nearer = jnp.where(first_half, line // 2, line // 2 - 1)
    farther = jnp.where(first_half, line - 1, 0)
    position = mine
    for number, place_there in ((1, pair), (2, nearer), (3, farther)):
        position = jnp.where(slot == number, place_there, position)
    wanted = 2 * position + (low if parity == 0 else 1 - low)
    row = jnp.int32(0)
    for r in range(1, count):
        row = row + jnp.where(slot_ref[r] == wanted, r, 0)
    return row


def pack_leaving_kernel(slot_ref, own_ref, q_ref, rope_ref, new_ref, out_ref, sems):
    copies = []
    for slot in range(out_ref.shape[0]):
        row = row_for(slot, 1, slot_ref, own_ref)
        start = 0
        for part, source in enumerate((q_ref, rope_ref, new_ref)):
            count = source.shape[1]
            copy = pltpu.make_async_copy(
                source.at[row], out_ref.at[slot, pl.ds(start, count)], sems.at[slot, part]
            )
            copy.start()
            copies.append(copy)
            start += count
    for copy in copies:
        copy.wait()


def pack_leaving(branch_slot, own, q_lat, q_rope, new):
    slots = branch_slot.shape[0] // 2
    sources = (q_lat, q_rope, new)
    rows = sum(x.shape[1] for x in sources)
    return pl.pallas_call(
        pack_leaving_kernel,
        out_shape=jax.ShapeDtypeStruct((slots, rows, q_lat.shape[2]), q_lat.dtype),
        in_specs=[pl.BlockSpec(memory_space=pltpu.SMEM)] * 2
        + [pl.BlockSpec(memory_space=pltpu.HBM)] * 3,
        out_specs=pl.BlockSpec(memory_space=pltpu.VMEM),
        scratch_shapes=[pltpu.SemaphoreType.DMA((slots, 3))],
        cost_estimate=SMALL,
        compiler_params=pltpu.CompilerParams(vmem_limit_bytes=LARGE),
        name="pack_leaving",
    )(branch_slot, own, *sources)


def spread_matrix(raw_rows, width):
    per_row = width // (LANES // 2)
    blocks = width // LANES
    shape = (raw_rows * per_row, raw_rows * blocks)
    row = lax.broadcasted_iota(jnp.int32, shape, 0)
    column = lax.broadcasted_iota(jnp.int32, shape, 1)
    wanted = ((row % per_row) // 2) * raw_rows + row // per_row
    return (column == wanted).astype(jnp.bfloat16)


def spread(matrix, raw):
    blocks = raw.shape[1] // LANES
    stacked = jnp.concatenate(
        [raw[:, b * LANES : (b + 1) * LANES] for b in range(blocks)], axis=0
    )
    rows = jnp.dot(matrix, stacked, preferred_element_type=jnp.float32)
    row = lax.broadcasted_iota(jnp.int32, rows.shape, 0)
    lane = lax.broadcasted_iota(jnp.int32, rows.shape, 1)
    return jnp.where(row % 2 == lane // (LANES // 2), rows, 0.0)


def build_attend(heads, steps, width, half, rope_rows, raw_group, chunk):
    q_rows = heads * steps
    token_rope = q_rows // 8

    factor = softmax_scale * log2e
    contract = (((1,), (1,)), ((), ()))

    def put_query_rope(rope_queries, number, raw_rope, matrix):
        grown = raw_group * width // (LANES // 2)
        for i, start in enumerate(range(0, token_rope, raw_group)):
            part = spread(matrix, raw_rope[start : start + raw_group, :])
            part = part + pltpu.roll(part, LANES // 2, 1)
            row = number * q_rows + i * grown
            rope_queries[row : row + grown, :] = part.astype(jnp.bfloat16)

    def merge_own(query, rope_query, fresh_all, peak, total, summed):
        fresh = fresh_all[0:PAD, :]
        fresh_rope = fresh_all[PAD : 2 * PAD, 0:LANES]
        own = lax.dot_general(
            query, fresh, contract, preferred_element_type=jnp.float32
        )
        own = own + lax.dot_general(
            rope_query, fresh_rope, contract, preferred_element_type=jnp.float32
        )
        row_step = lax.broadcasted_iota(jnp.int32, (q_rows, 1), 0) // heads
        columns = [jnp.where(row_step >= j, own[:, j : j + 1], -1e30) for j in range(steps)]
        top = peak
        for column in columns:
            top = jnp.maximum(top, column)
        share = jnp.exp2((peak - top) * factor)
        parts = [
            jnp.where(row_step >= j, jnp.exp2((column - top) * factor), 0.0)
            for j, column in enumerate(columns)
        ]
        denominator = total * share
        for part in parts:
            denominator = denominator + part
        inverse = 1.0 / denominator
        fresh32 = fresh.astype(jnp.float32)
        value = summed * (share * inverse)
        for j, part in enumerate(parts):
            value = value + (part * inverse) * fresh32[j : j + 1, :]
        return value.astype(jnp.bfloat16)

    def put_key_rope(rope_keys, first, raw_rope, matrix):
        grown = raw_group * width // (LANES // 2)
        for i, start in enumerate(range(0, rope_rows, raw_group)):
            part = spread(matrix, raw_rope[start : start + raw_group, :])
            row = first + i * grown
            rope_keys[row : row + grown, :] = part.astype(jnp.bfloat16)

    def kernel(slot, kinds, given_slots, has_placed, *refs):
        refs = list(refs)
        slot_ref, own_ref = refs.pop(0), refs.pop(0)
        guest = refs.pop(0) if "give" in kinds else None
        stay = [refs.pop(0) for _ in range(3)] if "keep" in kinds else None
        caches = [refs.pop(0) for _ in range(2)]
        arrived = [refs.pop(0) for _ in given_slots]
        if has_placed:
            refs.pop(0)
        give = refs.pop(0) if "give" in kinds else None
        placed = refs.pop(0) if ("keep" in kinds or given_slots) else None
        keys, rope_keys, key_rope, query_all, rope_queries, query_rope = refs[:6]
        fresh, scores, summed, result, staged, sems = refs[6:]
        used = [0]

        def start(source, there):
            copy = pltpu.make_async_copy(source, there, sems.at[used[0]])
            used[0] += 1
            copy.start()
            return copy

        kept_row = row_for(slot, 0, slot_ref, own_ref)
        query_copies, rope_copies = [], []
        middle = q_rows + token_rope
        for number, kind in enumerate(kinds):
            if kind == "give":
                lat = guest.at[slot, pl.ds(0, q_rows)]
                raw = guest.at[slot, pl.ds(q_rows, token_rope)]
                new = guest.at[slot, pl.ds(middle, 2 * PAD)]
            else:
                lat, raw, new = (source.at[kept_row] for source in stay)
            rope_copies.append(start(raw, query_rope.at[number]))
            there = query_all.at[pl.ds(number * q_rows, q_rows)]
            query_copies.append(start(lat, there))
            query_copies.append(start(new, fresh.at[number]))
        key_copies, key_rope_copies = [], []
        for i, cache in enumerate(caches):
            key_rope_copies.append(start(cache.at[pl.ds(half, rope_rows)], key_rope.at[i]))
            for first in range(0, half, chunk):
                there = keys.at[pl.ds(i * half + first, chunk)]
                key_copies.append(start(cache.at[pl.ds(first, chunk)], there))
        staging = [start(source, staged.at[i]) for i, source in enumerate(arrived)]
        matrix = spread_matrix(raw_group, width)
        for number, copy in enumerate(rope_copies):
            copy.wait()
            put_query_rope(rope_queries, number, query_rope.at[number], matrix)
        for i, copy in enumerate(key_rope_copies):
            copy.wait()
            put_key_rope(rope_keys, i * half, key_rope.at[i], matrix)
        for copy in query_copies:
            copy.wait()
        peak = None
        for number, copy in enumerate(key_copies):
            copy.wait()
            first = number * chunk
            part = lax.dot_general(
                query_all[...],
                keys[first : first + chunk, :],
                contract,
                preferred_element_type=jnp.float32,
            )
            part = part + lax.dot_general(
                rope_queries[...],
                rope_keys[first : first + chunk, :],
                contract,
                preferred_element_type=jnp.float32,
            )
            scores[:, first : first + chunk] = part
            high = jnp.max(part, axis=1, keepdims=True)
            peak = high if peak is None else jnp.maximum(peak, high)
        placing = []
        for i, (number, copy) in enumerate(zip(given_slots, staging)):
            copy.wait()
            placing.append(
                start(staged.at[i], placed.at[row_for(number, 1, slot_ref, own_ref)])
            )
        scaled = peak * factor
        total = None
        for first in range(0, 2 * half, chunk):
            weights = jnp.exp2(scores[:, first : first + chunk] * factor - scaled)
            part = jnp.sum(weights, axis=1, keepdims=True)
            value = jnp.dot(
                weights.astype(jnp.bfloat16),
                keys[first : first + chunk, :],
                preferred_element_type=jnp.float32,
            )
            if first == 0:
                total = part
                summed[...] = value
            else:
                total = total + part
                summed[...] += value
        for number, kind in enumerate(kinds):
            rows = slice(number * q_rows, (number + 1) * q_rows)
            result[number] = merge_own(
                query_all[rows, :],
                rope_queries[rows, :],
                fresh[number],
                peak[rows],
                total[rows],
                summed[rows, :],
            )
            there = give if kind == "give" else placed.at[kept_row]
            placing.append(start(result.at[number], there))
        for copy in placing:
            copy.wait()

    def call(scalars, kinds, slot, guest, stay, caches, arrived, placed):
        count = scalars[0].shape[0]
        n_tok = len(kinds)
        hbm = pl.BlockSpec(memory_space=pltpu.HBM)
        operands = [*scalars]
        if "give" in kinds:
            operands.append(guest)
        if "keep" in kinds:
            operands += stay
        given_slots = tuple(number for number, _ in arrived)
        operands += [*caches, *(value for _, value in arrived)]
        in_specs = [pl.BlockSpec(memory_space=pltpu.SMEM)] * len(scalars)
        in_specs += [hbm] * (len(operands) - len(scalars))
        out_shape, alias = [], {}
        if "give" in kinds:
            out_shape.append(jax.ShapeDtypeStruct((q_rows, width), jnp.bfloat16))
        if "keep" in kinds or arrived:
            out_shape.append(jax.ShapeDtypeStruct((count, q_rows, width), jnp.bfloat16))
        has_placed = placed is not None
        if has_placed:
            alias = {len(operands): len(out_shape) - 1}
            in_specs.append(hbm)
            operands.append(placed)
        copies = 4 * n_tok + 2 * (1 + half // chunk) + 2 * len(arrived)
        return pl.pallas_call(
            functools.partial(kernel, slot, kinds, given_slots, has_placed),
            out_shape=tuple(out_shape),
            in_specs=in_specs,
            out_specs=(hbm,) * len(out_shape),
            scratch_shapes=[
                pltpu.VMEM((2 * half, width), jnp.bfloat16),
                pltpu.VMEM((2 * half, LANES), jnp.bfloat16),
                pltpu.VMEM((2, rope_rows, width), jnp.bfloat16),
                pltpu.VMEM((n_tok * q_rows, width), jnp.bfloat16),
                pltpu.VMEM((n_tok * q_rows, LANES), jnp.bfloat16),
                pltpu.VMEM((n_tok, token_rope, width), jnp.bfloat16),
                pltpu.VMEM((n_tok, 2 * PAD, width), jnp.bfloat16),
                pltpu.VMEM((n_tok * q_rows, 2 * half), jnp.float32),
                pltpu.VMEM((n_tok * q_rows, width), jnp.float32),
                pltpu.VMEM((n_tok, q_rows, width), jnp.bfloat16),
                pltpu.VMEM((max(1, len(arrived)), q_rows, width), jnp.bfloat16),
                pltpu.SemaphoreType.DMA((copies,)),
            ],
            input_output_aliases=alias,
            cost_estimate=SMALL,
            compiler_params=pltpu.CompilerParams(vmem_limit_bytes=LARGE),
            name="attend_" + "_".join(kinds),
        )(*operands)

    return call


def place_kernel(slot, slot_ref, own_ref, source_ref, before, placed_ref, sem):
    row = row_for(slot, 1, slot_ref, own_ref)
    copy = pltpu.make_async_copy(source_ref, placed_ref.at[row], sem)
    copy.start()
    copy.wait()


def place(scalars, slot, source, placed):
    return pl.pallas_call(
        functools.partial(place_kernel, slot),
        out_shape=jax.ShapeDtypeStruct(placed.shape, placed.dtype),
        in_specs=[pl.BlockSpec(memory_space=pltpu.SMEM)] * 2
        + [pl.BlockSpec(memory_space=pltpu.VMEM), pl.BlockSpec(memory_space=pltpu.HBM)],
        out_specs=pl.BlockSpec(memory_space=pltpu.HBM),
        scratch_shapes=[pltpu.SemaphoreType.DMA],
        input_output_aliases={3: 0},
        cost_estimate=SMALL,
        compiler_params=pltpu.CompilerParams(vmem_limit_bytes=LARGE),
        name="place",
    )(*scalars, source, placed)


def dispatch_kernel(experts, block_ref, routes_ref, gate_ref, tokens_ref, out_ref, share_ref):
    block = block_ref[0]
    routes = routes_ref[...]
    gates = gate_ref[...]
    rows = routes.shape[0]
    down = lax.broadcasted_iota(jnp.int32, (rows, rows), 0)
    across = lax.broadcasted_iota(jnp.int32, (rows, rows), 1)
    same = (down == across).astype(jnp.float32)
    slots = experts * CAP
    slot_row = lax.broadcasted_iota(jnp.int32, (slots, rows), 0)
    slot_column = lax.broadcasted_iota(jnp.int32, (rows, slots), 1)
    placing = jnp.zeros((slots, rows), jnp.float32)
    share = jnp.zeros((rows, slots), jnp.float32)
    for k in range(experts):
        expert = lax.rem(block + k, experts)
        hit = routes == expert
        has = jnp.sum(hit.astype(jnp.float32), axis=1, keepdims=True)
        weight = jnp.sum(jnp.where(hit, gates, 0.0), axis=1, keepdims=True)
        has_row = jnp.sum(has * same, axis=0, keepdims=True)
        before_row = jnp.sum(jnp.where(down < across, has, 0.0), axis=0, keepdims=True)
        before = jnp.sum(jnp.where(across < down, has_row, 0.0), axis=1, keepdims=True)
        for c in range(CAP):
            slot = k * CAP + c
            placing += jnp.where((slot_row == slot) & (before_row == c), has_row, 0.0)
            share += jnp.where((slot_column == slot) & (before == c), weight, 0.0)
    out_ref[...] = jnp.dot(
        placing.astype(jnp.bfloat16), tokens_ref[...], preferred_element_type=jnp.float32
    ).astype(jnp.bfloat16)
    share_ref[...] = share


def dispatch(block, routes, gates, tokens, experts):
    slots = experts * CAP
    return pl.pallas_call(
        functools.partial(dispatch_kernel, experts),
        out_shape=(
            jax.ShapeDtypeStruct((slots, tokens.shape[1]), tokens.dtype),
            jax.ShapeDtypeStruct((tokens.shape[0], slots), jnp.float32),
        ),
        in_specs=[pl.BlockSpec(memory_space=pltpu.SMEM)]
        + [pl.BlockSpec(memory_space=pltpu.VMEM)] * 3,
        out_specs=(pl.BlockSpec(memory_space=pltpu.VMEM),) * 2,
        cost_estimate=SMALL,
        compiler_params=pltpu.CompilerParams(vmem_limit_bytes=8 * 1024 * 1024),
        name="dispatch",
    )(block, routes, gates, tokens)


def moved_rows(pieces, places, rows):
    total = None
    for piece, places_of_piece in zip(pieces, places):
        shape = (rows, piece.shape[0])
        row = lax.broadcasted_iota(jnp.int32, shape, 0)
        column = lax.broadcasted_iota(jnp.int32, shape, 1)
        chosen = jnp.zeros(shape, jnp.float32)
        for source, there in places_of_piece:
            chosen += ((row == there) & (column == source)).astype(jnp.float32)
        part = jnp.dot(
            chosen.astype(jnp.bfloat16), piece[...], preferred_element_type=jnp.float32
        )
        total = part if total is None else total + part
    return total.astype(jnp.bfloat16)


def move_kernel(count, plans, *refs):
    for plan, out_ref in zip(plans, refs[count:]):
        used = [i for i in range(count) if plan[i]]
        out_ref[...] = moved_rows(
            [refs[i] for i in used], [plan[i] for i in used], out_ref.shape[0]
        )


def move_rows(arrays, plans, rows, name):
    width = arrays[0].shape[1]
    return pl.pallas_call(
        functools.partial(move_kernel, len(arrays), plans),
        out_shape=tuple(jax.ShapeDtypeStruct((rows, width), jnp.bfloat16) for _ in plans),
        in_specs=[pl.BlockSpec(memory_space=pltpu.VMEM)] * len(arrays),
        out_specs=tuple(pl.BlockSpec(memory_space=pltpu.VMEM) for _ in plans),
        cost_estimate=SMALL,
        compiler_params=pltpu.CompilerParams(vmem_limit_bytes=8 * 1024 * 1024),
        name=name,
    )(*arrays)


def experts_kernel(mine_ref, theirs_ref, gate_hbm, up_hbm, down_hbm, keep_ref, send_ref, *scratch):
    gate_ref, up_ref, down_ref, sems = scratch
    copies = [
        pltpu.make_async_copy(source.at[0], there, sems.at[i])
        for i, (source, there) in enumerate(
            ((gate_hbm, gate_ref), (up_hbm, up_ref), (down_hbm, down_ref))
        )
    ]
    for copy in copies:
        copy.start()
    rows = jnp.concatenate([mine_ref[...], theirs_ref[...]], axis=0)
    copies[0].wait()
    gate = jnp.dot(rows, gate_ref[...], preferred_element_type=jnp.float32)
    copies[1].wait()
    lifted = jnp.dot(rows, up_ref[...], preferred_element_type=jnp.float32)
    hidden = (gate / (1.0 + jnp.exp(-gate)) * lifted).astype(jnp.bfloat16)
    copies[2].wait()
    parts = jnp.dot(hidden, down_ref[...], preferred_element_type=jnp.float32)
    count = mine_ref.shape[0]
    keep_ref[...] = parts[:count]
    send_ref[...] = parts[count:].astype(jnp.bfloat16)


def run_experts(mine, theirs, w_gate, w_up, w_down):
    return pl.pallas_call(
        experts_kernel,
        out_shape=(
            jax.ShapeDtypeStruct(mine.shape, jnp.float32),
            jax.ShapeDtypeStruct(mine.shape, jnp.bfloat16),
        ),
        in_specs=[pl.BlockSpec(memory_space=pltpu.VMEM)] * 2
        + [pl.BlockSpec(memory_space=pltpu.HBM)] * 3,
        out_specs=(pl.BlockSpec(memory_space=pltpu.VMEM),) * 2,
        scratch_shapes=[
            pltpu.VMEM(w_gate.shape[1:], w_gate.dtype),
            pltpu.VMEM(w_up.shape[1:], w_up.dtype),
            pltpu.VMEM(w_down.shape[1:], w_down.dtype),
            pltpu.SemaphoreType.DMA((3,)),
        ],
        cost_estimate=SMALL,
        compiler_params=pltpu.CompilerParams(vmem_limit_bytes=16 * 1024 * 1024),
        name="experts",
    )(mine, theirs, w_gate, w_up, w_down)


def halve_kernel(sum_ref, arrived_ref, keep_ref, send_ref):
    count = keep_ref.shape[0]
    total = sum_ref[...] + arrived_ref[...].astype(jnp.float32)
    keep_ref[...] = total[:count]
    send_ref[...] = total[count:].astype(jnp.bfloat16)


def halve(kept, arrived):
    shape = (kept.shape[0] // 2, kept.shape[1])
    return pl.pallas_call(
        halve_kernel,
        out_shape=(
            jax.ShapeDtypeStruct(shape, jnp.float32),
            jax.ShapeDtypeStruct(shape, jnp.bfloat16),
        ),
        cost_estimate=SMALL,
        compiler_params=pltpu.CompilerParams(vmem_limit_bytes=8 * 1024 * 1024),
        name="halve",
    )(kept, arrived)


def on_device(
    latent_cache,
    rope_cache,
    q_latent,
    q_rope,
    new_latent,
    new_rope,
    branch_slot,
    moe_input,
    routes,
    route_gate,
    w_gate,
    w_up,
    w_down,
):
    tok_rows, step_count, head_count, width = q_latent.shape
    rope_width = new_rope.shape[-1]
    line = tok_rows // 2
    q_rows = step_count * head_count
    half = latent_cache.shape[1]
    rope_rows = rope_cache.shape[1]
    branch = lax.axis_index("branch")
    own = branch % tok_rows
    low = own % 2
    high = own // 2
    middle = jnp.logical_and(high > 0, high < line - 1)

    outer = [(i, i ^ 1) for i in range(line)]
    inner = [(i, i + 1) for i in range(1, line - 1, 2)]
    inner = inner + [(j, i) for i, j in inner]
    outward = [(i, i ^ 1) for i in range(1, line - 1)]
    own_cache = pack_cache(latent_cache[0], rope_cache[0])
    cache_a = line_hop(own_cache, tok_rows, outer)
    first_b = line_hop(own_cache, tok_rows, inner)

    q_lat = q_latent.reshape(tok_rows, q_rows, width)
    rope_raw = q_rope.reshape(tok_rows, q_rows * rope_width // width, width)
    fresh = jnp.concatenate(
        [
            jnp.pad(new_latent, ((0, 0), (0, PAD - step_count), (0, 0))),
            jnp.pad(new_rope, ((0, 0), (0, PAD - step_count), (0, width - rope_width))),
        ],
        axis=1,
    )
    scalars = (branch_slot, own[None])
    stay = (q_lat, rope_raw, fresh)

    leave = pack_leaving(branch_slot, after(own[None], own_cache), *stay)
    guest = swapped(leave, "branch", 0)
    attend = build_attend(head_count, step_count, width, half, rope_rows, 32, half // 2)
    model_width = moe_input.shape[-1]
    tok_total = tok_rows * step_count
    device = branch * lax.axis_size("expert") + lax.axis_index("expert")
    experts = lax.axis_size("branch") * lax.axis_size("expert") // SHARDS
    cores = lax.axis_size("expert")
    shard_branches = SHARDS // cores
    block = device // SHARDS
    outgoing, share = dispatch(
        after(block[None], leave),
        routes.reshape(tok_total, -1),
        route_gate.reshape(tok_total, -1),
        moe_input.reshape(tok_total, model_width),
        experts,
    )

    around = shard_branches // 2

    def along(x, shift, flip):
        count = lax.axis_size("branch")
        there = [
            ((i // shard_branches + shift) % experts) * shard_branches
            + ((i % shard_branches) ^ (flip * 2))
            for i in range(count)
        ]
        return lax.ppermute(x, "branch", list(enumerate(there)))

    beside = swapped(outgoing, "branch", 0)
    cache_a, first_b, outgoing = lax.optimization_barrier((cache_a, first_b, outgoing))
    second_b = line_hop(first_b, tok_rows, outward)
    first_c = line_hop(cache_a, tok_rows, inner)
    pair = tuple(
        tuple(tuple((k * CAP + c, i * CAP + c) for c in range(CAP)) for i in range(2))
        for k in range(experts)
    )
    ways = [(k, m) for k in range(experts) for m in range(around)]

    def attend_slot(slot, cache, kinds, waiting, placed):
        keeps = "keep" in kinds
        results = attend(
            scalars,
            kinds,
            slot,
            guest,
            stay,
            cache,
            waiting if keeps else [],
            placed if keeps else None,
        )
        given = results[0] if "give" in kinds else None
        return given, (results[-1] if keeps else placed)

    def both_halves(cache):
        return cache, swapped(cache, "expert", 0)

    guest = after(guest, cache_a, first_b)
    both = ("give", "keep")
    given_0, placed = attend_slot(0, both_halves(own_cache), both, [], None)
    back_0 = swapped(given_0, "branch", 0)
    by_expert = move_rows((outgoing, after(beside, given_0)), pair, 2 * CAP, "pair_rows")
    pieces = [by_expert[k] if (k, m) == (0, 0) else along(by_expert[k], k, m) for k, m in ways]
    given_1, placed = attend_slot(1, both_halves(cache_a), both, [], placed)
    back_1 = swapped(given_1, "branch", 0)
    pieces = [after(piece, given_1) for piece in pieces]


    second_b, given_1, *pieces = lax.optimization_barrier((second_b, given_1, *pieces))
    first_c, second_b = lax.optimization_barrier((first_c, second_b))
    second_c = line_hop(first_c, tok_rows, outward)
    count = len(ways) * CAP
    stacked = tuple(
        tuple((i * CAP + c, i * count + w * CAP + c) for i in range(2) for c in range(CAP))
        for w in range(len(ways))
    )
    (rows,) = move_rows(tuple(pieces), (stacked,), 2 * count, "stack_rows")
    cache_b = jnp.where(middle, first_b, second_b)
    theirs = swapped(rows, "expert", 0)
    rows, theirs, back_0, back_1 = lax.optimization_barrier((rows, theirs, back_0, back_1))
    kept, sent = run_experts(rows, theirs, w_gate, w_up, w_down)
    kept, sent = halve(kept, swapped(sent, "expert", 0))
    given_2, placed = attend_slot(2, both_halves(cache_b), both, [], placed)
    back_2 = swapped(given_2, "branch", 0)

    second_c, back_2, kept, sent = lax.optimization_barrier((second_c, back_2, kept, sent))
    cache_c = both_halves(jnp.where(middle, first_c, second_c))
    parts = kept + swapped(sent, "branch", 0).astype(jnp.float32)
    homeward = [
        parts[w * CAP : (w + 1) * CAP].astype(jnp.float32 if way == (0, 0) else jnp.bfloat16)
        for w, way in enumerate(ways)
    ]
    guest, *homeward = lax.optimization_barrier((guest, *homeward))
    given_3, _ = attend_slot(3, cache_c, ("give",), [], None)
    homeward = [after(x, given_3) for x in homeward]
    back_3 = swapped(given_3, "branch", 0)
    _, placed = attend_slot(3, cache_c, ("keep",), [(0, back_0), (1, back_1), (2, back_2)], placed)
    placed = place(scalars, 3, back_3, placed)
    attended = placed.reshape(tok_rows, step_count, head_count, width)

    sums = [0.0] * experts
    for (k, m), piece in zip(ways, homeward):
        if (k, m) != (0, 0):
            piece = along(piece, -k, m).astype(jnp.float32)
        sums[k] = sums[k] + piece
    sums = jnp.concatenate(sums, axis=0)
    combined = jnp.sum(share[:, :, None] * sums[None, :, :], axis=1)
    moe_out = combined.astype(jnp.bfloat16).reshape(tok_rows, step_count, model_width)
    return (attended, moe_out)


def solution(mesh):
    return jax.shard_map(
        on_device,
        mesh=mesh,
        in_specs=(
            P(("group", "branch"), "expert", None),
            P(("group", "branch"), "expert", None),
            P(("group", "branch", "expert"), None, None, None),
            P(("group", "branch", "expert"), None, None),
            P(("group", "branch", "expert"), None, None),
            P(("group", "branch", "expert"), None, None),
            P(("group", "branch", "expert")),
            P(("group", "branch", "expert"), None, None),
            P(("group", "branch", "expert"), None, None),
            P(("group", "branch", "expert"), None, None),
            P(("branch", "expert"), None, None),
            P(("branch", "expert"), None, None),
            P(("branch", "expert"), None, None),
        ),
        out_specs=(
            P(("group", "branch", "expert"), None, None, None),
            P(("group", "branch", "expert"), None, None),
        ),
        check_vma=False,
    )
```

```python
import functools

import jax
import jax.numpy as jnp
from jax import lax
from jax.experimental import pallas as pl
from jax.experimental.pallas import tpu as pltpu
from jax.sharding import PartitionSpec as P

SHARDS = 8
CAP = 2
LANES = 128
PAD = 16

SMALL = pl.CostEstimate(flops=0, bytes_accessed=1024, transcendentals=0)

LARGE = 62 * 1024 * 1024

softmax_scale = 192.0 ** (-0.5)
log2e = 1.4426950408889634


def after(x, *earlier):
    return lax.optimization_barrier((x, *earlier))[0]


def swapped(x, axis, bit):
    return lax.ppermute(x, axis, [(i, i ^ 1 << bit) for i in range(lax.axis_size(axis))])


def line_hop(x, block, moves):
    pairs = []
    for base in range(0, lax.axis_size("branch"), block):
        for low in range(2):
            pairs += [(base + 2 * i + low, base + 2 * j + low) for i, j in moves]
    return lax.ppermute(x, "branch", pairs)


def pack_cache_kernel(lat_ref, rope_ref, out_ref, sems):
    rows = lat_ref.shape[0]
    copies = [
        pltpu.make_async_copy(lat_ref, out_ref.at[pl.ds(0, rows)], sems.at[0]),
        pltpu.make_async_copy(rope_ref, out_ref.at[pl.ds(rows, rope_ref.shape[0])], sems.at[1]),
    ]
    for copy in copies:
        copy.start()
    for copy in copies:
        copy.wait()


def pack_cache(lat, rope):
    return pl.pallas_call(
        pack_cache_kernel,
        out_shape=jax.ShapeDtypeStruct((lat.shape[0] + rope.shape[0], lat.shape[1]), lat.dtype),
        in_specs=[pl.BlockSpec(memory_space=pltpu.HBM)] * 2,
        out_specs=pl.BlockSpec(memory_space=pltpu.VMEM),
        scratch_shapes=[pltpu.SemaphoreType.DMA((2,))],
        cost_estimate=SMALL,
        compiler_params=pltpu.CompilerParams(vmem_limit_bytes=LARGE),
        name="pack_cache",
    )(lat, rope)


def row_for(slot, parity, slot_ref, own_ref):
    count = slot_ref.shape[0]
    line = count // 2
    own = own_ref[0]
    high = lax.div(own, 2)
    low = lax.rem(own, 2)
    mine = high
    pair = high + 1 - 2 * lax.rem(high, 2)
    first_half = high < line // 2
    nearer = jnp.where(first_half, line // 2, line // 2 - 1)
    farther = jnp.where(first_half, line - 1, 0)
    position = mine
    for number, place_there in ((1, pair), (2, nearer), (3, farther)):
        position = jnp.where(slot == number, place_there, position)
    wanted = 2 * position + (low if parity == 0 else 1 - low)
    row = jnp.int32(0)
    for r in range(1, count):
        row = row + jnp.where(slot_ref[r] == wanted, r, 0)
    return row


def pack_tokens_kernel(parity, slot_ref, own_ref, q_ref, rope_ref, new_ref, out_ref, sems):
    copies = []
    for slot in range(out_ref.shape[0]):
        row = row_for(slot, parity, slot_ref, own_ref)
        start = 0
        for part, source in enumerate((q_ref, rope_ref, new_ref)):
            count = source.shape[1]
            copy = pltpu.make_async_copy(
                source.at[row], out_ref.at[slot, pl.ds(start, count)], sems.at[slot, part]
            )
            copy.start()
            copies.append(copy)
            start += count
    for copy in copies:
        copy.wait()


def pack_tokens(parity, branch_slot, own, q_lat, q_rope, new):
    slots = branch_slot.shape[0] // 2
    sources = (q_lat, q_rope, new)
    rows = sum(x.shape[1] for x in sources)
    return pl.pallas_call(
        functools.partial(pack_tokens_kernel, parity),
        out_shape=jax.ShapeDtypeStruct((slots, rows, q_lat.shape[2]), q_lat.dtype),
        in_specs=[pl.BlockSpec(memory_space=pltpu.SMEM)] * 2
        + [pl.BlockSpec(memory_space=pl.ANY)] * 3,
        out_specs=pl.BlockSpec(memory_space=pltpu.VMEM),
        scratch_shapes=[pltpu.SemaphoreType.DMA((slots, 3))],
        cost_estimate=SMALL,
        compiler_params=pltpu.CompilerParams(vmem_limit_bytes=4 * 1024 * 1024),
        name="pack_tokens",
    )(branch_slot, own, *sources)


def spread_matrix(raw_rows, width):
    per_row = width // (LANES // 2)
    blocks = width // LANES
    shape = (raw_rows * per_row, raw_rows * blocks)
    row = lax.broadcasted_iota(jnp.int32, shape, 0)
    column = lax.broadcasted_iota(jnp.int32, shape, 1)
    wanted = ((row % per_row) // 2) * raw_rows + row // per_row
    return (column == wanted).astype(jnp.bfloat16)


def spread(matrix, raw):
    blocks = raw.shape[1] // LANES
    stacked = jnp.concatenate(
        [raw[:, b * LANES : (b + 1) * LANES] for b in range(blocks)], axis=0
    )
    rows = jnp.dot(matrix, stacked, preferred_element_type=jnp.float32)
    row = lax.broadcasted_iota(jnp.int32, rows.shape, 0)
    lane = lax.broadcasted_iota(jnp.int32, rows.shape, 1)
    return jnp.where(row % 2 == lane // (LANES // 2), rows, 0.0)


def build_attend(heads, steps, width, half, rope_rows, raw_group, chunk):
    q_rows = heads * steps
    token_rope = q_rows // 8

    factor = softmax_scale * log2e
    contract = (((1,), (1,)), ((), ()))

    def put_query_rope(rope_queries, number, raw_rope, matrix):
        grown = raw_group * width // (LANES // 2)
        for i, start in enumerate(range(0, token_rope, raw_group)):
            part = spread(matrix, raw_rope[start : start + raw_group, :])
            part = part + pltpu.roll(part, LANES // 2, 1)
            row = number * q_rows + i * grown
            rope_queries[row : row + grown, :] = part.astype(jnp.bfloat16)

    def merge_own(query, rope_query, fresh_all, peak, total, summed):
        fresh = fresh_all[0:PAD, :]
        fresh_rope = fresh_all[PAD : 2 * PAD, 0:LANES]
        own = lax.dot_general(
            query, fresh, contract, preferred_element_type=jnp.float32
        )
        own = own + lax.dot_general(
            rope_query, fresh_rope, contract, preferred_element_type=jnp.float32
        )
        row_step = lax.broadcasted_iota(jnp.int32, (q_rows, 1), 0) // heads
        columns = [jnp.where(row_step >= j, own[:, j : j + 1], -1e30) for j in range(steps)]
        top = peak
        for column in columns:
            top = jnp.maximum(top, column)
        share = jnp.exp2((peak - top) * factor)
        parts = [
            jnp.where(row_step >= j, jnp.exp2((column - top) * factor), 0.0)
            for j, column in enumerate(columns)
        ]
        denominator = total * share
        for part in parts:
            denominator = denominator + part
        inverse = 1.0 / denominator
        fresh32 = fresh.astype(jnp.float32)
        value = summed * (share * inverse)
        for j, part in enumerate(parts):
            value = value + (part * inverse) * fresh32[j : j + 1, :]
        return value.astype(jnp.bfloat16)

    def put_key_rope(rope_keys, first, raw_rope, matrix):
        grown = raw_group * width // (LANES // 2)
        for i, start in enumerate(range(0, rope_rows, raw_group)):
            part = spread(matrix, raw_rope[start : start + raw_group, :])
            row = first + i * grown
            rope_keys[row : row + grown, :] = part.astype(jnp.bfloat16)

    def kernel(slot, has_placed, slot_ref, own_ref, guest, stay, *refs):
        own_half, other_half = refs[:2]
        refs = refs[3:] if has_placed else refs[2:]
        give, placed, rope_keys, query_rope, scores, summed, result, sem = refs
        tokens = (guest.at[slot], stay.at[slot])
        matrix = spread_matrix(raw_group, width)
        middle = q_rows + token_rope
        for number, token in enumerate(tokens):
            put_query_rope(query_rope, number, token.at[pl.ds(q_rows, token_rope)], matrix)
        peak = None
        for i, cache in enumerate((own_half, other_half)):
            put_key_rope(rope_keys, 0, cache.at[pl.ds(half, rope_rows)], matrix)
            for first in range(0, half, chunk):
                highs = []
                for number, token in enumerate(tokens):
                    rows = slice(number * q_rows, (number + 1) * q_rows)
                    part = lax.dot_general(
                        token[0:q_rows, :],
                        cache[first : first + chunk, :],
                        contract,
                        preferred_element_type=jnp.float32,
                    )
                    part = part + lax.dot_general(
                        query_rope[rows, :],
                        rope_keys[first : first + chunk, :],
                        contract,
                        preferred_element_type=jnp.float32,
                    )
                    scores[rows, i * half + first : i * half + first + chunk] = part
                    highs.append(jnp.max(part, axis=1, keepdims=True))
                high = jnp.concatenate(highs, axis=0)
                peak = high if peak is None else jnp.maximum(peak, high)
        scaled = peak * factor
        total = None
        for first in range(0, 2 * half, chunk):
            cache = own_half if first < half else other_half
            weights = jnp.exp2(scores[:, first : first + chunk] * factor - scaled)
            part = jnp.sum(weights, axis=1, keepdims=True)
            value = jnp.dot(
                weights.astype(jnp.bfloat16),
                cache[first % half : first % half + chunk, :],
                preferred_element_type=jnp.float32,
            )
            if first == 0:
                total = part
                summed[...] = value
            else:
                total = total + part
                summed[...] += value
        for number, token in enumerate(tokens):
            rows = slice(number * q_rows, (number + 1) * q_rows)
            value = merge_own(
                token[0:q_rows, :],
                query_rope[rows, :],
                token[middle : middle + 2 * PAD, :],
                peak[rows],
                total[rows],
                summed[rows, :],
            )
            if number == 0:
                give[...] = value
            else:
                result[...] = value
        row = row_for(slot, 0, slot_ref, own_ref)
        copy = pltpu.make_async_copy(result, placed.at[row], sem)
        copy.start()
        copy.wait()

    def call(scalars, slot, guest, stay, caches, placed):
        count = scalars[0].shape[0]
        vmem = pl.BlockSpec(memory_space=pltpu.VMEM)
        anywhere = pl.BlockSpec(memory_space=pl.ANY)
        operands = [*scalars, guest, stay, *caches]
        in_specs = [pl.BlockSpec(memory_space=pltpu.SMEM)] * 2 + [vmem] * 4
        alias = {}
        if placed is not None:
            alias = {len(operands): 1}
            in_specs.append(anywhere)
            operands.append(placed)
        return pl.pallas_call(
            functools.partial(kernel, slot, placed is not None),
            out_shape=(
                jax.ShapeDtypeStruct((q_rows, width), jnp.bfloat16),
                jax.ShapeDtypeStruct((count, q_rows, width), jnp.bfloat16),
            ),
            in_specs=in_specs,
            out_specs=(vmem, anywhere),
            scratch_shapes=[
                pltpu.VMEM((half, LANES), jnp.bfloat16),
                pltpu.VMEM((2 * q_rows, LANES), jnp.bfloat16),
                pltpu.VMEM((2 * q_rows, 2 * half), jnp.float32),
                pltpu.VMEM((2 * q_rows, width), jnp.float32),
                pltpu.VMEM((q_rows, width), jnp.bfloat16),
                pltpu.SemaphoreType.DMA,
            ],
            input_output_aliases=alias,
            cost_estimate=SMALL,
            compiler_params=pltpu.CompilerParams(vmem_limit_bytes=16 * 1024 * 1024),
            name="attend",
        )(*operands)

    return call


def place_kernel(slot_ref, own_ref, *refs):
    sources, (before, placed_ref, sems) = refs[:-3], refs[-3:]
    copies = []
    for slot, source in enumerate(sources):
        row = row_for(slot, 1, slot_ref, own_ref)
        copies.append(pltpu.make_async_copy(source, placed_ref.at[row], sems.at[slot]))
    for copy in copies:
        copy.start()
    for copy in copies:
        copy.wait()


def place(scalars, sources, placed):
    vmem = pl.BlockSpec(memory_space=pltpu.VMEM)
    return pl.pallas_call(
        place_kernel,
        out_shape=jax.ShapeDtypeStruct(placed.shape, placed.dtype),
        in_specs=[pl.BlockSpec(memory_space=pltpu.SMEM)] * 2
        + [vmem] * len(sources)
        + [pl.BlockSpec(memory_space=pl.ANY)],
        out_specs=pl.BlockSpec(memory_space=pl.ANY),
        scratch_shapes=[pltpu.SemaphoreType.DMA((len(sources),))],
        input_output_aliases={2 + len(sources): 0},
        cost_estimate=SMALL,
        compiler_params=pltpu.CompilerParams(vmem_limit_bytes=4 * 1024 * 1024),
        name="place",
    )(*scalars, *sources, placed)


def dispatch_kernel(experts, block_ref, routes_ref, gate_ref, tokens_ref, out_ref, share_ref):
    block = block_ref[0]
    routes = routes_ref[...]
    gates = gate_ref[...]
    rows = routes.shape[0]
    down = lax.broadcasted_iota(jnp.int32, (rows, rows), 0)
    across = lax.broadcasted_iota(jnp.int32, (rows, rows), 1)
    same = (down == across).astype(jnp.float32)
    slots = experts * CAP
    slot_row = lax.broadcasted_iota(jnp.int32, (slots, rows), 0)
    slot_column = lax.broadcasted_iota(jnp.int32, (rows, slots), 1)
    placing = jnp.zeros((slots, rows), jnp.float32)
    share = jnp.zeros((rows, slots), jnp.float32)
    for expert in range(experts):
        hit = routes == expert
        has = jnp.sum(hit.astype(jnp.float32), axis=1, keepdims=True)
        weight = jnp.sum(jnp.where(hit, gates, 0.0), axis=1, keepdims=True)
        has_row = jnp.sum(has * same, axis=0, keepdims=True)
        before_row = jnp.sum(jnp.where(down < across, has, 0.0), axis=0, keepdims=True)
        before = jnp.sum(jnp.where(across < down, has_row, 0.0), axis=1, keepdims=True)
        away = lax.rem(expert + experts - block, experts)
        for c in range(CAP):
            slot = expert * CAP + c
            placing += jnp.where((slot_row == slot) & (before_row == c), has_row, 0.0)
            share += jnp.where((slot_column == away * CAP + c) & (before == c), weight, 0.0)
    out_ref[...] = jnp.dot(
        placing.astype(jnp.bfloat16), tokens_ref[...], preferred_element_type=jnp.float32
    ).astype(jnp.bfloat16)
    share_ref[...] = share


def dispatch(block, routes, gates, tokens, experts):
    slots = experts * CAP
    return pl.pallas_call(
        functools.partial(dispatch_kernel, experts),
        out_shape=(
            jax.ShapeDtypeStruct((slots, tokens.shape[1]), tokens.dtype),
            jax.ShapeDtypeStruct((tokens.shape[0], slots), jnp.float32),
        ),
        in_specs=[pl.BlockSpec(memory_space=pltpu.SMEM)]
        + [pl.BlockSpec(memory_space=pltpu.VMEM)] * 3,
        out_specs=(pl.BlockSpec(memory_space=pltpu.VMEM),) * 2,
        cost_estimate=SMALL,
        compiler_params=pltpu.CompilerParams(vmem_limit_bytes=8 * 1024 * 1024),
        name="dispatch",
    )(block, routes, gates, tokens)


def order_kernel(experts, device_ref, rows_ref, mine_ref, theirs_ref):
    device = device_ref[0]
    total = rows_ref.shape[0]
    count = mine_ref.shape[0]
    cores = total // count
    lines = SHARDS // (2 * cores)
    ways = experts * lines
    block = lax.div(device, SHARDS)
    within = lax.rem(device, SHARDS)
    shape = (count, total)
    row = lax.broadcasted_iota(jnp.int32, shape, 0)
    column = lax.broadcasted_iota(jnp.int32, shape, 1)
    slot = row % CAP
    way = (row // CAP) % ways
    beside = row // (CAP * ways)
    from_block = (block + experts - way // lines) % experts
    flip = (way % lines) * (2 * cores) + beside * cores
    for core, out_ref in enumerate((mine_ref, theirs_ref)):
        source = from_block * SHARDS + jnp.bitwise_xor(within, flip + core)
        chosen = (column == source * CAP + slot).astype(jnp.bfloat16)
        out_ref[...] = jnp.dot(
            chosen, rows_ref[...], preferred_element_type=jnp.float32
        ).astype(jnp.bfloat16)


def order_rows(device, rows, experts, cores):
    shape = jax.ShapeDtypeStruct((rows.shape[0] // cores, rows.shape[1]), rows.dtype)
    return pl.pallas_call(
        functools.partial(order_kernel, experts),
        out_shape=(shape, shape),
        in_specs=[
            pl.BlockSpec(memory_space=pltpu.SMEM),
            pl.BlockSpec(memory_space=pltpu.VMEM),
        ],
        out_specs=(pl.BlockSpec(memory_space=pltpu.VMEM),) * 2,
        cost_estimate=SMALL,
        compiler_params=pltpu.CompilerParams(vmem_limit_bytes=16 * 1024 * 1024),
        name="order_rows",
    )(device, rows)


def experts_kernel(mine_ref, theirs_ref, gate_hbm, up_hbm, down_hbm, keep_ref, send_ref, *scratch):
    gate_ref, up_ref, down_ref, sems = scratch
    copies = [
        pltpu.make_async_copy(source.at[0], there, sems.at[i])
        for i, (source, there) in enumerate(
            ((gate_hbm, gate_ref), (up_hbm, up_ref), (down_hbm, down_ref))
        )
    ]
    for copy in copies:
        copy.start()
    rows = jnp.concatenate([mine_ref[...], theirs_ref[...]], axis=0)
    copies[0].wait()
    gate = jnp.dot(rows, gate_ref[...], preferred_element_type=jnp.float32)
    copies[1].wait()
    lifted = jnp.dot(rows, up_ref[...], preferred_element_type=jnp.float32)
    hidden = (gate / (1.0 + jnp.exp(-gate)) * lifted).astype(jnp.bfloat16)
    copies[2].wait()
    parts = jnp.dot(hidden, down_ref[...], preferred_element_type=jnp.float32)
    count = mine_ref.shape[0]
    keep_ref[...] = parts[:count]
    send_ref[...] = parts[count:].astype(jnp.bfloat16)


def run_experts(mine, theirs, w_gate, w_up, w_down):
    return pl.pallas_call(
        experts_kernel,
        out_shape=(
            jax.ShapeDtypeStruct(mine.shape, jnp.float32),
            jax.ShapeDtypeStruct(mine.shape, jnp.bfloat16),
        ),
        in_specs=[pl.BlockSpec(memory_space=pltpu.VMEM)] * 2
        + [pl.BlockSpec(memory_space=pltpu.HBM)] * 3,
        out_specs=(pl.BlockSpec(memory_space=pltpu.VMEM),) * 2,
        scratch_shapes=[
            pltpu.VMEM(w_gate.shape[1:], w_gate.dtype),
            pltpu.VMEM(w_up.shape[1:], w_up.dtype),
            pltpu.VMEM(w_down.shape[1:], w_down.dtype),
            pltpu.SemaphoreType.DMA((3,)),
        ],
        cost_estimate=SMALL,
        compiler_params=pltpu.CompilerParams(vmem_limit_bytes=16 * 1024 * 1024),
        name="experts",
    )(mine, theirs, w_gate, w_up, w_down)


def halve_kernel(sum_ref, arrived_ref, keep_ref, send_ref):
    count = keep_ref.shape[0]
    total = sum_ref[...] + arrived_ref[...].astype(jnp.float32)
    keep_ref[...] = total[:count]
    send_ref[...] = total[count:].astype(jnp.bfloat16)


def halve(kept, arrived):
    shape = (kept.shape[0] // 2, kept.shape[1])
    return pl.pallas_call(
        halve_kernel,
        out_shape=(
            jax.ShapeDtypeStruct(shape, jnp.float32),
            jax.ShapeDtypeStruct(shape, jnp.bfloat16),
        ),
        cost_estimate=SMALL,
        compiler_params=pltpu.CompilerParams(vmem_limit_bytes=8 * 1024 * 1024),
        name="halve",
    )(kept, arrived)


def on_device(
    latent_cache,
    rope_cache,
    q_latent,
    q_rope,
    new_latent,
    new_rope,
    branch_slot,
    moe_input,
    routes,
    route_gate,
    w_gate,
    w_up,
    w_down,
):
    tok_rows, step_count, head_count, width = q_latent.shape
    rope_width = new_rope.shape[-1]
    line = tok_rows // 2
    q_rows = step_count * head_count
    half = latent_cache.shape[1]
    rope_rows = rope_cache.shape[1]
    branch = lax.axis_index("branch")
    own = branch % tok_rows
    low = own % 2
    high = own // 2
    middle = jnp.logical_and(high > 0, high < line - 1)

    outer = [(i, i ^ 1) for i in range(line)]
    inner = [(i, i + 1) for i in range(1, line - 1, 2)]
    inner = inner + [(j, i) for i, j in inner]
    outward = [(i, i ^ 1) for i in range(1, line - 1)]
    own_cache = pack_cache(latent_cache[0], rope_cache[0])
    cache_a = line_hop(own_cache, tok_rows, outer)
    first_b = line_hop(own_cache, tok_rows, inner)

    q_lat = q_latent.reshape(tok_rows, q_rows, width)
    rope_raw = q_rope.reshape(tok_rows, q_rows * rope_width // width, width)
    fresh = jnp.concatenate(
        [
            jnp.pad(new_latent, ((0, 0), (0, PAD - step_count), (0, 0))),
            jnp.pad(new_rope, ((0, 0), (0, PAD - step_count), (0, width - rope_width))),
        ],
        axis=1,
    )
    scalars = (branch_slot, own[None])
    sources = (q_lat, rope_raw, fresh)
    leave = pack_tokens(1, branch_slot, after(own[None], own_cache), *sources)
    guest = swapped(leave, "branch", 0)
    stay = pack_tokens(0, branch_slot, after(own[None], leave), *sources)
    attend = build_attend(head_count, step_count, width, half, rope_rows, 32, half // 2)
    model_width = moe_input.shape[-1]
    tok_total = tok_rows * step_count
    device = branch * lax.axis_size("expert") + lax.axis_index("expert")
    experts = lax.axis_size("branch") * lax.axis_size("expert") // SHARDS
    cores = lax.axis_size("expert")
    shard_branches = SHARDS // cores
    block = device // SHARDS
    outgoing, share = dispatch(
        after(block[None], leave),
        routes.reshape(tok_total, -1),
        route_gate.reshape(tok_total, -1),
        moe_input.reshape(tok_total, model_width),
        experts,
    )

    around = shard_branches // 2

    def along(x, shift, flip):
        count = lax.axis_size("branch")
        there = [
            ((i // shard_branches + shift) % experts) * shard_branches
            + ((i % shard_branches) ^ (flip * 2))
            for i in range(count)
        ]
        return lax.ppermute(x, "branch", list(enumerate(there)))

    gathered = lax.all_gather(outgoing, ("branch", "expert"), axis=0, tiled=False)
    cache_a, first_b, outgoing = lax.optimization_barrier((cache_a, first_b, outgoing))
    second_b = line_hop(first_b, tok_rows, outward)
    first_c = line_hop(cache_a, tok_rows, inner)
    ways = [(k, m) for k in range(experts) for m in range(around)]

    def both_halves(cache):
        return cache, swapped(cache, "expert", 0)

    guest = after(guest, cache_a, first_b)
    given_0, placed = attend(scalars, 0, guest, stay, both_halves(own_cache), None)
    back_0 = swapped(given_0, "branch", 0)
    gathered = after(gathered, given_0)
    picked = lax.dynamic_slice_in_dim(gathered, block * CAP, CAP, axis=1)
    mine, theirs = order_rows(
        device[None], picked.reshape(-1, model_width), experts, cores
    )
    kept, sent = run_experts(mine, theirs, w_gate, w_up, w_down)
    kept, sent = halve(kept, swapped(sent, "expert", 0))
    given_1, placed = attend(scalars, 1, guest, stay, both_halves(cache_a), placed)
    back_1 = swapped(given_1, "branch", 0)

    second_b, given_1, kept, sent = lax.optimization_barrier((second_b, given_1, kept, sent))
    first_c, second_b = lax.optimization_barrier((first_c, second_b))
    second_c = line_hop(first_c, tok_rows, outward)
    cache_b = jnp.where(middle, first_b, second_b)
    given_2, placed = attend(scalars, 2, guest, stay, both_halves(cache_b), placed)
    back_2 = swapped(given_2, "branch", 0)
    parts = kept + swapped(sent, "branch", 0).astype(jnp.float32)

    second_c, back_0, back_1, back_2, parts = lax.optimization_barrier(
        (second_c, back_0, back_1, back_2, parts)
    )
    cache_c = both_halves(jnp.where(middle, first_c, second_c))
    homeward = [
        parts[w * CAP : (w + 1) * CAP].astype(jnp.float32 if way == (0, 0) else jnp.bfloat16)
        for w, way in enumerate(ways)
    ]
    guest, *homeward = lax.optimization_barrier((guest, *homeward))
    given_3, placed = attend(scalars, 3, guest, stay, cache_c, placed)
    back_3 = swapped(given_3, "branch", 0)
    homeward = [after(x, given_3) for x in homeward]
    placed = place(scalars, (back_0, back_1, back_2, back_3), placed)
    attended = placed.reshape(tok_rows, step_count, head_count, width)

    sums = [0.0] * experts
    for (k, m), piece in zip(ways, homeward):
        if (k, m) != (0, 0):
            piece = along(piece, -k, m).astype(jnp.float32)
        sums[k] = sums[k] + piece
    sums = jnp.concatenate(sums, axis=0)
    combined = jnp.sum(share[:, :, None] * sums[None, :, :], axis=1)
    moe_out = combined.astype(jnp.bfloat16).reshape(tok_rows, step_count, model_width)
    return (attended, moe_out)


def solution(mesh):
    return jax.shard_map(
        on_device,
        mesh=mesh,
        in_specs=(
            P(("group", "branch"), "expert", None),
            P(("group", "branch"), "expert", None),
            P(("group", "branch", "expert"), None, None, None),
            P(("group", "branch", "expert"), None, None),
            P(("group", "branch", "expert"), None, None),
            P(("group", "branch", "expert"), None, None),
            P(("group", "branch", "expert")),
            P(("group", "branch", "expert"), None, None),
            P(("group", "branch", "expert"), None, None),
            P(("group", "branch", "expert"), None, None),
            P(("branch", "expert"), None, None),
            P(("branch", "expert"), None, None),
            P(("branch", "expert"), None, None),
        ),
        out_specs=(
            P(("group", "branch", "expert"), None, None, None),
            P(("group", "branch", "expert"), None, None),
        ),
        check_vma=False,
    )
```

```python
import functools

import jax
import jax.numpy as jnp
from jax import lax
from jax.experimental import pallas as pl
from jax.experimental.pallas import tpu as pltpu
from jax.sharding import PartitionSpec as P

SHARDS = 8
CAP = 2
LANES = 128
PAD = 16

SMALL = pl.CostEstimate(flops=0, bytes_accessed=1024, transcendentals=0)

LARGE = 62 * 1024 * 1024

softmax_scale = 192.0 ** (-0.5)
log2e = 1.4426950408889634


def after(x, *earlier):
    return lax.optimization_barrier((x, *earlier))[0]


def swapped(x, axis, bit):
    return lax.ppermute(x, axis, [(i, i ^ 1 << bit) for i in range(lax.axis_size(axis))])


def line_hop(x, block, moves):
    pairs = []
    for base in range(0, lax.axis_size("branch"), block):
        for low in range(2):
            pairs += [(base + 2 * i + low, base + 2 * j + low) for i, j in moves]
    return lax.ppermute(x, "branch", pairs)


def pack_cache_kernel(lat_ref, rope_ref, out_ref, sems):
    rows = lat_ref.shape[0]
    copies = [
        pltpu.make_async_copy(lat_ref, out_ref.at[pl.ds(0, rows)], sems.at[0]),
        pltpu.make_async_copy(rope_ref, out_ref.at[pl.ds(rows, rope_ref.shape[0])], sems.at[1]),
    ]
    for copy in copies:
        copy.start()
    for copy in copies:
        copy.wait()


def pack_cache(lat, rope):
    return pl.pallas_call(
        pack_cache_kernel,
        out_shape=jax.ShapeDtypeStruct((lat.shape[0] + rope.shape[0], lat.shape[1]), lat.dtype),
        in_specs=[pl.BlockSpec(memory_space=pltpu.HBM)] * 2,
        out_specs=pl.BlockSpec(memory_space=pltpu.VMEM),
        scratch_shapes=[pltpu.SemaphoreType.DMA((2,))],
        cost_estimate=SMALL,
        compiler_params=pltpu.CompilerParams(vmem_limit_bytes=LARGE),
        name="pack_cache",
    )(lat, rope)


def row_for(slot, parity, slot_ref, own_ref):
    count = slot_ref.shape[0]
    line = count // 2
    own = own_ref[0]
    high = lax.div(own, 2)
    low = lax.rem(own, 2)
    mine = high
    pair = high + 1 - 2 * lax.rem(high, 2)
    first_half = high < line // 2
    nearer = jnp.where(first_half, line // 2, line // 2 - 1)
    farther = jnp.where(first_half, line - 1, 0)
    position = mine
    for number, place_there in ((1, pair), (2, nearer), (3, farther)):
        position = jnp.where(slot == number, place_there, position)
    wanted = 2 * position + (low if parity == 0 else 1 - low)
    row = jnp.int32(0)
    for r in range(1, count):
        row = row + jnp.where(slot_ref[r] == wanted, r, 0)
    return row


def pack_tokens_kernel(parity, slot_ref, own_ref, q_ref, rope_ref, new_ref, out_ref, sems):
    copies = []
    for slot in range(out_ref.shape[0]):
        row = row_for(slot, parity, slot_ref, own_ref)
        start = 0
        for part, source in enumerate((q_ref, rope_ref, new_ref)):
            count = source.shape[1]
            copy = pltpu.make_async_copy(
                source.at[row], out_ref.at[slot, pl.ds(start, count)], sems.at[slot, part]
            )
            copy.start()
            copies.append(copy)
            start += count
    for copy in copies:
        copy.wait()


def pack_tokens(parity, branch_slot, own, q_lat, q_rope, new):
    slots = branch_slot.shape[0] // 2
    sources = (q_lat, q_rope, new)
    rows = sum(x.shape[1] for x in sources)
    return pl.pallas_call(
        functools.partial(pack_tokens_kernel, parity),
        out_shape=jax.ShapeDtypeStruct((slots, rows, q_lat.shape[2]), q_lat.dtype),
        in_specs=[pl.BlockSpec(memory_space=pltpu.SMEM)] * 2
        + [pl.BlockSpec(memory_space=pl.ANY)] * 3,
        out_specs=pl.BlockSpec(memory_space=pltpu.VMEM),
        scratch_shapes=[pltpu.SemaphoreType.DMA((slots, 3))],
        cost_estimate=SMALL,
        compiler_params=pltpu.CompilerParams(vmem_limit_bytes=4 * 1024 * 1024),
        name="pack_tokens",
    )(branch_slot, own, *sources)


def spread_matrix(raw_rows, width):
    per_row = width // (LANES // 2)
    blocks = width // LANES
    shape = (raw_rows * per_row, raw_rows * blocks)
    row = lax.broadcasted_iota(jnp.int32, shape, 0)
    column = lax.broadcasted_iota(jnp.int32, shape, 1)
    wanted = ((row % per_row) // 2) * raw_rows + row // per_row
    return (column == wanted).astype(jnp.bfloat16)


def spread(matrix, raw):
    blocks = raw.shape[1] // LANES
    stacked = jnp.concatenate(
        [raw[:, b * LANES : (b + 1) * LANES] for b in range(blocks)], axis=0
    )
    rows = jnp.dot(matrix, stacked, preferred_element_type=jnp.float32)
    row = lax.broadcasted_iota(jnp.int32, rows.shape, 0)
    lane = lax.broadcasted_iota(jnp.int32, rows.shape, 1)
    return jnp.where(row % 2 == lane // (LANES // 2), rows, 0.0)


def build_attend(heads, steps, width, half, rope_rows, raw_group, chunk):
    q_rows = heads * steps
    token_rope = q_rows // 8

    factor = softmax_scale * log2e
    contract = (((1,), (1,)), ((), ()))

    def put_query_rope(rope_queries, number, raw_rope, matrix):
        grown = raw_group * width // (LANES // 2)
        for i, start in enumerate(range(0, token_rope, raw_group)):
            part = spread(matrix, raw_rope[start : start + raw_group, :])
            part = part + pltpu.roll(part, LANES // 2, 1)
            row = number * q_rows + i * grown
            rope_queries[row : row + grown, :] = part.astype(jnp.bfloat16)

    def merge_own(query, rope_query, fresh_all, peak, total, summed):
        fresh = fresh_all[0:PAD, :]
        fresh_rope = fresh_all[PAD : 2 * PAD, 0:LANES]
        own = lax.dot_general(
            query, fresh, contract, preferred_element_type=jnp.float32
        )
        own = own + lax.dot_general(
            rope_query, fresh_rope, contract, preferred_element_type=jnp.float32
        )
        row_step = lax.broadcasted_iota(jnp.int32, (q_rows, 1), 0) // heads
        columns = [jnp.where(row_step >= j, own[:, j : j + 1], -1e30) for j in range(steps)]
        top = peak
        for column in columns:
            top = jnp.maximum(top, column)
        share = jnp.exp2((peak - top) * factor)
        parts = [
            jnp.where(row_step >= j, jnp.exp2((column - top) * factor), 0.0)
            for j, column in enumerate(columns)
        ]
        denominator = total * share
        for part in parts:
            denominator = denominator + part
        inverse = 1.0 / denominator
        fresh32 = fresh.astype(jnp.float32)
        value = summed * (share * inverse)
        for j, part in enumerate(parts):
            value = value + (part * inverse) * fresh32[j : j + 1, :]
        return value.astype(jnp.bfloat16)

    def put_key_rope(rope_keys, first, raw_rope, matrix):
        grown = raw_group * width // (LANES // 2)
        for i, start in enumerate(range(0, rope_rows, raw_group)):
            part = spread(matrix, raw_rope[start : start + raw_group, :])
            row = first + i * grown
            rope_keys[row : row + grown, :] = part.astype(jnp.bfloat16)

    def kernel(slot, has_placed, slot_ref, own_ref, guest, stay, *refs):
        own_half, other_half = refs[:2]
        refs = refs[3:] if has_placed else refs[2:]
        give, placed, rope_keys, query_rope, scores, summed, result, sem = refs
        tokens = (guest.at[slot], stay.at[slot])
        matrix = spread_matrix(raw_group, width)
        middle = q_rows + token_rope
        for number, token in enumerate(tokens):
            put_query_rope(query_rope, number, token.at[pl.ds(q_rows, token_rope)], matrix)
        peak = None
        for i, cache in enumerate((own_half, other_half)):
            put_key_rope(rope_keys, 0, cache.at[pl.ds(half, rope_rows)], matrix)
            for first in range(0, half, chunk):
                highs = []
                for number, token in enumerate(tokens):
                    rows = slice(number * q_rows, (number + 1) * q_rows)
                    part = lax.dot_general(
                        token[0:q_rows, :],
                        cache[first : first + chunk, :],
                        contract,
                        preferred_element_type=jnp.float32,
                    )
                    part = part + lax.dot_general(
                        query_rope[rows, :],
                        rope_keys[first : first + chunk, :],
                        contract,
                        preferred_element_type=jnp.float32,
                    )
                    scores[rows, i * half + first : i * half + first + chunk] = part
                    highs.append(jnp.max(part, axis=1, keepdims=True))
                high = jnp.concatenate(highs, axis=0)
                peak = high if peak is None else jnp.maximum(peak, high)
        scaled = peak * factor
        total = None
        for first in range(0, 2 * half, chunk):
            cache = own_half if first < half else other_half
            weights = jnp.exp2(scores[:, first : first + chunk] * factor - scaled)
            part = jnp.sum(weights, axis=1, keepdims=True)
            value = jnp.dot(
                weights.astype(jnp.bfloat16),
                cache[first % half : first % half + chunk, :],
                preferred_element_type=jnp.float32,
            )
            if first == 0:
                total = part
                summed[...] = value
            else:
                total = total + part
                summed[...] += value
        for number, token in enumerate(tokens):
            rows = slice(number * q_rows, (number + 1) * q_rows)
            value = merge_own(
                token[0:q_rows, :],
                query_rope[rows, :],
                token[middle : middle + 2 * PAD, :],
                peak[rows],
                total[rows],
                summed[rows, :],
            )
            if number == 0:
                give[...] = value
            else:
                result[...] = value
        row = row_for(slot, 0, slot_ref, own_ref)
        copy = pltpu.make_async_copy(result, placed.at[row], sem)
        copy.start()
        copy.wait()

    def call(scalars, slot, guest, stay, caches, placed):
        count = scalars[0].shape[0]
        vmem = pl.BlockSpec(memory_space=pltpu.VMEM)
        anywhere = pl.BlockSpec(memory_space=pl.ANY)
        operands = [*scalars, guest, stay, *caches]
        in_specs = [pl.BlockSpec(memory_space=pltpu.SMEM)] * 2 + [vmem] * 4
        alias = {}
        if placed is not None:
            alias = {len(operands): 1}
            in_specs.append(anywhere)
            operands.append(placed)
        return pl.pallas_call(
            functools.partial(kernel, slot, placed is not None),
            out_shape=(
                jax.ShapeDtypeStruct((q_rows, width), jnp.bfloat16),
                jax.ShapeDtypeStruct((count, q_rows, width), jnp.bfloat16),
            ),
            in_specs=in_specs,
            out_specs=(vmem, anywhere),
            scratch_shapes=[
                pltpu.VMEM((half, LANES), jnp.bfloat16),
                pltpu.VMEM((2 * q_rows, LANES), jnp.bfloat16),
                pltpu.VMEM((2 * q_rows, 2 * half), jnp.float32),
                pltpu.VMEM((2 * q_rows, width), jnp.float32),
                pltpu.VMEM((q_rows, width), jnp.bfloat16),
                pltpu.SemaphoreType.DMA,
            ],
            input_output_aliases=alias,
            cost_estimate=SMALL,
            compiler_params=pltpu.CompilerParams(vmem_limit_bytes=16 * 1024 * 1024),
            name="attend",
        )(*operands)

    return call


def place_kernel(slot_ref, own_ref, *refs):
    sources, (before, placed_ref, sems) = refs[:-3], refs[-3:]
    copies = []
    for slot, source in enumerate(sources):
        row = row_for(slot, 1, slot_ref, own_ref)
        copies.append(pltpu.make_async_copy(source, placed_ref.at[row], sems.at[slot]))
    for copy in copies:
        copy.start()
    for copy in copies:
        copy.wait()


def place(scalars, sources, placed):
    vmem = pl.BlockSpec(memory_space=pltpu.VMEM)
    return pl.pallas_call(
        place_kernel,
        out_shape=jax.ShapeDtypeStruct(placed.shape, placed.dtype),
        in_specs=[pl.BlockSpec(memory_space=pltpu.SMEM)] * 2
        + [vmem] * len(sources)
        + [pl.BlockSpec(memory_space=pl.ANY)],
        out_specs=pl.BlockSpec(memory_space=pl.ANY),
        scratch_shapes=[pltpu.SemaphoreType.DMA((len(sources),))],
        input_output_aliases={2 + len(sources): 0},
        cost_estimate=SMALL,
        compiler_params=pltpu.CompilerParams(vmem_limit_bytes=4 * 1024 * 1024),
        name="place",
    )(*scalars, *sources, placed)


def dispatch_kernel(experts, block_ref, routes_ref, gate_ref, tokens_ref, *out_refs):
    block = block_ref[0]
    routes = routes_ref[...]
    gates = gate_ref[...]
    rows = routes.shape[0]
    down = lax.broadcasted_iota(jnp.int32, (rows, rows), 0)
    across = lax.broadcasted_iota(jnp.int32, (rows, rows), 1)
    same = (down == across).astype(jnp.float32)
    slots = experts * CAP
    slot_row = lax.broadcasted_iota(jnp.int32, (slots, rows), 0)
    slot_column = lax.broadcasted_iota(jnp.int32, (rows, slots), 1)
    placing = jnp.zeros((slots, rows), jnp.float32)
    share = jnp.zeros((rows, slots), jnp.float32)
    for k in range(experts):
        expert = lax.rem(block + k, experts)
        hit = routes == expert
        has = jnp.sum(hit.astype(jnp.float32), axis=1, keepdims=True)
        weight = jnp.sum(jnp.where(hit, gates, 0.0), axis=1, keepdims=True)
        has_row = jnp.sum(has * same, axis=0, keepdims=True)
        before_row = jnp.sum(jnp.where(down < across, has, 0.0), axis=0, keepdims=True)
        before = jnp.sum(jnp.where(across < down, has_row, 0.0), axis=1, keepdims=True)
        for c in range(CAP):
            slot = k * CAP + c
            placing += jnp.where((slot_row == slot) & (before_row == c), has_row, 0.0)
            share += jnp.where((slot_column == slot) & (before == c), weight, 0.0)
    for k in range(experts):
        out_refs[k][...] = jnp.dot(
            placing[k * CAP : (k + 1) * CAP].astype(jnp.bfloat16),
            tokens_ref[...],
            preferred_element_type=jnp.float32,
        ).astype(jnp.bfloat16)
    out_refs[experts][...] = share


def dispatch(block, routes, gates, tokens, experts):
    slots = experts * CAP
    return pl.pallas_call(
        functools.partial(dispatch_kernel, experts),
        out_shape=(
            *(jax.ShapeDtypeStruct((CAP, tokens.shape[1]), tokens.dtype) for _ in range(experts)),
            jax.ShapeDtypeStruct((tokens.shape[0], slots), jnp.float32),
        ),
        in_specs=[pl.BlockSpec(memory_space=pltpu.SMEM)]
        + [pl.BlockSpec(memory_space=pltpu.VMEM)] * 3,
        out_specs=(pl.BlockSpec(memory_space=pltpu.VMEM),) * (experts + 1),
        cost_estimate=SMALL,
        compiler_params=pltpu.CompilerParams(vmem_limit_bytes=8 * 1024 * 1024),
        name="dispatch",
    )(block, routes, gates, tokens)


def moved_rows(pieces, places, rows):
    total = None
    for piece, places_of_piece in zip(pieces, places):
        shape = (rows, piece.shape[0])
        row = lax.broadcasted_iota(jnp.int32, shape, 0)
        column = lax.broadcasted_iota(jnp.int32, shape, 1)
        chosen = jnp.zeros(shape, jnp.float32)
        for source, there in places_of_piece:
            chosen += ((row == there) & (column == source)).astype(jnp.float32)
        part = jnp.dot(
            chosen.astype(jnp.bfloat16), piece[...], preferred_element_type=jnp.float32
        )
        total = part if total is None else total + part
    return total.astype(jnp.bfloat16)


def stack_kernel(*refs):
    arrays, out_ref = refs[:-1], refs[-1]
    places, start = [], 0
    for array in arrays:
        places.append([(r, start + r) for r in range(array.shape[0])])
        start += array.shape[0]
    out_ref[...] = moved_rows(arrays, places, start)


def stack_rows(*arrays):
    rows = sum(array.shape[0] for array in arrays)
    return pl.pallas_call(
        stack_kernel,
        out_shape=jax.ShapeDtypeStruct((rows, arrays[0].shape[1]), arrays[0].dtype),
        in_specs=[pl.BlockSpec(memory_space=pltpu.VMEM)] * len(arrays),
        out_specs=pl.BlockSpec(memory_space=pltpu.VMEM),
        cost_estimate=SMALL,
        compiler_params=pltpu.CompilerParams(vmem_limit_bytes=8 * 1024 * 1024),
        name="stack_rows",
    )(*arrays)


def experts_kernel(mine_ref, theirs_ref, gate_hbm, up_hbm, down_hbm, keep_ref, send_ref, *scratch):
    gate_ref, up_ref, down_ref, sems = scratch
    copies = [
        pltpu.make_async_copy(source.at[0], there, sems.at[i])
        for i, (source, there) in enumerate(
            ((gate_hbm, gate_ref), (up_hbm, up_ref), (down_hbm, down_ref))
        )
    ]
    for copy in copies:
        copy.start()
    rows = jnp.concatenate([mine_ref[...], theirs_ref[...]], axis=0)
    copies[0].wait()
    gate = jnp.dot(rows, gate_ref[...], preferred_element_type=jnp.float32)
    copies[1].wait()
    lifted = jnp.dot(rows, up_ref[...], preferred_element_type=jnp.float32)
    hidden = (gate / (1.0 + jnp.exp(-gate)) * lifted).astype(jnp.bfloat16)
    copies[2].wait()
    parts = jnp.dot(hidden, down_ref[...], preferred_element_type=jnp.float32)
    count = mine_ref.shape[0]
    keep_ref[...] = parts[:count]
    send_ref[...] = parts[count:].astype(jnp.bfloat16)


def run_experts(mine, theirs, w_gate, w_up, w_down):
    return pl.pallas_call(
        experts_kernel,
        out_shape=(
            jax.ShapeDtypeStruct(mine.shape, jnp.float32),
            jax.ShapeDtypeStruct(mine.shape, jnp.bfloat16),
        ),
        in_specs=[pl.BlockSpec(memory_space=pltpu.VMEM)] * 2
        + [pl.BlockSpec(memory_space=pltpu.HBM)] * 3,
        out_specs=(pl.BlockSpec(memory_space=pltpu.VMEM),) * 2,
        scratch_shapes=[
            pltpu.VMEM(w_gate.shape[1:], w_gate.dtype),
            pltpu.VMEM(w_up.shape[1:], w_up.dtype),
            pltpu.VMEM(w_down.shape[1:], w_down.dtype),
            pltpu.SemaphoreType.DMA((3,)),
        ],
        cost_estimate=SMALL,
        compiler_params=pltpu.CompilerParams(vmem_limit_bytes=16 * 1024 * 1024),
        name="experts",
    )(mine, theirs, w_gate, w_up, w_down)


def halve_kernel(sum_ref, arrived_ref, keep_ref, send_ref):
    count = keep_ref.shape[0]
    total = sum_ref[...] + arrived_ref[...].astype(jnp.float32)
    keep_ref[...] = total[:count]
    send_ref[...] = total[count:].astype(jnp.bfloat16)


def halve(kept, arrived):
    shape = (kept.shape[0] // 2, kept.shape[1])
    return pl.pallas_call(
        halve_kernel,
        out_shape=(
            jax.ShapeDtypeStruct(shape, jnp.float32),
            jax.ShapeDtypeStruct(shape, jnp.bfloat16),
        ),
        cost_estimate=SMALL,
        compiler_params=pltpu.CompilerParams(vmem_limit_bytes=8 * 1024 * 1024),
        name="halve",
    )(kept, arrived)


def on_device(
    latent_cache,
    rope_cache,
    q_latent,
    q_rope,
    new_latent,
    new_rope,
    branch_slot,
    moe_input,
    routes,
    route_gate,
    w_gate,
    w_up,
    w_down,
):
    tok_rows, step_count, head_count, width = q_latent.shape
    rope_width = new_rope.shape[-1]
    line = tok_rows // 2
    q_rows = step_count * head_count
    half = latent_cache.shape[1]
    rope_rows = rope_cache.shape[1]
    branch = lax.axis_index("branch")
    own = branch % tok_rows
    low = own % 2
    high = own // 2
    middle = jnp.logical_and(high > 0, high < line - 1)

    outer = [(i, i ^ 1) for i in range(line)]
    inner = [(i, i + 1) for i in range(1, line - 1, 2)]
    inner = inner + [(j, i) for i, j in inner]
    outward = [(i, i ^ 1) for i in range(1, line - 1)]
    own_cache = pack_cache(latent_cache[0], rope_cache[0])
    cache_a = line_hop(own_cache, tok_rows, outer)
    first_b = line_hop(own_cache, tok_rows, inner)

    q_lat = q_latent.reshape(tok_rows, q_rows, width)
    rope_raw = q_rope.reshape(tok_rows, q_rows * rope_width // width, width)
    fresh = jnp.concatenate(
        [
            jnp.pad(new_latent, ((0, 0), (0, PAD - step_count), (0, 0))),
            jnp.pad(new_rope, ((0, 0), (0, PAD - step_count), (0, width - rope_width))),
        ],
        axis=1,
    )
    scalars = (branch_slot, own[None])
    sources = (q_lat, rope_raw, fresh)
    leave = pack_tokens(1, branch_slot, after(own[None], own_cache), *sources)
    guest = swapped(leave, "branch", 0)
    stay = pack_tokens(0, branch_slot, after(own[None], leave), *sources)
    attend = build_attend(head_count, step_count, width, half, rope_rows, 32, half // 2)
    model_width = moe_input.shape[-1]
    tok_total = tok_rows * step_count
    device = branch * lax.axis_size("expert") + lax.axis_index("expert")
    experts = lax.axis_size("branch") * lax.axis_size("expert") // SHARDS
    cores = lax.axis_size("expert")
    shard_branches = SHARDS // cores
    block = device // SHARDS
    *outgoing, share = dispatch(
        after(block[None], leave),
        routes.reshape(tok_total, -1),
        route_gate.reshape(tok_total, -1),
        moe_input.reshape(tok_total, model_width),
        experts,
    )

    around = shard_branches // 2

    def along(x, shift, flip):
        count = lax.axis_size("branch")
        there = [
            ((i // shard_branches + shift) % experts) * shard_branches
            + ((i % shard_branches) ^ (flip * 2))
            for i in range(count)
        ]
        return lax.ppermute(x, "branch", list(enumerate(there)))

    ways = [(k, m) for m in range(around) for k in range(experts)]
    pieces = outgoing[:1] + [along(outgoing[k], k, 0) for k in range(1, experts)]
    cache_a, first_b, *pieces = lax.optimization_barrier((cache_a, first_b, *pieces))
    second_b = line_hop(first_b, tok_rows, outward)
    first_c = line_hop(cache_a, tok_rows, inner)

    def both_halves(cache):
        return cache, swapped(cache, "expert", 0)

    guest = after(guest, cache_a, first_b)
    rows = stack_rows(*pieces)
    rows = stack_rows(rows, *(along(rows, 0, m) for m in range(1, around)))
    given_0, placed = attend(scalars, 0, guest, stay, both_halves(own_cache), None)
    back_0 = swapped(given_0, "branch", 0)
    given_1, placed = attend(scalars, 1, guest, stay, both_halves(cache_a), placed)
    back_1 = swapped(given_1, "branch", 0)
    rows = after(rows, given_0)
    rows = stack_rows(rows, swapped(rows, "branch", 0))

    second_b, given_1, rows = lax.optimization_barrier((second_b, given_1, rows))
    first_c, second_b = lax.optimization_barrier((first_c, second_b))
    second_c = line_hop(first_c, tok_rows, outward)
    cache_b = jnp.where(middle, first_b, second_b)
    given_2, placed = attend(scalars, 2, guest, stay, both_halves(cache_b), placed)
    back_2 = swapped(given_2, "branch", 0)
    theirs = swapped(rows, "expert", 0)
    rows, theirs, back_0, back_1 = lax.optimization_barrier((rows, theirs, back_0, back_1))
    kept, sent = run_experts(rows, theirs, w_gate, w_up, w_down)
    kept, sent = halve(kept, swapped(sent, "expert", 0))

    second_c, back_2, kept, sent = lax.optimization_barrier((second_c, back_2, kept, sent))
    cache_c = both_halves(jnp.where(middle, first_c, second_c))
    parts = kept + swapped(sent, "branch", 0).astype(jnp.float32)
    homeward = [
        parts[w * CAP : (w + 1) * CAP].astype(jnp.float32 if way == (0, 0) else jnp.bfloat16)
        for w, way in enumerate(ways)
    ]
    guest, *homeward = lax.optimization_barrier((guest, *homeward))
    given_3, placed = attend(scalars, 3, guest, stay, cache_c, placed)
    back_3 = swapped(given_3, "branch", 0)
    homeward = [after(x, given_3) for x in homeward]
    placed = place(scalars, (back_0, back_1, back_2, back_3), placed)
    attended = placed.reshape(tok_rows, step_count, head_count, width)

    sums = [0.0] * experts
    for (k, m), piece in zip(ways, homeward):
        if (k, m) != (0, 0):
            piece = along(piece, -k, m).astype(jnp.float32)
        sums[k] = sums[k] + piece
    sums = jnp.concatenate(sums, axis=0)
    combined = jnp.sum(share[:, :, None] * sums[None, :, :], axis=1)
    moe_out = combined.astype(jnp.bfloat16).reshape(tok_rows, step_count, model_width)
    return (attended, moe_out)


def solution(mesh):
    return jax.shard_map(
        on_device,
        mesh=mesh,
        in_specs=(
            P(("group", "branch"), "expert", None),
            P(("group", "branch"), "expert", None),
            P(("group", "branch", "expert"), None, None, None),
            P(("group", "branch", "expert"), None, None),
            P(("group", "branch", "expert"), None, None),
            P(("group", "branch", "expert"), None, None),
            P(("group", "branch", "expert")),
            P(("group", "branch", "expert"), None, None),
            P(("group", "branch", "expert"), None, None),
            P(("group", "branch", "expert"), None, None),
            P(("branch", "expert"), None, None),
            P(("branch", "expert"), None, None),
            P(("branch", "expert"), None, None),
        ),
        out_specs=(
            P(("group", "branch", "expert"), None, None, None),
            P(("group", "branch", "expert"), None, None),
        ),
        check_vma=False,
    )
```

```python
import functools

import jax
import jax.numpy as jnp
from jax import lax
from jax.experimental import pallas as pl
from jax.experimental.pallas import tpu as pltpu
from jax.sharding import PartitionSpec as P

SHARDS = 8
CAP = 2
LANES = 128
PAD = 16

SMALL = pl.CostEstimate(flops=0, bytes_accessed=1024, transcendentals=0)

LARGE = 62 * 1024 * 1024

softmax_scale = 192.0 ** (-0.5)
log2e = 1.4426950408889634


def after(x, *earlier):
    return lax.optimization_barrier((x, *earlier))[0]


def swapped(x, axis, bit):
    return lax.ppermute(x, axis, [(i, i ^ 1 << bit) for i in range(lax.axis_size(axis))])


def line_hop(x, block, moves):
    pairs = []
    for base in range(0, lax.axis_size("branch"), block):
        for low in range(2):
            pairs += [(base + 2 * i + low, base + 2 * j + low) for i, j in moves]
    return lax.ppermute(x, "branch", pairs)


def pack_cache_kernel(lat_ref, rope_ref, out_ref, sems):
    rows = lat_ref.shape[0]
    copies = [
        pltpu.make_async_copy(lat_ref, out_ref.at[pl.ds(0, rows)], sems.at[0]),
        pltpu.make_async_copy(rope_ref, out_ref.at[pl.ds(rows, rope_ref.shape[0])], sems.at[1]),
    ]
    for copy in copies:
        copy.start()
    for copy in copies:
        copy.wait()


def pack_cache(lat, rope):
    return pl.pallas_call(
        pack_cache_kernel,
        out_shape=jax.ShapeDtypeStruct((lat.shape[0] + rope.shape[0], lat.shape[1]), lat.dtype),
        in_specs=[pl.BlockSpec(memory_space=pltpu.HBM)] * 2,
        out_specs=pl.BlockSpec(memory_space=pltpu.VMEM),
        scratch_shapes=[pltpu.SemaphoreType.DMA((2,))],
        cost_estimate=SMALL,
        compiler_params=pltpu.CompilerParams(vmem_limit_bytes=LARGE),
        name="pack_cache",
    )(lat, rope)


def row_for(slot, parity, slot_ref, own_ref):
    count = slot_ref.shape[0]
    line = count // 2
    own = own_ref[0]
    high = lax.div(own, 2)
    low = lax.rem(own, 2)
    mine = high
    pair = high + 1 - 2 * lax.rem(high, 2)
    first_half = high < line // 2
    nearer = jnp.where(first_half, line // 2, line // 2 - 1)
    farther = jnp.where(first_half, line - 1, 0)
    position = mine
    for number, place_there in ((1, pair), (2, nearer), (3, farther)):
        position = jnp.where(slot == number, place_there, position)
    wanted = 2 * position + (low if parity == 0 else 1 - low)
    row = jnp.int32(0)
    for r in range(1, count):
        row = row + jnp.where(slot_ref[r] == wanted, r, 0)
    return row


def pack_tokens_kernel(parity, slot_ref, own_ref, q_ref, rope_ref, new_ref, out_ref, sems):
    copies = []
    for slot in range(out_ref.shape[0]):
        row = row_for(slot, parity, slot_ref, own_ref)
        start = 0
        for part, source in enumerate((q_ref, rope_ref, new_ref)):
            count = source.shape[1]
            copy = pltpu.make_async_copy(
                source.at[row], out_ref.at[slot, pl.ds(start, count)], sems.at[slot, part]
            )
            copy.start()
            copies.append(copy)
            start += count
    for copy in copies:
        copy.wait()


def pack_tokens(parity, branch_slot, own, q_lat, q_rope, new):
    slots = branch_slot.shape[0] // 2
    sources = (q_lat, q_rope, new)
    rows = sum(x.shape[1] for x in sources)
    return pl.pallas_call(
        functools.partial(pack_tokens_kernel, parity),
        out_shape=jax.ShapeDtypeStruct((slots, rows, q_lat.shape[2]), q_lat.dtype),
        in_specs=[pl.BlockSpec(memory_space=pltpu.SMEM)] * 2
        + [pl.BlockSpec(memory_space=pl.ANY)] * 3,
        out_specs=pl.BlockSpec(memory_space=pltpu.VMEM),
        scratch_shapes=[pltpu.SemaphoreType.DMA((slots, 3))],
        cost_estimate=SMALL,
        compiler_params=pltpu.CompilerParams(vmem_limit_bytes=4 * 1024 * 1024),
        name="pack_tokens",
    )(branch_slot, own, *sources)


def spread_matrix(raw_rows, width):
    per_row = width // (LANES // 2)
    blocks = width // LANES
    shape = (raw_rows * per_row, raw_rows * blocks)
    row = lax.broadcasted_iota(jnp.int32, shape, 0)
    column = lax.broadcasted_iota(jnp.int32, shape, 1)
    wanted = ((row % per_row) // 2) * raw_rows + row // per_row
    return (column == wanted).astype(jnp.bfloat16)


def spread(matrix, raw):
    blocks = raw.shape[1] // LANES
    stacked = jnp.concatenate(
        [raw[:, b * LANES : (b + 1) * LANES] for b in range(blocks)], axis=0
    )
    rows = jnp.dot(matrix, stacked, preferred_element_type=jnp.float32)
    row = lax.broadcasted_iota(jnp.int32, rows.shape, 0)
    lane = lax.broadcasted_iota(jnp.int32, rows.shape, 1)
    return jnp.where(row % 2 == lane // (LANES // 2), rows, 0.0)


def build_attend(heads, steps, width, half, rope_rows, raw_group, chunk):
    q_rows = heads * steps
    token_rope = q_rows // 8

    factor = softmax_scale * log2e
    contract = (((1,), (1,)), ((), ()))

    def put_query_rope(rope_queries, number, raw_rope, matrix):
        grown = raw_group * width // (LANES // 2)
        for i, start in enumerate(range(0, token_rope, raw_group)):
            part = spread(matrix, raw_rope[start : start + raw_group, :])
            part = part + pltpu.roll(part, LANES // 2, 1)
            row = number * q_rows + i * grown
            rope_queries[row : row + grown, :] = part.astype(jnp.bfloat16)

    def merge_own(query, rope_query, fresh_all, peak, total, summed):
        fresh = fresh_all[0:PAD, :]
        fresh_rope = fresh_all[PAD : 2 * PAD, 0:LANES]
        own = lax.dot_general(
            query, fresh, contract, preferred_element_type=jnp.float32
        )
        own = own + lax.dot_general(
            rope_query, fresh_rope, contract, preferred_element_type=jnp.float32
        )
        row_step = lax.broadcasted_iota(jnp.int32, (q_rows, 1), 0) // heads
        columns = [jnp.where(row_step >= j, own[:, j : j + 1], -1e30) for j in range(steps)]
        top = peak
        for column in columns:
            top = jnp.maximum(top, column)
        share = jnp.exp2((peak - top) * factor)
        parts = [
            jnp.where(row_step >= j, jnp.exp2((column - top) * factor), 0.0)
            for j, column in enumerate(columns)
        ]
        denominator = total * share
        for part in parts:
            denominator = denominator + part
        inverse = 1.0 / denominator
        fresh32 = fresh.astype(jnp.float32)
        value = summed * (share * inverse)
        for j, part in enumerate(parts):
            value = value + (part * inverse) * fresh32[j : j + 1, :]
        return value.astype(jnp.bfloat16)

    def put_key_rope(rope_keys, first, raw_rope, matrix):
        grown = raw_group * width // (LANES // 2)
        for i, start in enumerate(range(0, rope_rows, raw_group)):
            part = spread(matrix, raw_rope[start : start + raw_group, :])
            row = first + i * grown
            rope_keys[row : row + grown, :] = part.astype(jnp.bfloat16)

    def kernel(slot, has_placed, slot_ref, own_ref, guest, stay, *refs):
        own_half, other_half = refs[:2]
        refs = refs[3:] if has_placed else refs[2:]
        give, placed, rope_keys, query_rope, scores, summed, result, sem = refs
        tokens = (guest.at[slot], stay.at[slot])
        matrix = spread_matrix(raw_group, width)
        middle = q_rows + token_rope
        for number, token in enumerate(tokens):
            put_query_rope(query_rope, number, token.at[pl.ds(q_rows, token_rope)], matrix)
        peak = None
        for i, cache in enumerate((own_half, other_half)):
            put_key_rope(rope_keys, 0, cache.at[pl.ds(half, rope_rows)], matrix)
            for first in range(0, half, chunk):
                highs = []
                for number, token in enumerate(tokens):
                    rows = slice(number * q_rows, (number + 1) * q_rows)
                    part = lax.dot_general(
                        token[0:q_rows, :],
                        cache[first : first + chunk, :],
                        contract,
                        preferred_element_type=jnp.float32,
                    )
                    part = part + lax.dot_general(
                        query_rope[rows, :],
                        rope_keys[first : first + chunk, :],
                        contract,
                        preferred_element_type=jnp.float32,
                    )
                    scores[rows, i * half + first : i * half + first + chunk] = part
                    highs.append(jnp.max(part, axis=1, keepdims=True))
                high = jnp.concatenate(highs, axis=0)
                peak = high if peak is None else jnp.maximum(peak, high)
        scaled = peak * factor
        total = None
        for first in range(0, 2 * half, chunk):
            cache = own_half if first < half else other_half
            weights = jnp.exp2(scores[:, first : first + chunk] * factor - scaled)
            part = jnp.sum(weights, axis=1, keepdims=True)
            value = jnp.dot(
                weights.astype(jnp.bfloat16),
                cache[first % half : first % half + chunk, :],
                preferred_element_type=jnp.float32,
            )
            if first == 0:
                total = part
                summed[...] = value
            else:
                total = total + part
                summed[...] += value
        for number, token in enumerate(tokens):
            rows = slice(number * q_rows, (number + 1) * q_rows)
            value = merge_own(
                token[0:q_rows, :],
                query_rope[rows, :],
                token[middle : middle + 2 * PAD, :],
                peak[rows],
                total[rows],
                summed[rows, :],
            )
            if number == 0:
                give[...] = value
            else:
                result[...] = value
        row = row_for(slot, 0, slot_ref, own_ref)
        copy = pltpu.make_async_copy(result, placed.at[row], sem)
        copy.start()
        copy.wait()

    def call(scalars, slot, guest, stay, caches, placed):
        count = scalars[0].shape[0]
        vmem = pl.BlockSpec(memory_space=pltpu.VMEM)
        anywhere = pl.BlockSpec(memory_space=pl.ANY)
        operands = [*scalars, guest, stay, *caches]
        in_specs = [pl.BlockSpec(memory_space=pltpu.SMEM)] * 2 + [vmem] * 4
        alias = {}
        if placed is not None:
            alias = {len(operands): 1}
            in_specs.append(anywhere)
            operands.append(placed)
        return pl.pallas_call(
            functools.partial(kernel, slot, placed is not None),
            out_shape=(
                jax.ShapeDtypeStruct((q_rows, width), jnp.bfloat16),
                jax.ShapeDtypeStruct((count, q_rows, width), jnp.bfloat16),
            ),
            in_specs=in_specs,
            out_specs=(vmem, anywhere),
            scratch_shapes=[
                pltpu.VMEM((half, LANES), jnp.bfloat16),
                pltpu.VMEM((2 * q_rows, LANES), jnp.bfloat16),
                pltpu.VMEM((2 * q_rows, 2 * half), jnp.float32),
                pltpu.VMEM((2 * q_rows, width), jnp.float32),
                pltpu.VMEM((q_rows, width), jnp.bfloat16),
                pltpu.SemaphoreType.DMA,
            ],
            input_output_aliases=alias,
            cost_estimate=SMALL,
            compiler_params=pltpu.CompilerParams(vmem_limit_bytes=16 * 1024 * 1024),
            name="attend",
        )(*operands)

    return call


def place_kernel(slot_ref, own_ref, *refs):
    sources, (before, placed_ref, sems) = refs[:-3], refs[-3:]
    copies = []
    for slot, source in enumerate(sources):
        row = row_for(slot, 1, slot_ref, own_ref)
        copies.append(pltpu.make_async_copy(source, placed_ref.at[row], sems.at[slot]))
    for copy in copies:
        copy.start()
    for copy in copies:
        copy.wait()


def place(scalars, sources, placed):
    vmem = pl.BlockSpec(memory_space=pltpu.VMEM)
    return pl.pallas_call(
        place_kernel,
        out_shape=jax.ShapeDtypeStruct(placed.shape, placed.dtype),
        in_specs=[pl.BlockSpec(memory_space=pltpu.SMEM)] * 2
        + [vmem] * len(sources)
        + [pl.BlockSpec(memory_space=pl.ANY)],
        out_specs=pl.BlockSpec(memory_space=pl.ANY),
        scratch_shapes=[pltpu.SemaphoreType.DMA((len(sources),))],
        input_output_aliases={2 + len(sources): 0},
        cost_estimate=SMALL,
        compiler_params=pltpu.CompilerParams(vmem_limit_bytes=4 * 1024 * 1024),
        name="place",
    )(*scalars, *sources, placed)


def dispatch_kernel(experts, block_ref, routes_ref, gate_ref, tokens_ref, *out_refs):
    block = block_ref[0]
    routes = routes_ref[...]
    gates = gate_ref[...]
    rows = routes.shape[0]
    down = lax.broadcasted_iota(jnp.int32, (rows, rows), 0)
    across = lax.broadcasted_iota(jnp.int32, (rows, rows), 1)
    same = (down == across).astype(jnp.float32)
    slots = experts * CAP
    slot_row = lax.broadcasted_iota(jnp.int32, (slots, rows), 0)
    slot_column = lax.broadcasted_iota(jnp.int32, (rows, slots), 1)
    placing = jnp.zeros((slots, rows), jnp.float32)
    share = jnp.zeros((rows, slots), jnp.float32)
    for k in range(experts):
        expert = lax.rem(block + k, experts)
        hit = routes == expert
        has = jnp.sum(hit.astype(jnp.float32), axis=1, keepdims=True)
        weight = jnp.sum(jnp.where(hit, gates, 0.0), axis=1, keepdims=True)
        has_row = jnp.sum(has * same, axis=0, keepdims=True)
        before_row = jnp.sum(jnp.where(down < across, has, 0.0), axis=0, keepdims=True)
        before = jnp.sum(jnp.where(across < down, has_row, 0.0), axis=1, keepdims=True)
        for c in range(CAP):
            slot = k * CAP + c
            placing += jnp.where((slot_row == slot) & (before_row == c), has_row, 0.0)
            share += jnp.where((slot_column == slot) & (before == c), weight, 0.0)
    for k in range(experts):
        out_refs[k][...] = jnp.dot(
            placing[k * CAP : (k + 1) * CAP].astype(jnp.bfloat16),
            tokens_ref[...],
            preferred_element_type=jnp.float32,
        ).astype(jnp.bfloat16)
    out_refs[experts][...] = share


def dispatch(block, routes, gates, tokens, experts):
    slots = experts * CAP
    return pl.pallas_call(
        functools.partial(dispatch_kernel, experts),
        out_shape=(
            *(jax.ShapeDtypeStruct((CAP, tokens.shape[1]), tokens.dtype) for _ in range(experts)),
            jax.ShapeDtypeStruct((tokens.shape[0], slots), jnp.float32),
        ),
        in_specs=[pl.BlockSpec(memory_space=pltpu.SMEM)]
        + [pl.BlockSpec(memory_space=pltpu.VMEM)] * 3,
        out_specs=(pl.BlockSpec(memory_space=pltpu.VMEM),) * (experts + 1),
        cost_estimate=SMALL,
        compiler_params=pltpu.CompilerParams(vmem_limit_bytes=8 * 1024 * 1024),
        name="dispatch",
    )(block, routes, gates, tokens)


def moved_rows(pieces, places, rows):
    total = None
    for piece, places_of_piece in zip(pieces, places):
        shape = (rows, piece.shape[0])
        row = lax.broadcasted_iota(jnp.int32, shape, 0)
        column = lax.broadcasted_iota(jnp.int32, shape, 1)
        chosen = jnp.zeros(shape, jnp.float32)
        for source, there in places_of_piece:
            chosen += ((row == there) & (column == source)).astype(jnp.float32)
        part = jnp.dot(
            chosen.astype(jnp.bfloat16), piece[...], preferred_element_type=jnp.float32
        )
        total = part if total is None else total + part
    return total.astype(jnp.bfloat16)


def stack_kernel(*refs):
    arrays, out_ref = refs[:-1], refs[-1]
    places, start = [], 0
    for array in arrays:
        places.append([(r, start + r) for r in range(array.shape[0])])
        start += array.shape[0]
    out_ref[...] = moved_rows(arrays, places, start)


def stack_rows(*arrays):
    rows = sum(array.shape[0] for array in arrays)
    return pl.pallas_call(
        stack_kernel,
        out_shape=jax.ShapeDtypeStruct((rows, arrays[0].shape[1]), arrays[0].dtype),
        in_specs=[pl.BlockSpec(memory_space=pltpu.VMEM)] * len(arrays),
        out_specs=pl.BlockSpec(memory_space=pltpu.VMEM),
        cost_estimate=SMALL,
        compiler_params=pltpu.CompilerParams(vmem_limit_bytes=8 * 1024 * 1024),
        name="stack_rows",
    )(*arrays)


def experts_kernel(count, *refs):
    row_refs, (gate_hbm, up_hbm, down_hbm) = refs[:count], refs[count : count + 3]
    out_refs = refs[count + 3 : 2 * count + 3]
    gate_ref, up_ref, down_ref, sems = refs[2 * count + 3 :]
    copies = [
        pltpu.make_async_copy(source.at[0], there, sems.at[i])
        for i, (source, there) in enumerate(
            ((gate_hbm, gate_ref), (up_hbm, up_ref), (down_hbm, down_ref))
        )
    ]
    for copy in copies:
        copy.start()
    rows = jnp.concatenate([ref[...].astype(jnp.float32) for ref in row_refs], axis=0)
    rows = rows.astype(jnp.bfloat16)
    copies[0].wait()
    gate = jnp.dot(rows, gate_ref[...], preferred_element_type=jnp.float32)
    copies[1].wait()
    lifted = jnp.dot(rows, up_ref[...], preferred_element_type=jnp.float32)
    hidden = (gate / (1.0 + jnp.exp(-gate)) * lifted).astype(jnp.bfloat16)
    copies[2].wait()
    parts = jnp.dot(hidden, down_ref[...], preferred_element_type=jnp.float32)
    for i, (row_ref, out_ref) in enumerate(zip(row_refs, out_refs)):
        size = row_ref.shape[0]
        out_ref[...] = parts[i * size : (i + 1) * size].astype(out_ref.dtype)


def run_experts(groups, w_gate, w_up, w_down):
    count = len(groups)
    vmem = pl.BlockSpec(memory_space=pltpu.VMEM)
    return pl.pallas_call(
        functools.partial(experts_kernel, count),
        out_shape=tuple(
            jax.ShapeDtypeStruct(x.shape, jnp.bfloat16 if i else jnp.float32)
            for i, x in enumerate(groups)
        ),
        in_specs=[vmem] * count + [pl.BlockSpec(memory_space=pltpu.HBM)] * 3,
        out_specs=(vmem,) * count,
        scratch_shapes=[
            pltpu.VMEM(w_gate.shape[1:], w_gate.dtype),
            pltpu.VMEM(w_up.shape[1:], w_up.dtype),
            pltpu.VMEM(w_down.shape[1:], w_down.dtype),
            pltpu.SemaphoreType.DMA((3,)),
        ],
        cost_estimate=SMALL,
        compiler_params=pltpu.CompilerParams(vmem_limit_bytes=16 * 1024 * 1024),
        name="experts",
    )(*groups, w_gate, w_up, w_down)


def on_device(
    latent_cache,
    rope_cache,
    q_latent,
    q_rope,
    new_latent,
    new_rope,
    branch_slot,
    moe_input,
    routes,
    route_gate,
    w_gate,
    w_up,
    w_down,
):
    tok_rows, step_count, head_count, width = q_latent.shape
    rope_width = new_rope.shape[-1]
    line = tok_rows // 2
    q_rows = step_count * head_count
    half = latent_cache.shape[1]
    rope_rows = rope_cache.shape[1]
    branch = lax.axis_index("branch")
    own = branch % tok_rows
    low = own % 2
    high = own // 2
    middle = jnp.logical_and(high > 0, high < line - 1)

    outer = [(i, i ^ 1) for i in range(line)]
    inner = [(i, i + 1) for i in range(1, line - 1, 2)]
    inner = inner + [(j, i) for i, j in inner]
    outward = [(i, i ^ 1) for i in range(1, line - 1)]
    own_cache = pack_cache(latent_cache[0], rope_cache[0])
    cache_a = line_hop(own_cache, tok_rows, outer)
    first_b = line_hop(own_cache, tok_rows, inner)

    q_lat = q_latent.reshape(tok_rows, q_rows, width)
    rope_raw = q_rope.reshape(tok_rows, q_rows * rope_width // width, width)
    fresh = jnp.concatenate(
        [
            jnp.pad(new_latent, ((0, 0), (0, PAD - step_count), (0, 0))),
            jnp.pad(new_rope, ((0, 0), (0, PAD - step_count), (0, width - rope_width))),
        ],
        axis=1,
    )
    scalars = (branch_slot, own[None])
    sources = (q_lat, rope_raw, fresh)
    leave = pack_tokens(1, branch_slot, after(own[None], own_cache), *sources)
    guest = swapped(leave, "branch", 0)
    stay = pack_tokens(0, branch_slot, after(own[None], leave), *sources)
    attend = build_attend(head_count, step_count, width, half, rope_rows, 32, half // 2)
    model_width = moe_input.shape[-1]
    tok_total = tok_rows * step_count
    device = branch * lax.axis_size("expert") + lax.axis_index("expert")
    experts = lax.axis_size("branch") * lax.axis_size("expert") // SHARDS
    cores = lax.axis_size("expert")
    shard_branches = SHARDS // cores
    block = device // SHARDS
    *outgoing, share = dispatch(
        after(block[None], leave),
        routes.reshape(tok_total, -1),
        route_gate.reshape(tok_total, -1),
        moe_input.reshape(tok_total, model_width),
        experts,
    )

    around = shard_branches // 2

    def along(x, shift, flip):
        count = lax.axis_size("branch")
        there = [
            ((i // shard_branches + shift) % experts) * shard_branches
            + ((i % shard_branches) ^ (flip * 2))
            for i in range(count)
        ]
        return lax.ppermute(x, "branch", list(enumerate(there)))

    ways = [(k, m) for m in range(around) for k in range(experts)]
    pieces = outgoing[:1] + [along(outgoing[k], k, 0) for k in range(1, experts)]
    cache_a, first_b, stay, *pieces = lax.optimization_barrier(
        (cache_a, first_b, stay, *pieces)
    )
    second_b = line_hop(first_b, tok_rows, outward)
    first_c = line_hop(cache_a, tok_rows, inner)

    def both_halves(cache):
        return cache, swapped(cache, "expert", 0)

    guest = after(guest, cache_a, first_b)
    given_0, placed = attend(scalars, 0, guest, stay, both_halves(own_cache), None)
    back_0 = swapped(given_0, "branch", 0)
    rows = stack_rows(*lax.optimization_barrier((given_0, *pieces))[1:])
    rows = [rows] + [along(rows, 0, m) for m in range(1, around)]
    given_1, placed = attend(scalars, 1, guest, stay, both_halves(cache_a), placed)
    back_1 = swapped(given_1, "branch", 0)

    second_b, given_1, back_0, *rows = lax.optimization_barrier(
        (second_b, given_1, back_0, *rows)
    )
    first_c, second_b = lax.optimization_barrier((first_c, second_b))
    second_c = line_hop(first_c, tok_rows, outward)
    cache_b = jnp.where(middle, first_b, second_b)
    given_2, placed = attend(scalars, 2, guest, stay, both_halves(cache_b), placed)
    back_2 = swapped(given_2, "branch", 0)
    rows = stack_rows(*rows)

    def around_chip(x, i):
        pairs = []
        for there in range(lax.axis_size("branch") * cores):
            row, core = there // cores, there % cores
            pairs.append((there, (row ^ (i & 1)) * cores + (core ^ (i >> 1))))
        return lax.ppermute(x, ("branch", "expert"), pairs)

    groups = [rows] + [around_chip(rows, i) for i in range(1, 2 * cores)]
    groups = lax.optimization_barrier((given_2, *groups))[1:]
    parts, *others = run_experts(groups, w_gate, w_up, w_down)
    others = [around_chip(x, i + 1) for i, x in enumerate(others)]

    second_c, back_1, parts, *others = lax.optimization_barrier(
        (second_c, back_1, parts, *others)
    )
    for other in others:
        parts = parts + other.astype(jnp.float32)
    cache_c = both_halves(jnp.where(middle, first_c, second_c))
    homeward = [
        parts[w * CAP : (w + 1) * CAP].astype(jnp.float32 if way == (0, 0) else jnp.bfloat16)
        for w, way in enumerate(ways)
    ]
    homeward = [
        piece if (k, m) == (0, 0) else along(piece, -k, m)
        for (k, m), piece in zip(ways, homeward)
    ]
    guest, back_2 = lax.optimization_barrier((guest, back_2))
    given_3, placed = attend(scalars, 3, guest, stay, cache_c, placed)
    back_3 = swapped(given_3, "branch", 0)
    homeward = [after(x, given_3).astype(jnp.float32) for x in homeward]
    placed = place(scalars, (back_0, back_1, back_2, back_3), placed)
    attended = placed.reshape(tok_rows, step_count, head_count, width)

    sums = [0.0] * experts
    for (k, _), piece in zip(ways, homeward):
        sums[k] = sums[k] + piece
    sums = jnp.concatenate(sums, axis=0)
    combined = jnp.sum(share[:, :, None] * sums[None, :, :], axis=1)
    moe_out = combined.astype(jnp.bfloat16).reshape(tok_rows, step_count, model_width)
    return (attended, moe_out)


def solution(mesh):
    return jax.shard_map(
        on_device,
        mesh=mesh,
        in_specs=(
            P(("group", "branch"), "expert", None),
            P(("group", "branch"), "expert", None),
            P(("group", "branch", "expert"), None, None, None),
            P(("group", "branch", "expert"), None, None),
            P(("group", "branch", "expert"), None, None),
            P(("group", "branch", "expert"), None, None),
            P(("group", "branch", "expert")),
            P(("group", "branch", "expert"), None, None),
            P(("group", "branch", "expert"), None, None),
            P(("group", "branch", "expert"), None, None),
            P(("branch", "expert"), None, None),
            P(("branch", "expert"), None, None),
            P(("branch", "expert"), None, None),
        ),
        out_specs=(
            P(("group", "branch", "expert"), None, None, None),
            P(("group", "branch", "expert"), None, None),
        ),
        check_vma=False,
    )
```

```python
import functools

import jax
import jax.numpy as jnp
from jax import lax
from jax.experimental import pallas as pl
from jax.experimental.pallas import tpu as pltpu
from jax.sharding import PartitionSpec as P

SHARDS = 8
CAP = 2
LANES = 128
PAD = 16

SMALL = pl.CostEstimate(flops=0, bytes_accessed=1024, transcendentals=0)

LARGE = 62 * 1024 * 1024

softmax_scale = 192.0 ** (-0.5)
log2e = 1.4426950408889634


def after(x, *earlier):
    return lax.optimization_barrier((x, *earlier))[0]


def swapped(x, axis, bit):
    return lax.ppermute(x, axis, [(i, i ^ 1 << bit) for i in range(lax.axis_size(axis))])


def line_hop(x, block, moves):
    pairs = []
    for base in range(0, lax.axis_size("branch"), block):
        for low in range(2):
            pairs += [(base + 2 * i + low, base + 2 * j + low) for i, j in moves]
    return lax.ppermute(x, "branch", pairs)


def pack_cache_kernel(lat_ref, rope_ref, out_ref, sems):
    rows = lat_ref.shape[0]
    copies = [
        pltpu.make_async_copy(lat_ref, out_ref.at[pl.ds(0, rows)], sems.at[0]),
        pltpu.make_async_copy(rope_ref, out_ref.at[pl.ds(rows, rope_ref.shape[0])], sems.at[1]),
    ]
    for copy in copies:
        copy.start()
    for copy in copies:
        copy.wait()


def pack_cache(lat, rope):
    return pl.pallas_call(
        pack_cache_kernel,
        out_shape=jax.ShapeDtypeStruct((lat.shape[0] + rope.shape[0], lat.shape[1]), lat.dtype),
        in_specs=[pl.BlockSpec(memory_space=pltpu.HBM)] * 2,
        out_specs=pl.BlockSpec(memory_space=pltpu.VMEM),
        scratch_shapes=[pltpu.SemaphoreType.DMA((2,))],
        cost_estimate=SMALL,
        compiler_params=pltpu.CompilerParams(vmem_limit_bytes=LARGE),
        name="pack_cache",
    )(lat, rope)


def row_for(slot, parity, slot_ref, own_ref):
    count = slot_ref.shape[0]
    line = count // 2
    own = own_ref[0]
    high = lax.div(own, 2)
    low = lax.rem(own, 2)
    mine = high
    pair = high + 1 - 2 * lax.rem(high, 2)
    first_half = high < line // 2
    nearer = jnp.where(first_half, line // 2, line // 2 - 1)
    farther = jnp.where(first_half, line - 1, 0)
    position = mine
    for number, place_there in ((1, pair), (2, nearer), (3, farther)):
        position = jnp.where(slot == number, place_there, position)
    wanted = 2 * position + (low if parity == 0 else 1 - low)
    row = jnp.int32(0)
    for r in range(1, count):
        row = row + jnp.where(slot_ref[r] == wanted, r, 0)
    return row


def pack_tokens_kernel(parity, slot_ref, own_ref, q_ref, rope_ref, new_ref, out_ref, sems):
    copies = []
    for slot in range(out_ref.shape[0]):
        row = row_for(slot, parity, slot_ref, own_ref)
        start = 0
        for part, source in enumerate((q_ref, rope_ref, new_ref)):
            count = source.shape[1]
            copy = pltpu.make_async_copy(
                source.at[row], out_ref.at[slot, pl.ds(start, count)], sems.at[slot, part]
            )
            copy.start()
            copies.append(copy)
            start += count
    for copy in copies:
        copy.wait()


def pack_tokens(parity, branch_slot, own, q_lat, q_rope, new):
    slots = branch_slot.shape[0] // 2
    sources = (q_lat, q_rope, new)
    rows = sum(x.shape[1] for x in sources)
    return pl.pallas_call(
        functools.partial(pack_tokens_kernel, parity),
        out_shape=jax.ShapeDtypeStruct((slots, rows, q_lat.shape[2]), q_lat.dtype),
        in_specs=[pl.BlockSpec(memory_space=pltpu.SMEM)] * 2
        + [pl.BlockSpec(memory_space=pl.ANY)] * 3,
        out_specs=pl.BlockSpec(memory_space=pltpu.VMEM),
        scratch_shapes=[pltpu.SemaphoreType.DMA((slots, 3))],
        cost_estimate=SMALL,
        compiler_params=pltpu.CompilerParams(vmem_limit_bytes=4 * 1024 * 1024),
        name="pack_tokens",
    )(branch_slot, own, *sources)


def spread_matrix(raw_rows, width):
    per_row = width // (LANES // 2)
    blocks = width // LANES
    shape = (raw_rows * per_row, raw_rows * blocks)
    row = lax.broadcasted_iota(jnp.int32, shape, 0)
    column = lax.broadcasted_iota(jnp.int32, shape, 1)
    wanted = ((row % per_row) // 2) * raw_rows + row // per_row
    return (column == wanted).astype(jnp.bfloat16)


def spread(matrix, raw):
    blocks = raw.shape[1] // LANES
    stacked = jnp.concatenate(
        [raw[:, b * LANES : (b + 1) * LANES] for b in range(blocks)], axis=0
    )
    rows = jnp.dot(matrix, stacked, preferred_element_type=jnp.float32)
    row = lax.broadcasted_iota(jnp.int32, rows.shape, 0)
    lane = lax.broadcasted_iota(jnp.int32, rows.shape, 1)
    return jnp.where(row % 2 == lane // (LANES // 2), rows, 0.0)


def build_attend(heads, steps, width, half, rope_rows, raw_group, chunk):
    q_rows = heads * steps
    token_rope = q_rows // 8

    factor = softmax_scale * log2e
    contract = (((1,), (1,)), ((), ()))

    def put_query_rope(rope_queries, number, raw_rope, matrix):
        grown = raw_group * width // (LANES // 2)
        for i, start in enumerate(range(0, token_rope, raw_group)):
            part = spread(matrix, raw_rope[start : start + raw_group, :])
            part = part + pltpu.roll(part, LANES // 2, 1)
            row = number * q_rows + i * grown
            rope_queries[row : row + grown, :] = part.astype(jnp.bfloat16)

    def merge_own(query, rope_query, fresh_all, peak, total, summed):
        fresh = fresh_all[0:PAD, :]
        fresh_rope = fresh_all[PAD : 2 * PAD, 0:LANES]
        own = lax.dot_general(
            query, fresh, contract, preferred_element_type=jnp.float32
        )
        own = own + lax.dot_general(
            rope_query, fresh_rope, contract, preferred_element_type=jnp.float32
        )
        row_step = lax.broadcasted_iota(jnp.int32, (q_rows, 1), 0) // heads
        columns = [jnp.where(row_step >= j, own[:, j : j + 1], -1e30) for j in range(steps)]
        top = peak
        for column in columns:
            top = jnp.maximum(top, column)
        share = jnp.exp2((peak - top) * factor)
        parts = [
            jnp.where(row_step >= j, jnp.exp2((column - top) * factor), 0.0)
            for j, column in enumerate(columns)
        ]
        denominator = total * share
        for part in parts:
            denominator = denominator + part
        inverse = 1.0 / denominator
        fresh32 = fresh.astype(jnp.float32)
        value = summed * (share * inverse)
        for j, part in enumerate(parts):
            value = value + (part * inverse) * fresh32[j : j + 1, :]
        return value.astype(jnp.bfloat16)

    def put_key_rope(rope_keys, first, raw_rope, matrix):
        grown = raw_group * width // (LANES // 2)
        for i, start in enumerate(range(0, rope_rows, raw_group)):
            part = spread(matrix, raw_rope[start : start + raw_group, :])
            row = first + i * grown
            rope_keys[row : row + grown, :] = part.astype(jnp.bfloat16)

    def kernel(slot, gives, keeps, has_placed, slot_ref, own_ref, *refs):
        refs = list(refs)
        tokens = [refs.pop(0).at[slot] for _ in range(gives + keeps)]
        own_half, other_half = refs.pop(0), refs.pop(0)
        if has_placed:
            refs.pop(0)
        give = refs.pop(0) if gives else None
        placed = refs.pop(0) if keeps else None
        rope_keys, query_rope, scores, summed, result, sem = refs
        matrix = spread_matrix(raw_group, width)
        middle = q_rows + token_rope
        for number, token in enumerate(tokens):
            put_query_rope(query_rope, number, token.at[pl.ds(q_rows, token_rope)], matrix)
        peak = None
        for i, cache in enumerate((own_half, other_half)):
            put_key_rope(rope_keys, 0, cache.at[pl.ds(half, rope_rows)], matrix)
            for first in range(0, half, chunk):
                highs = []
                for number, token in enumerate(tokens):
                    rows = slice(number * q_rows, (number + 1) * q_rows)
                    part = lax.dot_general(
                        token[0:q_rows, :],
                        cache[first : first + chunk, :],
                        contract,
                        preferred_element_type=jnp.float32,
                    )
                    part = part + lax.dot_general(
                        query_rope[rows, :],
                        rope_keys[first : first + chunk, :],
                        contract,
                        preferred_element_type=jnp.float32,
                    )
                    scores[rows, i * half + first : i * half + first + chunk] = part
                    highs.append(jnp.max(part, axis=1, keepdims=True))
                high = jnp.concatenate(highs, axis=0) if len(highs) > 1 else highs[0]
                peak = high if peak is None else jnp.maximum(peak, high)
        scaled = peak * factor
        total = None
        for first in range(0, 2 * half, chunk):
            cache = own_half if first < half else other_half
            weights = jnp.exp2(scores[:, first : first + chunk] * factor - scaled)
            part = jnp.sum(weights, axis=1, keepdims=True)
            value = jnp.dot(
                weights.astype(jnp.bfloat16),
                cache[first % half : first % half + chunk, :],
                preferred_element_type=jnp.float32,
            )
            if first == 0:
                total = part
                summed[...] = value
            else:
                total = total + part
                summed[...] += value
        for number, token in enumerate(tokens):
            rows = slice(number * q_rows, (number + 1) * q_rows)
            value = merge_own(
                token[0:q_rows, :],
                query_rope[rows, :],
                token[middle : middle + 2 * PAD, :],
                peak[rows],
                total[rows],
                summed[rows, :],
            )
            if number < gives:
                give[...] = value
            else:
                result[...] = value
        if keeps:
            row = row_for(slot, 0, slot_ref, own_ref)
            copy = pltpu.make_async_copy(result, placed.at[row], sem)
            copy.start()
            copy.wait()

    def call(scalars, slot, guest, stay, caches, placed):
        count = scalars[0].shape[0]
        vmem = pl.BlockSpec(memory_space=pltpu.VMEM)
        anywhere = pl.BlockSpec(memory_space=pl.ANY)
        gives, keeps = int(guest is not None), int(stay is not None)
        n_tok = gives + keeps
        operands = [x for x in (guest, stay) if x is not None] + [*caches]
        in_specs = [pl.BlockSpec(memory_space=pltpu.SMEM)] * 2 + [vmem] * len(operands)
        operands = [*scalars, *operands]
        out_shape, out_specs, alias = [], [], {}
        if gives:
            out_shape.append(jax.ShapeDtypeStruct((q_rows, width), jnp.bfloat16))
            out_specs.append(vmem)
        if keeps:
            out_shape.append(jax.ShapeDtypeStruct((count, q_rows, width), jnp.bfloat16))
            out_specs.append(anywhere)
        has_placed = bool(keeps and placed is not None)
        if has_placed:
            alias = {len(operands): gives}
            in_specs.append(anywhere)
            operands.append(placed)
        return pl.pallas_call(
            functools.partial(kernel, slot, gives, keeps, has_placed),
            out_shape=tuple(out_shape),
            in_specs=in_specs,
            out_specs=tuple(out_specs),
            scratch_shapes=[
                pltpu.VMEM((half, LANES), jnp.bfloat16),
                pltpu.VMEM((n_tok * q_rows, LANES), jnp.bfloat16),
                pltpu.VMEM((n_tok * q_rows, 2 * half), jnp.float32),
                pltpu.VMEM((n_tok * q_rows, width), jnp.float32),
                pltpu.VMEM((q_rows, width), jnp.bfloat16),
                pltpu.SemaphoreType.DMA,
            ],
            input_output_aliases=alias,
            cost_estimate=SMALL,
            compiler_params=pltpu.CompilerParams(vmem_limit_bytes=16 * 1024 * 1024),
            name="attend",
        )(*operands)

    return call


def place_kernel(slot_ref, own_ref, *refs):
    sources, (before, placed_ref, sems) = refs[:-3], refs[-3:]
    copies = []
    for slot, source in enumerate(sources):
        row = row_for(slot, 1, slot_ref, own_ref)
        copies.append(pltpu.make_async_copy(source, placed_ref.at[row], sems.at[slot]))
    for copy in copies:
        copy.start()
    for copy in copies:
        copy.wait()


def place(scalars, sources, placed):
    vmem = pl.BlockSpec(memory_space=pltpu.VMEM)
    return pl.pallas_call(
        place_kernel,
        out_shape=jax.ShapeDtypeStruct(placed.shape, placed.dtype),
        in_specs=[pl.BlockSpec(memory_space=pltpu.SMEM)] * 2
        + [vmem] * len(sources)
        + [pl.BlockSpec(memory_space=pl.ANY)],
        out_specs=pl.BlockSpec(memory_space=pl.ANY),
        scratch_shapes=[pltpu.SemaphoreType.DMA((len(sources),))],
        input_output_aliases={2 + len(sources): 0},
        cost_estimate=SMALL,
        compiler_params=pltpu.CompilerParams(vmem_limit_bytes=4 * 1024 * 1024),
        name="place",
    )(*scalars, *sources, placed)


def dispatch_kernel(experts, block_ref, routes_ref, gate_ref, tokens_ref, *out_refs):
    block = block_ref[0]
    routes = routes_ref[...]
    gates = gate_ref[...]
    rows = routes.shape[0]
    down = lax.broadcasted_iota(jnp.int32, (rows, rows), 0)
    across = lax.broadcasted_iota(jnp.int32, (rows, rows), 1)
    same = (down == across).astype(jnp.float32)
    slots = experts * CAP
    slot_row = lax.broadcasted_iota(jnp.int32, (slots, rows), 0)
    slot_column = lax.broadcasted_iota(jnp.int32, (rows, slots), 1)
    placing = jnp.zeros((slots, rows), jnp.float32)
    share = jnp.zeros((rows, slots), jnp.float32)
    for k in range(experts):
        expert = lax.rem(block + k, experts)
        hit = routes == expert
        has = jnp.sum(hit.astype(jnp.float32), axis=1, keepdims=True)
        weight = jnp.sum(jnp.where(hit, gates, 0.0), axis=1, keepdims=True)
        has_row = jnp.sum(has * same, axis=0, keepdims=True)
        before_row = jnp.sum(jnp.where(down < across, has, 0.0), axis=0, keepdims=True)
        before = jnp.sum(jnp.where(across < down, has_row, 0.0), axis=1, keepdims=True)
        for c in range(CAP):
            slot = k * CAP + c
            placing += jnp.where((slot_row == slot) & (before_row == c), has_row, 0.0)
            share += jnp.where((slot_column == slot) & (before == c), weight, 0.0)
    for k in range(experts):
        out_refs[k][...] = jnp.dot(
            placing[k * CAP : (k + 1) * CAP].astype(jnp.bfloat16),
            tokens_ref[...],
            preferred_element_type=jnp.float32,
        ).astype(jnp.bfloat16)
    out_refs[experts][...] = share


def dispatch(block, routes, gates, tokens, experts):
    slots = experts * CAP
    return pl.pallas_call(
        functools.partial(dispatch_kernel, experts),
        out_shape=(
            *(jax.ShapeDtypeStruct((CAP, tokens.shape[1]), tokens.dtype) for _ in range(experts)),
            jax.ShapeDtypeStruct((tokens.shape[0], slots), jnp.float32),
        ),
        in_specs=[pl.BlockSpec(memory_space=pltpu.SMEM)]
        + [pl.BlockSpec(memory_space=pltpu.VMEM)] * 3,
        out_specs=(pl.BlockSpec(memory_space=pltpu.VMEM),) * (experts + 1),
        cost_estimate=SMALL,
        compiler_params=pltpu.CompilerParams(vmem_limit_bytes=8 * 1024 * 1024),
        name="dispatch",
    )(block, routes, gates, tokens)


def moved_rows(pieces, places, rows):
    total = None
    for piece, places_of_piece in zip(pieces, places):
        shape = (rows, piece.shape[0])
        row = lax.broadcasted_iota(jnp.int32, shape, 0)
        column = lax.broadcasted_iota(jnp.int32, shape, 1)
        chosen = jnp.zeros(shape, jnp.float32)
        for source, there in places_of_piece:
            chosen += ((row == there) & (column == source)).astype(jnp.float32)
        part = jnp.dot(
            chosen.astype(jnp.bfloat16), piece[...], preferred_element_type=jnp.float32
        )
        total = part if total is None else total + part
    return total.astype(jnp.bfloat16)


def stack_kernel(*refs):
    arrays, out_ref = refs[:-1], refs[-1]
    places, start = [], 0
    for array in arrays:
        places.append([(r, start + r) for r in range(array.shape[0])])
        start += array.shape[0]
    out_ref[...] = moved_rows(arrays, places, start)


def stack_rows(*arrays):
    rows = sum(array.shape[0] for array in arrays)
    return pl.pallas_call(
        stack_kernel,
        out_shape=jax.ShapeDtypeStruct((rows, arrays[0].shape[1]), arrays[0].dtype),
        in_specs=[pl.BlockSpec(memory_space=pltpu.VMEM)] * len(arrays),
        out_specs=pl.BlockSpec(memory_space=pltpu.VMEM),
        cost_estimate=SMALL,
        compiler_params=pltpu.CompilerParams(vmem_limit_bytes=8 * 1024 * 1024),
        name="stack_rows",
    )(*arrays)


def experts_kernel(count, *refs):
    row_refs, (gate_hbm, up_hbm, down_hbm) = refs[:count], refs[count : count + 3]
    out_refs = refs[count + 3 : 2 * count + 3]
    gate_ref, up_ref, down_ref, sems = refs[2 * count + 3 :]
    copies = [
        pltpu.make_async_copy(source.at[0], there, sems.at[i])
        for i, (source, there) in enumerate(
            ((gate_hbm, gate_ref), (up_hbm, up_ref), (down_hbm, down_ref))
        )
    ]
    for copy in copies:
        copy.start()
    rows = jnp.concatenate([ref[...].astype(jnp.float32) for ref in row_refs], axis=0)
    rows = rows.astype(jnp.bfloat16)
    copies[0].wait()
    gate = jnp.dot(rows, gate_ref[...], preferred_element_type=jnp.float32)
    copies[1].wait()
    lifted = jnp.dot(rows, up_ref[...], preferred_element_type=jnp.float32)
    hidden = (gate / (1.0 + jnp.exp(-gate)) * lifted).astype(jnp.bfloat16)
    copies[2].wait()
    parts = jnp.dot(hidden, down_ref[...], preferred_element_type=jnp.float32)
    for i, (row_ref, out_ref) in enumerate(zip(row_refs, out_refs)):
        size = row_ref.shape[0]
        out_ref[...] = parts[i * size : (i + 1) * size].astype(out_ref.dtype)


def run_experts(groups, w_gate, w_up, w_down):
    count = len(groups)
    vmem = pl.BlockSpec(memory_space=pltpu.VMEM)
    return pl.pallas_call(
        functools.partial(experts_kernel, count),
        out_shape=tuple(
            jax.ShapeDtypeStruct(x.shape, jnp.bfloat16 if i else jnp.float32)
            for i, x in enumerate(groups)
        ),
        in_specs=[vmem] * count + [pl.BlockSpec(memory_space=pltpu.HBM)] * 3,
        out_specs=(vmem,) * count,
        scratch_shapes=[
            pltpu.VMEM(w_gate.shape[1:], w_gate.dtype),
            pltpu.VMEM(w_up.shape[1:], w_up.dtype),
            pltpu.VMEM(w_down.shape[1:], w_down.dtype),
            pltpu.SemaphoreType.DMA((3,)),
        ],
        cost_estimate=SMALL,
        compiler_params=pltpu.CompilerParams(vmem_limit_bytes=16 * 1024 * 1024),
        name="experts",
    )(*groups, w_gate, w_up, w_down)


def on_device(
    latent_cache,
    rope_cache,
    q_latent,
    q_rope,
    new_latent,
    new_rope,
    branch_slot,
    moe_input,
    routes,
    route_gate,
    w_gate,
    w_up,
    w_down,
):
    tok_rows, step_count, head_count, width = q_latent.shape
    rope_width = new_rope.shape[-1]
    line = tok_rows // 2
    q_rows = step_count * head_count
    half = latent_cache.shape[1]
    rope_rows = rope_cache.shape[1]
    branch = lax.axis_index("branch")
    own = branch % tok_rows
    low = own % 2
    high = own // 2
    middle = jnp.logical_and(high > 0, high < line - 1)

    outer = [(i, i ^ 1) for i in range(line)]
    inner = [(i, i + 1) for i in range(1, line - 1, 2)]
    inner = inner + [(j, i) for i, j in inner]
    outward = [(i, i ^ 1) for i in range(1, line - 1)]
    own_cache = pack_cache(latent_cache[0], rope_cache[0])
    cache_a = line_hop(own_cache, tok_rows, outer)
    first_b = line_hop(own_cache, tok_rows, inner)

    q_lat = q_latent.reshape(tok_rows, q_rows, width)
    rope_raw = q_rope.reshape(tok_rows, q_rows * rope_width // width, width)
    fresh = jnp.concatenate(
        [
            jnp.pad(new_latent, ((0, 0), (0, PAD - step_count), (0, 0))),
            jnp.pad(new_rope, ((0, 0), (0, PAD - step_count), (0, width - rope_width))),
        ],
        axis=1,
    )
    scalars = (branch_slot, own[None])
    sources = (q_lat, rope_raw, fresh)
    leave = pack_tokens(1, branch_slot, after(own[None], own_cache), *sources)
    guest = swapped(leave, "branch", 0)
    stay = pack_tokens(0, branch_slot, after(own[None], leave), *sources)
    attend = build_attend(head_count, step_count, width, half, rope_rows, 32, half // 2)
    model_width = moe_input.shape[-1]
    tok_total = tok_rows * step_count
    device = branch * lax.axis_size("expert") + lax.axis_index("expert")
    experts = lax.axis_size("branch") * lax.axis_size("expert") // SHARDS
    cores = lax.axis_size("expert")
    shard_branches = SHARDS // cores
    block = device // SHARDS
    *outgoing, share = dispatch(
        after(block[None], leave),
        routes.reshape(tok_total, -1),
        route_gate.reshape(tok_total, -1),
        moe_input.reshape(tok_total, model_width),
        experts,
    )

    around = shard_branches // 2

    def along(x, shift, flip):
        count = lax.axis_size("branch")
        there = [
            ((i // shard_branches + shift) % experts) * shard_branches
            + ((i % shard_branches) ^ (flip * 2))
            for i in range(count)
        ]
        return lax.ppermute(x, "branch", list(enumerate(there)))

    ways = [(k, m) for m in range(around) for k in range(experts)]
    pieces = outgoing[:1] + [along(outgoing[k], k, 0) for k in range(1, experts)]
    cache_a, first_b, stay, *pieces = lax.optimization_barrier(
        (cache_a, first_b, stay, *pieces)
    )
    second_b = line_hop(first_b, tok_rows, outward)
    first_c = line_hop(cache_a, tok_rows, inner)

    def both_halves(cache):
        return cache, swapped(cache, "expert", 0)

    guest = after(guest, cache_a, first_b)
    given_0, placed = attend(scalars, 0, guest, stay, both_halves(own_cache), None)
    back_0 = swapped(given_0, "branch", 0)
    rows = stack_rows(*lax.optimization_barrier((given_0, *pieces))[1:])
    rows = [rows] + [along(rows, 0, m) for m in range(1, around)]
    given_1, placed = attend(scalars, 1, guest, stay, both_halves(cache_a), placed)
    back_1 = swapped(given_1, "branch", 0)

    first_c, given_1, back_0, first_b, *rows = lax.optimization_barrier(
        (first_c, given_1, back_0, first_b, *rows)
    )
    second_c = line_hop(first_c, tok_rows, outward)
    cache_b = jnp.where(middle, first_b, second_b)
    given_2, placed = attend(scalars, 2, guest, stay, both_halves(cache_b), placed)
    back_2 = swapped(given_2, "branch", 0)
    rows = stack_rows(*rows)

    def around_chip(x, i):
        pairs = []
        for there in range(lax.axis_size("branch") * cores):
            row, core = there // cores, there % cores
            pairs.append((there, (row ^ (i & 1)) * cores + (core ^ (i >> 1))))
        return lax.ppermute(x, ("branch", "expert"), pairs)

    groups = [rows] + [around_chip(rows, i) for i in range(1, 2 * cores)]
    groups = lax.optimization_barrier((given_2, *groups))[1:]
    parts, *others = run_experts(groups, w_gate, w_up, w_down)
    others = [around_chip(x, i + 1) for i, x in enumerate(others)]

    second_c, back_1, parts, *others = lax.optimization_barrier(
        (second_c, back_1, parts, *others)
    )
    for other in others:
        parts = parts + other.astype(jnp.float32)
    cache_c = both_halves(jnp.where(middle, first_c, second_c))
    homeward = [
        parts[w * CAP : (w + 1) * CAP].astype(jnp.float32 if way == (0, 0) else jnp.bfloat16)
        for w, way in enumerate(ways)
    ]
    homeward = [
        piece if (k, m) == (0, 0) else along(piece, -k, m)
        for (k, m), piece in zip(ways, homeward)
    ]
    guest, back_2 = lax.optimization_barrier((guest, back_2))
    (given_3,) = attend(scalars, 3, guest, None, cache_c, None)
    back_3 = swapped(given_3, "branch", 0)
    (placed,) = attend(scalars, 3, None, after(stay, given_3), cache_c, placed)
    homeward = [after(x, given_3).astype(jnp.float32) for x in homeward]
    placed = place(scalars, (back_0, back_1, back_2, back_3), placed)
    attended = placed.reshape(tok_rows, step_count, head_count, width)

    sums = [0.0] * experts
    for (k, _), piece in zip(ways, homeward):
        sums[k] = sums[k] + piece
    sums = jnp.concatenate(sums, axis=0)
    combined = jnp.sum(share[:, :, None] * sums[None, :, :], axis=1)
    moe_out = combined.astype(jnp.bfloat16).reshape(tok_rows, step_count, model_width)
    return (attended, moe_out)


def solution(mesh):
    return jax.shard_map(
        on_device,
        mesh=mesh,
        in_specs=(
            P(("group", "branch"), "expert", None),
            P(("group", "branch"), "expert", None),
            P(("group", "branch", "expert"), None, None, None),
            P(("group", "branch", "expert"), None, None),
            P(("group", "branch", "expert"), None, None),
            P(("group", "branch", "expert"), None, None),
            P(("group", "branch", "expert")),
            P(("group", "branch", "expert"), None, None),
            P(("group", "branch", "expert"), None, None),
            P(("group", "branch", "expert"), None, None),
            P(("branch", "expert"), None, None),
            P(("branch", "expert"), None, None),
            P(("branch", "expert"), None, None),
        ),
        out_specs=(
            P(("group", "branch", "expert"), None, None, None),
            P(("group", "branch", "expert"), None, None),
        ),
        check_vma=False,
    )
```

```python
import functools

import jax
import jax.numpy as jnp
from jax import lax
from jax.experimental import pallas as pl
from jax.experimental.pallas import tpu as pltpu
from jax.sharding import PartitionSpec as P

SHARDS = 8
CAP = 2
LANES = 128
PAD = 16

SMALL = pl.CostEstimate(flops=0, bytes_accessed=1024, transcendentals=0)

LARGE = 62 * 1024 * 1024

softmax_scale = 192.0 ** (-0.5)
log2e = 1.4426950408889634


def after(x, *earlier):
    return lax.optimization_barrier((x, *earlier))[0]


def swapped(x, axis, bit):
    return lax.ppermute(x, axis, [(i, i ^ 1 << bit) for i in range(lax.axis_size(axis))])


def line_hop(x, block, moves):
    pairs = []
    for base in range(0, lax.axis_size("branch"), block):
        for low in range(2):
            pairs += [(base + 2 * i + low, base + 2 * j + low) for i, j in moves]
    return lax.ppermute(x, "branch", pairs)


def pack_cache_kernel(lat_ref, rope_ref, out_ref, sems):
    rows = lat_ref.shape[0]
    copies = [
        pltpu.make_async_copy(lat_ref, out_ref.at[pl.ds(0, rows)], sems.at[0]),
        pltpu.make_async_copy(rope_ref, out_ref.at[pl.ds(rows, rope_ref.shape[0])], sems.at[1]),
    ]
    for copy in copies:
        copy.start()
    for copy in copies:
        copy.wait()


def pack_cache(lat, rope):
    return pl.pallas_call(
        pack_cache_kernel,
        out_shape=jax.ShapeDtypeStruct((lat.shape[0] + rope.shape[0], lat.shape[1]), lat.dtype),
        in_specs=[pl.BlockSpec(memory_space=pltpu.HBM)] * 2,
        out_specs=pl.BlockSpec(memory_space=pltpu.VMEM),
        scratch_shapes=[pltpu.SemaphoreType.DMA((2,))],
        cost_estimate=SMALL,
        compiler_params=pltpu.CompilerParams(vmem_limit_bytes=LARGE),
        name="pack_cache",
    )(lat, rope)


def row_for(slot, parity, slot_ref, own_ref):
    count = slot_ref.shape[0]
    line = count // 2
    own = own_ref[0]
    high = lax.div(own, 2)
    low = lax.rem(own, 2)
    mine = high
    pair = high + 1 - 2 * lax.rem(high, 2)
    first_half = high < line // 2
    nearer = jnp.where(first_half, line // 2, line // 2 - 1)
    farther = jnp.where(first_half, line - 1, 0)
    position = mine
    for number, place_there in ((1, pair), (2, nearer), (3, farther)):
        position = jnp.where(slot == number, place_there, position)
    wanted = 2 * position + (low if parity == 0 else 1 - low)
    row = jnp.int32(0)
    for r in range(1, count):
        row = row + jnp.where(slot_ref[r] == wanted, r, 0)
    return row


def pack_tokens_kernel(parity, slot_ref, own_ref, q_ref, rope_ref, new_ref, out_ref, sems):
    copies = []
    for slot in range(out_ref.shape[0]):
        row = row_for(slot, parity, slot_ref, own_ref)
        start = 0
        for part, source in enumerate((q_ref, rope_ref, new_ref)):
            count = source.shape[1]
            copy = pltpu.make_async_copy(
                source.at[row], out_ref.at[slot, pl.ds(start, count)], sems.at[slot, part]
            )
            copy.start()
            copies.append(copy)
            start += count
    for copy in copies:
        copy.wait()


def pack_tokens(parity, branch_slot, own, q_lat, q_rope, new):
    slots = branch_slot.shape[0] // 2
    sources = (q_lat, q_rope, new)
    rows = sum(x.shape[1] for x in sources)
    return pl.pallas_call(
        functools.partial(pack_tokens_kernel, parity),
        out_shape=jax.ShapeDtypeStruct((slots, rows, q_lat.shape[2]), q_lat.dtype),
        in_specs=[pl.BlockSpec(memory_space=pltpu.SMEM)] * 2
        + [pl.BlockSpec(memory_space=pl.ANY)] * 3,
        out_specs=pl.BlockSpec(memory_space=pltpu.VMEM),
        scratch_shapes=[pltpu.SemaphoreType.DMA((slots, 3))],
        cost_estimate=SMALL,
        compiler_params=pltpu.CompilerParams(vmem_limit_bytes=4 * 1024 * 1024),
        name="pack_tokens",
    )(branch_slot, own, *sources)


def spread_matrix(raw_rows, width):
    per_row = width // (LANES // 2)
    blocks = width // LANES
    shape = (raw_rows * per_row, raw_rows * blocks)
    row = lax.broadcasted_iota(jnp.int32, shape, 0)
    column = lax.broadcasted_iota(jnp.int32, shape, 1)
    wanted = ((row % per_row) // 2) * raw_rows + row // per_row
    return (column == wanted).astype(jnp.bfloat16)


def spread(matrix, raw):
    blocks = raw.shape[1] // LANES
    stacked = jnp.concatenate(
        [raw[:, b * LANES : (b + 1) * LANES] for b in range(blocks)], axis=0
    )
    rows = jnp.dot(matrix, stacked, preferred_element_type=jnp.float32)
    row = lax.broadcasted_iota(jnp.int32, rows.shape, 0)
    lane = lax.broadcasted_iota(jnp.int32, rows.shape, 1)
    return jnp.where(row % 2 == lane // (LANES // 2), rows, 0.0)


def build_attend(heads, steps, width, half, rope_rows, raw_group, chunk):
    q_rows = heads * steps
    token_rope = q_rows // 8

    factor = softmax_scale * log2e
    contract = (((1,), (1,)), ((), ()))

    def put_query_rope(rope_queries, number, raw_rope, matrix):
        grown = raw_group * width // (LANES // 2)
        for i, start in enumerate(range(0, token_rope, raw_group)):
            part = spread(matrix, raw_rope[start : start + raw_group, :])
            part = part + pltpu.roll(part, LANES // 2, 1)
            row = number * q_rows + i * grown
            rope_queries[row : row + grown, :] = part.astype(jnp.bfloat16)

    def merge_own(query, rope_query, fresh_all, peak, total, summed):
        fresh = fresh_all[0:PAD, :]
        fresh_rope = fresh_all[PAD : 2 * PAD, 0:LANES]
        own = lax.dot_general(
            query, fresh, contract, preferred_element_type=jnp.float32
        )
        own = own + lax.dot_general(
            rope_query, fresh_rope, contract, preferred_element_type=jnp.float32
        )
        row_step = lax.broadcasted_iota(jnp.int32, (q_rows, 1), 0) // heads
        columns = [jnp.where(row_step >= j, own[:, j : j + 1], -1e30) for j in range(steps)]
        top = peak
        for column in columns:
            top = jnp.maximum(top, column)
        share = jnp.exp2((peak - top) * factor)
        parts = [
            jnp.where(row_step >= j, jnp.exp2((column - top) * factor), 0.0)
            for j, column in enumerate(columns)
        ]
        denominator = total * share
        for part in parts:
            denominator = denominator + part
        inverse = 1.0 / denominator
        fresh32 = fresh.astype(jnp.float32)
        value = summed * (share * inverse)
        for j, part in enumerate(parts):
            value = value + (part * inverse) * fresh32[j : j + 1, :]
        return value.astype(jnp.bfloat16)

    def put_key_rope(rope_keys, first, raw_rope, matrix):
        grown = raw_group * width // (LANES // 2)
        for i, start in enumerate(range(0, rope_rows, raw_group)):
            part = spread(matrix, raw_rope[start : start + raw_group, :])
            row = first + i * grown
            rope_keys[row : row + grown, :] = part.astype(jnp.bfloat16)

    def kernel(slot, gives, keeps, has_placed, slot_ref, own_ref, *refs):
        refs = list(refs)
        tokens = [refs.pop(0).at[slot] for _ in range(gives + keeps)]
        own_half, other_half = refs.pop(0), refs.pop(0)
        if has_placed:
            refs.pop(0)
        give = refs.pop(0) if gives else None
        placed = refs.pop(0) if keeps else None
        rope_keys, query_rope, scores, summed, result, sem = refs
        matrix = spread_matrix(raw_group, width)
        middle = q_rows + token_rope
        for number, token in enumerate(tokens):
            put_query_rope(query_rope, number, token.at[pl.ds(q_rows, token_rope)], matrix)
        peak = None
        for i, cache in enumerate((own_half, other_half)):
            put_key_rope(rope_keys, 0, cache.at[pl.ds(half, rope_rows)], matrix)
            for first in range(0, half, chunk):
                highs = []
                for number, token in enumerate(tokens):
                    rows = slice(number * q_rows, (number + 1) * q_rows)
                    part = lax.dot_general(
                        token[0:q_rows, :],
                        cache[first : first + chunk, :],
                        contract,
                        preferred_element_type=jnp.float32,
                    )
                    part = part + lax.dot_general(
                        query_rope[rows, :],
                        rope_keys[first : first + chunk, :],
                        contract,
                        preferred_element_type=jnp.float32,
                    )
                    scores[rows, i * half + first : i * half + first + chunk] = part
                    highs.append(jnp.max(part, axis=1, keepdims=True))
                high = jnp.concatenate(highs, axis=0) if len(highs) > 1 else highs[0]
                peak = high if peak is None else jnp.maximum(peak, high)
        scaled = peak * factor
        total = None
        for first in range(0, 2 * half, chunk):
            cache = own_half if first < half else other_half
            weights = jnp.exp2(scores[:, first : first + chunk] * factor - scaled)
            part = jnp.sum(weights, axis=1, keepdims=True)
            value = jnp.dot(
                weights.astype(jnp.bfloat16),
                cache[first % half : first % half + chunk, :],
                preferred_element_type=jnp.float32,
            )
            if first == 0:
                total = part
                summed[...] = value
            else:
                total = total + part
                summed[...] += value
        for number, token in enumerate(tokens):
            rows = slice(number * q_rows, (number + 1) * q_rows)
            value = merge_own(
                token[0:q_rows, :],
                query_rope[rows, :],
                token[middle : middle + 2 * PAD, :],
                peak[rows],
                total[rows],
                summed[rows, :],
            )
            if number < gives:
                give[...] = value
            else:
                result[...] = value
        if keeps:
            row = row_for(slot, 0, slot_ref, own_ref)
            copy = pltpu.make_async_copy(result, placed.at[row], sem)
            copy.start()
            copy.wait()

    def call(scalars, slot, guest, stay, caches, placed):
        count = scalars[0].shape[0]
        vmem = pl.BlockSpec(memory_space=pltpu.VMEM)
        anywhere = pl.BlockSpec(memory_space=pl.ANY)
        gives, keeps = int(guest is not None), int(stay is not None)
        n_tok = gives + keeps
        operands = [x for x in (guest, stay) if x is not None] + [*caches]
        in_specs = [pl.BlockSpec(memory_space=pltpu.SMEM)] * 2 + [vmem] * len(operands)
        operands = [*scalars, *operands]
        out_shape, out_specs, alias = [], [], {}
        if gives:
            out_shape.append(jax.ShapeDtypeStruct((q_rows, width), jnp.bfloat16))
            out_specs.append(vmem)
        if keeps:
            out_shape.append(jax.ShapeDtypeStruct((count, q_rows, width), jnp.bfloat16))
            out_specs.append(anywhere)
        has_placed = bool(keeps and placed is not None)
        if has_placed:
            alias = {len(operands): gives}
            in_specs.append(anywhere)
            operands.append(placed)
        return pl.pallas_call(
            functools.partial(kernel, slot, gives, keeps, has_placed),
            out_shape=tuple(out_shape),
            in_specs=in_specs,
            out_specs=tuple(out_specs),
            scratch_shapes=[
                pltpu.VMEM((half, LANES), jnp.bfloat16),
                pltpu.VMEM((n_tok * q_rows, LANES), jnp.bfloat16),
                pltpu.VMEM((n_tok * q_rows, 2 * half), jnp.float32),
                pltpu.VMEM((n_tok * q_rows, width), jnp.float32),
                pltpu.VMEM((q_rows, width), jnp.bfloat16),
                pltpu.SemaphoreType.DMA,
            ],
            input_output_aliases=alias,
            cost_estimate=SMALL,
            compiler_params=pltpu.CompilerParams(vmem_limit_bytes=16 * 1024 * 1024),
            name="attend",
        )(*operands)

    return call


def place_kernel(slot_ref, own_ref, *refs):
    sources, (before, placed_ref, sems) = refs[:-3], refs[-3:]
    copies = []
    for slot, source in enumerate(sources):
        row = row_for(slot, 1, slot_ref, own_ref)
        copies.append(pltpu.make_async_copy(source, placed_ref.at[row], sems.at[slot]))
    for copy in copies:
        copy.start()
    for copy in copies:
        copy.wait()


def place(scalars, sources, placed):
    vmem = pl.BlockSpec(memory_space=pltpu.VMEM)
    return pl.pallas_call(
        place_kernel,
        out_shape=jax.ShapeDtypeStruct(placed.shape, placed.dtype),
        in_specs=[pl.BlockSpec(memory_space=pltpu.SMEM)] * 2
        + [vmem] * len(sources)
        + [pl.BlockSpec(memory_space=pl.ANY)],
        out_specs=pl.BlockSpec(memory_space=pl.ANY),
        scratch_shapes=[pltpu.SemaphoreType.DMA((len(sources),))],
        input_output_aliases={2 + len(sources): 0},
        cost_estimate=SMALL,
        compiler_params=pltpu.CompilerParams(vmem_limit_bytes=4 * 1024 * 1024),
        name="place",
    )(*scalars, *sources, placed)


def dispatch_kernel(experts, block_ref, routes_ref, gate_ref, tokens_ref, *out_refs):
    block = block_ref[0]
    routes = routes_ref[...]
    gates = gate_ref[...]
    rows = routes.shape[0]
    down = lax.broadcasted_iota(jnp.int32, (rows, rows), 0)
    across = lax.broadcasted_iota(jnp.int32, (rows, rows), 1)
    same = (down == across).astype(jnp.float32)
    slots = experts * CAP
    slot_row = lax.broadcasted_iota(jnp.int32, (slots, rows), 0)
    slot_column = lax.broadcasted_iota(jnp.int32, (rows, slots), 1)
    placing = jnp.zeros((slots, rows), jnp.float32)
    share = jnp.zeros((rows, slots), jnp.float32)
    for k in range(experts):
        expert = lax.rem(block + k, experts)
        hit = routes == expert
        has = jnp.sum(hit.astype(jnp.float32), axis=1, keepdims=True)
        weight = jnp.sum(jnp.where(hit, gates, 0.0), axis=1, keepdims=True)
        has_row = jnp.sum(has * same, axis=0, keepdims=True)
        before_row = jnp.sum(jnp.where(down < across, has, 0.0), axis=0, keepdims=True)
        before = jnp.sum(jnp.where(across < down, has_row, 0.0), axis=1, keepdims=True)
        for c in range(CAP):
            slot = k * CAP + c
            placing += jnp.where((slot_row == slot) & (before_row == c), has_row, 0.0)
            share += jnp.where((slot_column == slot) & (before == c), weight, 0.0)
    for k in range(experts):
        out_refs[k][...] = jnp.dot(
            placing[k * CAP : (k + 1) * CAP].astype(jnp.bfloat16),
            tokens_ref[...],
            preferred_element_type=jnp.float32,
        ).astype(jnp.bfloat16)
    out_refs[experts][...] = share


def dispatch(block, routes, gates, tokens, experts):
    slots = experts * CAP
    return pl.pallas_call(
        functools.partial(dispatch_kernel, experts),
        out_shape=(
            *(jax.ShapeDtypeStruct((CAP, tokens.shape[1]), tokens.dtype) for _ in range(experts)),
            jax.ShapeDtypeStruct((tokens.shape[0], slots), jnp.float32),
        ),
        in_specs=[pl.BlockSpec(memory_space=pltpu.SMEM)]
        + [pl.BlockSpec(memory_space=pltpu.VMEM)] * 3,
        out_specs=(pl.BlockSpec(memory_space=pltpu.VMEM),) * (experts + 1),
        cost_estimate=SMALL,
        compiler_params=pltpu.CompilerParams(vmem_limit_bytes=8 * 1024 * 1024),
        name="dispatch",
    )(block, routes, gates, tokens)


def moved_rows(pieces, places, rows):
    total = None
    for piece, places_of_piece in zip(pieces, places):
        shape = (rows, piece.shape[0])
        row = lax.broadcasted_iota(jnp.int32, shape, 0)
        column = lax.broadcasted_iota(jnp.int32, shape, 1)
        chosen = jnp.zeros(shape, jnp.float32)
        for source, there in places_of_piece:
            chosen += ((row == there) & (column == source)).astype(jnp.float32)
        part = jnp.dot(
            chosen.astype(jnp.bfloat16), piece[...], preferred_element_type=jnp.float32
        )
        total = part if total is None else total + part
    return total.astype(jnp.bfloat16)


def stack_kernel(*refs):
    arrays, out_ref = refs[:-1], refs[-1]
    places, start = [], 0
    for array in arrays:
        places.append([(r, start + r) for r in range(array.shape[0])])
        start += array.shape[0]
    out_ref[...] = moved_rows(arrays, places, start)


def stack_rows(*arrays):
    rows = sum(array.shape[0] for array in arrays)
    return pl.pallas_call(
        stack_kernel,
        out_shape=jax.ShapeDtypeStruct((rows, arrays[0].shape[1]), arrays[0].dtype),
        in_specs=[pl.BlockSpec(memory_space=pltpu.VMEM)] * len(arrays),
        out_specs=pl.BlockSpec(memory_space=pltpu.VMEM),
        cost_estimate=SMALL,
        compiler_params=pltpu.CompilerParams(vmem_limit_bytes=8 * 1024 * 1024),
        name="stack_rows",
    )(*arrays)


def experts_kernel(count, *refs):
    row_refs, (gate_hbm, up_hbm, down_hbm) = refs[:count], refs[count : count + 3]
    out_refs = refs[count + 3 : 2 * count + 3]
    gate_ref, up_ref, down_ref, sems = refs[2 * count + 3 :]
    copies = [
        pltpu.make_async_copy(source.at[0], there, sems.at[i])
        for i, (source, there) in enumerate(
            ((gate_hbm, gate_ref), (up_hbm, up_ref), (down_hbm, down_ref))
        )
    ]
    for copy in copies:
        copy.start()
    rows = jnp.concatenate([ref[...].astype(jnp.float32) for ref in row_refs], axis=0)
    rows = rows.astype(jnp.bfloat16)
    copies[0].wait()
    gate = jnp.dot(rows, gate_ref[...], preferred_element_type=jnp.float32)
    copies[1].wait()
    lifted = jnp.dot(rows, up_ref[...], preferred_element_type=jnp.float32)
    hidden = (gate / (1.0 + jnp.exp(-gate)) * lifted).astype(jnp.bfloat16)
    copies[2].wait()
    parts = jnp.dot(hidden, down_ref[...], preferred_element_type=jnp.float32)
    for i, (row_ref, out_ref) in enumerate(zip(row_refs, out_refs)):
        size = row_ref.shape[0]
        out_ref[...] = parts[i * size : (i + 1) * size].astype(out_ref.dtype)


def run_experts(groups, w_gate, w_up, w_down):
    count = len(groups)
    vmem = pl.BlockSpec(memory_space=pltpu.VMEM)
    return pl.pallas_call(
        functools.partial(experts_kernel, count),
        out_shape=tuple(
            jax.ShapeDtypeStruct(x.shape, jnp.bfloat16 if i else jnp.float32)
            for i, x in enumerate(groups)
        ),
        in_specs=[vmem] * count + [pl.BlockSpec(memory_space=pltpu.HBM)] * 3,
        out_specs=(vmem,) * count,
        scratch_shapes=[
            pltpu.VMEM(w_gate.shape[1:], w_gate.dtype),
            pltpu.VMEM(w_up.shape[1:], w_up.dtype),
            pltpu.VMEM(w_down.shape[1:], w_down.dtype),
            pltpu.SemaphoreType.DMA((3,)),
        ],
        cost_estimate=SMALL,
        compiler_params=pltpu.CompilerParams(vmem_limit_bytes=16 * 1024 * 1024),
        name="experts",
    )(*groups, w_gate, w_up, w_down)


def on_device(
    latent_cache,
    rope_cache,
    q_latent,
    q_rope,
    new_latent,
    new_rope,
    branch_slot,
    moe_input,
    routes,
    route_gate,
    w_gate,
    w_up,
    w_down,
):
    tok_rows, step_count, head_count, width = q_latent.shape
    rope_width = new_rope.shape[-1]
    line = tok_rows // 2
    q_rows = step_count * head_count
    half = latent_cache.shape[1]
    rope_rows = rope_cache.shape[1]
    branch = lax.axis_index("branch")
    own = branch % tok_rows
    low = own % 2
    high = own // 2
    middle = jnp.logical_and(high > 0, high < line - 1)

    outer = [(i, i ^ 1) for i in range(line)]
    inner = [(i, i + 1) for i in range(1, line - 1, 2)]
    inner = inner + [(j, i) for i, j in inner]
    outward = [(i, i ^ 1) for i in range(1, line - 1)]
    own_cache = pack_cache(latent_cache[0], rope_cache[0])
    cache_a = line_hop(own_cache, tok_rows, outer)
    first_b = line_hop(own_cache, tok_rows, inner)

    q_lat = q_latent.reshape(tok_rows, q_rows, width)
    rope_raw = q_rope.reshape(tok_rows, q_rows * rope_width // width, width)
    fresh = jnp.concatenate(
        [
            jnp.pad(new_latent, ((0, 0), (0, PAD - step_count), (0, 0))),
            jnp.pad(new_rope, ((0, 0), (0, PAD - step_count), (0, width - rope_width))),
        ],
        axis=1,
    )
    scalars = (branch_slot, own[None])
    sources = (q_lat, rope_raw, fresh)
    leave = pack_tokens(1, branch_slot, after(own[None], own_cache), *sources)
    guest = swapped(leave, "branch", 0)
    stay = pack_tokens(0, branch_slot, after(own[None], leave), *sources)
    attend = build_attend(head_count, step_count, width, half, rope_rows, 32, half // 2)
    model_width = moe_input.shape[-1]
    tok_total = tok_rows * step_count
    device = branch * lax.axis_size("expert") + lax.axis_index("expert")
    experts = lax.axis_size("branch") * lax.axis_size("expert") // SHARDS
    cores = lax.axis_size("expert")
    shard_branches = SHARDS // cores
    block = device // SHARDS
    *outgoing, share = dispatch(
        after(block[None], leave),
        routes.reshape(tok_total, -1),
        route_gate.reshape(tok_total, -1),
        moe_input.reshape(tok_total, model_width),
        experts,
    )

    around = shard_branches // 2

    def along(x, shift, flip):
        count = lax.axis_size("branch")
        there = [
            ((i // shard_branches + shift) % experts) * shard_branches
            + ((i % shard_branches) ^ (flip * 2))
            for i in range(count)
        ]
        return lax.ppermute(x, "branch", list(enumerate(there)))

    ways = [(k, m) for m in range(around) for k in range(experts)]
    cache_a, first_b, stay, *outgoing = lax.optimization_barrier(
        (cache_a, first_b, stay, *outgoing)
    )
    second_b = line_hop(first_b, tok_rows, outward)
    first_c = line_hop(cache_a, tok_rows, inner)

    def both_halves(cache):
        return cache, swapped(cache, "expert", 0)

    guest = after(guest, cache_a, first_b)
    given_0, placed = attend(scalars, 0, guest, stay, both_halves(own_cache), None)
    back_0 = swapped(given_0, "branch", 0)
    given_1, placed = attend(scalars, 1, guest, stay, both_halves(cache_a), placed)
    back_1 = swapped(given_1, "branch", 0)

    first_c, given_1, first_b = lax.optimization_barrier((first_c, given_1, first_b))
    second_c = line_hop(first_c, tok_rows, outward)
    cache_b = jnp.where(middle, first_b, second_b)
    given_2, placed = attend(scalars, 2, guest, stay, both_halves(cache_b), placed)
    back_2 = swapped(given_2, "branch", 0)
    def around_chip(x, i):
        pairs = []
        for there in range(lax.axis_size("branch") * cores):
            row, core = there // cores, there % cores
            pairs.append((there, (row ^ (i & 1)) * cores + (core ^ (i >> 1))))
        return lax.ppermute(x, ("branch", "expert"), pairs)

    outgoing = lax.optimization_barrier((given_2, back_0, back_1, *outgoing))[3:]
    pieces = [
        outgoing[k] if (k, m) == (0, 0) else along(outgoing[k], k, m) for k, m in ways
    ]

    second_c, back_1, back_2, *pieces = lax.optimization_barrier(
        (second_c, back_1, back_2, *pieces)
    )
    cache_c = both_halves(jnp.where(middle, first_c, second_c))
    rows = stack_rows(*pieces)
    groups = [rows] + [around_chip(rows, i) for i in range(1, 2 * cores)]
    parts, *others = run_experts(groups, w_gate, w_up, w_down)
    others = [around_chip(x, i + 1) for i, x in enumerate(others)]
    guest, parts = lax.optimization_barrier((guest, parts))
    given_3, placed = attend(scalars, 3, guest, stay, cache_c, placed)
    back_3 = swapped(given_3, "branch", 0)
    others = [after(other, given_3) for other in others]
    for other in others:
        parts = parts + other.astype(jnp.float32)
    homeward = [
        parts[w * CAP : (w + 1) * CAP].astype(jnp.float32 if way == (0, 0) else jnp.bfloat16)
        for w, way in enumerate(ways)
    ]
    homeward = [
        piece if (k, m) == (0, 0) else along(piece, -k, m)
        for (k, m), piece in zip(ways, homeward)
    ]
    homeward = [x.astype(jnp.float32) for x in homeward]
    placed = place(scalars, (back_0, back_1, back_2, back_3), placed)
    attended = placed.reshape(tok_rows, step_count, head_count, width)

    sums = [0.0] * experts
    for (k, _), piece in zip(ways, homeward):
        sums[k] = sums[k] + piece
    sums = jnp.concatenate(sums, axis=0)
    combined = jnp.sum(share[:, :, None] * sums[None, :, :], axis=1)
    moe_out = combined.astype(jnp.bfloat16).reshape(tok_rows, step_count, model_width)
    return (attended, moe_out)


def solution(mesh):
    return jax.shard_map(
        on_device,
        mesh=mesh,
        in_specs=(
            P(("group", "branch"), "expert", None),
            P(("group", "branch"), "expert", None),
            P(("group", "branch", "expert"), None, None, None),
            P(("group", "branch", "expert"), None, None),
            P(("group", "branch", "expert"), None, None),
            P(("group", "branch", "expert"), None, None),
            P(("group", "branch", "expert")),
            P(("group", "branch", "expert"), None, None),
            P(("group", "branch", "expert"), None, None),
            P(("group", "branch", "expert"), None, None),
            P(("branch", "expert"), None, None),
            P(("branch", "expert"), None, None),
            P(("branch", "expert"), None, None),
        ),
        out_specs=(
            P(("group", "branch", "expert"), None, None, None),
            P(("group", "branch", "expert"), None, None),
        ),
        check_vma=False,
    )
```

```python
import functools

import jax
import jax.numpy as jnp
from jax import lax
from jax.experimental import pallas as pl
from jax.experimental.pallas import tpu as pltpu
from jax.sharding import PartitionSpec as P

SHARDS = 8
CAP = 2
LANES = 128
PAD = 16

SMALL = pl.CostEstimate(flops=0, bytes_accessed=1024, transcendentals=0)

LARGE = 62 * 1024 * 1024

softmax_scale = 192.0 ** (-0.5)
log2e = 1.4426950408889634


def after(x, *earlier):
    return lax.optimization_barrier((x, *earlier))[0]


def swapped(x, axis, bit):
    return lax.ppermute(x, axis, [(i, i ^ 1 << bit) for i in range(lax.axis_size(axis))])


def line_hop(x, block, moves):
    pairs = []
    for base in range(0, lax.axis_size("branch"), block):
        for low in range(2):
            pairs += [(base + 2 * i + low, base + 2 * j + low) for i, j in moves]
    return lax.ppermute(x, "branch", pairs)


def pack_cache_kernel(lat_ref, rope_ref, out_ref, sems):
    rows = lat_ref.shape[0]
    copies = [
        pltpu.make_async_copy(lat_ref, out_ref.at[pl.ds(0, rows)], sems.at[0]),
        pltpu.make_async_copy(rope_ref, out_ref.at[pl.ds(rows, rope_ref.shape[0])], sems.at[1]),
    ]
    for copy in copies:
        copy.start()
    for copy in copies:
        copy.wait()


def pack_cache(lat, rope):
    return pl.pallas_call(
        pack_cache_kernel,
        out_shape=jax.ShapeDtypeStruct((lat.shape[0] + rope.shape[0], lat.shape[1]), lat.dtype),
        in_specs=[pl.BlockSpec(memory_space=pltpu.HBM)] * 2,
        out_specs=pl.BlockSpec(memory_space=pltpu.VMEM),
        scratch_shapes=[pltpu.SemaphoreType.DMA((2,))],
        cost_estimate=SMALL,
        compiler_params=pltpu.CompilerParams(vmem_limit_bytes=LARGE),
        name="pack_cache",
    )(lat, rope)


def row_for(slot, parity, slot_ref, own_ref):
    count = slot_ref.shape[0]
    line = count // 2
    own = own_ref[0]
    high = lax.div(own, 2)
    low = lax.rem(own, 2)
    mine = high
    pair = high + 1 - 2 * lax.rem(high, 2)
    first_half = high < line // 2
    nearer = jnp.where(first_half, line // 2, line // 2 - 1)
    farther = jnp.where(first_half, line - 1, 0)
    position = mine
    for number, place_there in ((1, pair), (2, nearer), (3, farther)):
        position = jnp.where(slot == number, place_there, position)
    wanted = 2 * position + (low if parity == 0 else 1 - low)
    row = jnp.int32(0)
    for r in range(1, count):
        row = row + jnp.where(slot_ref[r] == wanted, r, 0)
    return row


def pack_tokens_kernel(parity, slot_ref, own_ref, q_ref, rope_ref, new_ref, out_ref, sems):
    copies = []
    for slot in range(out_ref.shape[0]):
        row = row_for(slot, parity, slot_ref, own_ref)
        start = 0
        for part, source in enumerate((q_ref, rope_ref, new_ref)):
            count = source.shape[1]
            copy = pltpu.make_async_copy(
                source.at[row], out_ref.at[slot, pl.ds(start, count)], sems.at[slot, part]
            )
            copy.start()
            copies.append(copy)
            start += count
    for copy in copies:
        copy.wait()


def pack_tokens(parity, branch_slot, own, q_lat, q_rope, new):
    slots = branch_slot.shape[0] // 2
    sources = (q_lat, q_rope, new)
    rows = sum(x.shape[1] for x in sources)
    return pl.pallas_call(
        functools.partial(pack_tokens_kernel, parity),
        out_shape=jax.ShapeDtypeStruct((slots, rows, q_lat.shape[2]), q_lat.dtype),
        in_specs=[pl.BlockSpec(memory_space=pltpu.SMEM)] * 2
        + [pl.BlockSpec(memory_space=pl.ANY)] * 3,
        out_specs=pl.BlockSpec(memory_space=pltpu.VMEM),
        scratch_shapes=[pltpu.SemaphoreType.DMA((slots, 3))],
        cost_estimate=SMALL,
        compiler_params=pltpu.CompilerParams(vmem_limit_bytes=4 * 1024 * 1024),
        name="pack_tokens",
    )(branch_slot, own, *sources)


def spread_matrix(raw_rows, width):
    per_row = width // (LANES // 2)
    blocks = width // LANES
    shape = (raw_rows * per_row, raw_rows * blocks)
    row = lax.broadcasted_iota(jnp.int32, shape, 0)
    column = lax.broadcasted_iota(jnp.int32, shape, 1)
    wanted = ((row % per_row) // 2) * raw_rows + row // per_row
    return (column == wanted).astype(jnp.bfloat16)


def spread(matrix, raw):
    blocks = raw.shape[1] // LANES
    stacked = jnp.concatenate(
        [raw[:, b * LANES : (b + 1) * LANES] for b in range(blocks)], axis=0
    )
    rows = jnp.dot(matrix, stacked, preferred_element_type=jnp.float32)
    row = lax.broadcasted_iota(jnp.int32, rows.shape, 0)
    lane = lax.broadcasted_iota(jnp.int32, rows.shape, 1)
    return jnp.where(row % 2 == lane // (LANES // 2), rows, 0.0)


def build_attend(heads, steps, width, half, rope_rows, raw_group, chunk):
    q_rows = heads * steps
    token_rope = q_rows // 8

    factor = softmax_scale * log2e
    contract = (((1,), (1,)), ((), ()))

    def put_query_rope(rope_queries, number, raw_rope, matrix):
        grown = raw_group * width // (LANES // 2)
        for i, start in enumerate(range(0, token_rope, raw_group)):
            part = spread(matrix, raw_rope[start : start + raw_group, :])
            part = part + pltpu.roll(part, LANES // 2, 1)
            row = number * q_rows + i * grown
            rope_queries[row : row + grown, :] = part.astype(jnp.bfloat16)

    def merge_own(query, rope_query, fresh_all, peak, total, summed):
        fresh = fresh_all[0:PAD, :]
        fresh_rope = fresh_all[PAD : 2 * PAD, 0:LANES]
        own = lax.dot_general(
            query, fresh, contract, preferred_element_type=jnp.float32
        )
        own = own + lax.dot_general(
            rope_query, fresh_rope, contract, preferred_element_type=jnp.float32
        )
        row_step = lax.broadcasted_iota(jnp.int32, (q_rows, 1), 0) // heads
        columns = [jnp.where(row_step >= j, own[:, j : j + 1], -1e30) for j in range(steps)]
        top = peak
        for column in columns:
            top = jnp.maximum(top, column)
        share = jnp.exp2((peak - top) * factor)
        parts = [
            jnp.where(row_step >= j, jnp.exp2((column - top) * factor), 0.0)
            for j, column in enumerate(columns)
        ]
        denominator = total * share
        for part in parts:
            denominator = denominator + part
        inverse = 1.0 / denominator
        fresh32 = fresh.astype(jnp.float32)
        value = summed * (share * inverse)
        for j, part in enumerate(parts):
            value = value + (part * inverse) * fresh32[j : j + 1, :]
        return value.astype(jnp.bfloat16)

    def put_key_rope(rope_keys, first, raw_rope, matrix):
        grown = raw_group * width // (LANES // 2)
        for i, start in enumerate(range(0, rope_rows, raw_group)):
            part = spread(matrix, raw_rope[start : start + raw_group, :])
            row = first + i * grown
            rope_keys[row : row + grown, :] = part.astype(jnp.bfloat16)

    def kernel(slot, gives, keeps, has_placed, slot_ref, own_ref, *refs):
        refs = list(refs)
        tokens = [refs.pop(0).at[slot] for _ in range(gives + keeps)]
        own_half, other_half = refs.pop(0), refs.pop(0)
        if has_placed:
            refs.pop(0)
        give = refs.pop(0) if gives else None
        placed = refs.pop(0) if keeps else None
        rope_keys, query_rope, scores, summed, result, sem = refs
        matrix = spread_matrix(raw_group, width)
        middle = q_rows + token_rope
        for number, token in enumerate(tokens):
            put_query_rope(query_rope, number, token.at[pl.ds(q_rows, token_rope)], matrix)
        peak = None
        for i, cache in enumerate((own_half, other_half)):
            put_key_rope(rope_keys, 0, cache.at[pl.ds(half, rope_rows)], matrix)
            for first in range(0, half, chunk):
                highs = []
                for number, token in enumerate(tokens):
                    rows = slice(number * q_rows, (number + 1) * q_rows)
                    part = lax.dot_general(
                        token[0:q_rows, :],
                        cache[first : first + chunk, :],
                        contract,
                        preferred_element_type=jnp.float32,
                    )
                    part = part + lax.dot_general(
                        query_rope[rows, :],
                        rope_keys[first : first + chunk, :],
                        contract,
                        preferred_element_type=jnp.float32,
                    )
                    scores[rows, i * half + first : i * half + first + chunk] = part
                    highs.append(jnp.max(part, axis=1, keepdims=True))
                high = jnp.concatenate(highs, axis=0) if len(highs) > 1 else highs[0]
                peak = high if peak is None else jnp.maximum(peak, high)
        scaled = peak * factor
        total = None
        for first in range(0, 2 * half, chunk):
            cache = own_half if first < half else other_half
            weights = jnp.exp2(scores[:, first : first + chunk] * factor - scaled)
            part = jnp.sum(weights, axis=1, keepdims=True)
            value = jnp.dot(
                weights.astype(jnp.bfloat16),
                cache[first % half : first % half + chunk, :],
                preferred_element_type=jnp.float32,
            )
            if first == 0:
                total = part
                summed[...] = value
            else:
                total = total + part
                summed[...] += value
        for number, token in enumerate(tokens):
            rows = slice(number * q_rows, (number + 1) * q_rows)
            value = merge_own(
                token[0:q_rows, :],
                query_rope[rows, :],
                token[middle : middle + 2 * PAD, :],
                peak[rows],
                total[rows],
                summed[rows, :],
            )
            if number < gives:
                give[...] = value
            else:
                result[...] = value
        if keeps:
            row = row_for(slot, 0, slot_ref, own_ref)
            copy = pltpu.make_async_copy(result, placed.at[row], sem)
            copy.start()
            copy.wait()

    def call(scalars, slot, guest, stay, caches, placed):
        count = scalars[0].shape[0]
        vmem = pl.BlockSpec(memory_space=pltpu.VMEM)
        anywhere = pl.BlockSpec(memory_space=pl.ANY)
        gives, keeps = int(guest is not None), int(stay is not None)
        n_tok = gives + keeps
        operands = [x for x in (guest, stay) if x is not None] + [*caches]
        in_specs = [pl.BlockSpec(memory_space=pltpu.SMEM)] * 2 + [vmem] * len(operands)
        operands = [*scalars, *operands]
        out_shape, out_specs, alias = [], [], {}
        if gives:
            out_shape.append(jax.ShapeDtypeStruct((q_rows, width), jnp.bfloat16))
            out_specs.append(vmem)
        if keeps:
            out_shape.append(jax.ShapeDtypeStruct((count, q_rows, width), jnp.bfloat16))
            out_specs.append(anywhere)
        has_placed = bool(keeps and placed is not None)
        if has_placed:
            alias = {len(operands): gives}
            in_specs.append(anywhere)
            operands.append(placed)
        return pl.pallas_call(
            functools.partial(kernel, slot, gives, keeps, has_placed),
            out_shape=tuple(out_shape),
            in_specs=in_specs,
            out_specs=tuple(out_specs),
            scratch_shapes=[
                pltpu.VMEM((half, LANES), jnp.bfloat16),
                pltpu.VMEM((n_tok * q_rows, LANES), jnp.bfloat16),
                pltpu.VMEM((n_tok * q_rows, 2 * half), jnp.float32),
                pltpu.VMEM((n_tok * q_rows, width), jnp.float32),
                pltpu.VMEM((q_rows, width), jnp.bfloat16),
                pltpu.SemaphoreType.DMA,
            ],
            input_output_aliases=alias,
            cost_estimate=SMALL,
            compiler_params=pltpu.CompilerParams(vmem_limit_bytes=(4 + 4 * n_tok) * 1024 * 1024),
            name="attend",
        )(*operands)

    return call


def place_kernel(slot_ref, own_ref, *refs):
    sources, (before, placed_ref, sems) = refs[:-3], refs[-3:]
    copies = []
    for slot, source in enumerate(sources):
        row = row_for(slot, 1, slot_ref, own_ref)
        copies.append(pltpu.make_async_copy(source, placed_ref.at[row], sems.at[slot]))
    for copy in copies:
        copy.start()
    for copy in copies:
        copy.wait()


def place(scalars, sources, placed):
    vmem = pl.BlockSpec(memory_space=pltpu.VMEM)
    return pl.pallas_call(
        place_kernel,
        out_shape=jax.ShapeDtypeStruct(placed.shape, placed.dtype),
        in_specs=[pl.BlockSpec(memory_space=pltpu.SMEM)] * 2
        + [vmem] * len(sources)
        + [pl.BlockSpec(memory_space=pl.ANY)],
        out_specs=pl.BlockSpec(memory_space=pl.ANY),
        scratch_shapes=[pltpu.SemaphoreType.DMA((len(sources),))],
        input_output_aliases={2 + len(sources): 0},
        cost_estimate=SMALL,
        compiler_params=pltpu.CompilerParams(vmem_limit_bytes=4 * 1024 * 1024),
        name="place",
    )(*scalars, *sources, placed)


def dispatch_kernel(experts, block_ref, routes_ref, gate_ref, tokens_ref, *out_refs):
    block = block_ref[0]
    routes = routes_ref[...]
    gates = gate_ref[...]
    rows = routes.shape[0]
    down = lax.broadcasted_iota(jnp.int32, (rows, rows), 0)
    across = lax.broadcasted_iota(jnp.int32, (rows, rows), 1)
    same = (down == across).astype(jnp.float32)
    slots = experts * CAP
    slot_row = lax.broadcasted_iota(jnp.int32, (slots, rows), 0)
    slot_column = lax.broadcasted_iota(jnp.int32, (rows, slots), 1)
    placing = jnp.zeros((slots, rows), jnp.float32)
    share = jnp.zeros((rows, slots), jnp.float32)
    for k in range(experts):
        expert = lax.rem(block + k, experts)
        hit = routes == expert
        has = jnp.sum(hit.astype(jnp.float32), axis=1, keepdims=True)
        weight = jnp.sum(jnp.where(hit, gates, 0.0), axis=1, keepdims=True)
        has_row = jnp.sum(has * same, axis=0, keepdims=True)
        before_row = jnp.sum(jnp.where(down < across, has, 0.0), axis=0, keepdims=True)
        before = jnp.sum(jnp.where(across < down, has_row, 0.0), axis=1, keepdims=True)
        for c in range(CAP):
            slot = k * CAP + c
            placing += jnp.where((slot_row == slot) & (before_row == c), has_row, 0.0)
            share += jnp.where((slot_column == slot) & (before == c), weight, 0.0)
    for k in range(experts):
        out_refs[k][...] = jnp.dot(
            placing[k * CAP : (k + 1) * CAP].astype(jnp.bfloat16),
            tokens_ref[...],
            preferred_element_type=jnp.float32,
        ).astype(jnp.bfloat16)
    out_refs[experts][...] = share


def dispatch(block, routes, gates, tokens, experts):
    slots = experts * CAP
    return pl.pallas_call(
        functools.partial(dispatch_kernel, experts),
        out_shape=(
            *(jax.ShapeDtypeStruct((CAP, tokens.shape[1]), tokens.dtype) for _ in range(experts)),
            jax.ShapeDtypeStruct((tokens.shape[0], slots), jnp.float32),
        ),
        in_specs=[pl.BlockSpec(memory_space=pltpu.SMEM)]
        + [pl.BlockSpec(memory_space=pltpu.VMEM)] * 3,
        out_specs=(pl.BlockSpec(memory_space=pltpu.VMEM),) * (experts + 1),
        cost_estimate=SMALL,
        compiler_params=pltpu.CompilerParams(vmem_limit_bytes=8 * 1024 * 1024),
        name="dispatch",
    )(block, routes, gates, tokens)


def moved_rows(pieces, places, rows):
    total = None
    for piece, places_of_piece in zip(pieces, places):
        shape = (rows, piece.shape[0])
        row = lax.broadcasted_iota(jnp.int32, shape, 0)
        column = lax.broadcasted_iota(jnp.int32, shape, 1)
        chosen = jnp.zeros(shape, jnp.float32)
        for source, there in places_of_piece:
            chosen += ((row == there) & (column == source)).astype(jnp.float32)
        part = jnp.dot(
            chosen.astype(jnp.bfloat16), piece[...], preferred_element_type=jnp.float32
        )
        total = part if total is None else total + part
    return total.astype(jnp.bfloat16)


def stack_kernel(*refs):
    arrays, out_ref = refs[:-1], refs[-1]
    places, start = [], 0
    for array in arrays:
        places.append([(r, start + r) for r in range(array.shape[0])])
        start += array.shape[0]
    out_ref[...] = moved_rows(arrays, places, start)


def stack_rows(*arrays):
    rows = sum(array.shape[0] for array in arrays)
    return pl.pallas_call(
        stack_kernel,
        out_shape=jax.ShapeDtypeStruct((rows, arrays[0].shape[1]), arrays[0].dtype),
        in_specs=[pl.BlockSpec(memory_space=pltpu.VMEM)] * len(arrays),
        out_specs=pl.BlockSpec(memory_space=pltpu.VMEM),
        cost_estimate=SMALL,
        compiler_params=pltpu.CompilerParams(vmem_limit_bytes=8 * 1024 * 1024),
        name="stack_rows",
    )(*arrays)


def experts_kernel(count, *refs):
    row_refs, (gate_hbm, up_hbm, down_hbm) = refs[:count], refs[count : count + 3]
    out_refs = refs[count + 3 : 2 * count + 3]
    gate_ref, up_ref, down_ref, sems = refs[2 * count + 3 :]
    copies = [
        pltpu.make_async_copy(source.at[0], there, sems.at[i])
        for i, (source, there) in enumerate(
            ((gate_hbm, gate_ref), (up_hbm, up_ref), (down_hbm, down_ref))
        )
    ]
    for copy in copies:
        copy.start()
    rows = jnp.concatenate([ref[...].astype(jnp.float32) for ref in row_refs], axis=0)
    rows = rows.astype(jnp.bfloat16)
    copies[0].wait()
    gate = jnp.dot(rows, gate_ref[...], preferred_element_type=jnp.float32)
    copies[1].wait()
    lifted = jnp.dot(rows, up_ref[...], preferred_element_type=jnp.float32)
    hidden = (gate / (1.0 + jnp.exp(-gate)) * lifted).astype(jnp.bfloat16)
    copies[2].wait()
    parts = jnp.dot(hidden, down_ref[...], preferred_element_type=jnp.float32)
    for i, (row_ref, out_ref) in enumerate(zip(row_refs, out_refs)):
        size = row_ref.shape[0]
        out_ref[...] = parts[i * size : (i + 1) * size].astype(out_ref.dtype)


def run_experts(groups, w_gate, w_up, w_down):
    count = len(groups)
    vmem = pl.BlockSpec(memory_space=pltpu.VMEM)
    return pl.pallas_call(
        functools.partial(experts_kernel, count),
        out_shape=tuple(
            jax.ShapeDtypeStruct(x.shape, jnp.bfloat16 if i else jnp.float32)
            for i, x in enumerate(groups)
        ),
        in_specs=[vmem] * count + [pl.BlockSpec(memory_space=pltpu.HBM)] * 3,
        out_specs=(vmem,) * count,
        scratch_shapes=[
            pltpu.VMEM(w_gate.shape[1:], w_gate.dtype),
            pltpu.VMEM(w_up.shape[1:], w_up.dtype),
            pltpu.VMEM(w_down.shape[1:], w_down.dtype),
            pltpu.SemaphoreType.DMA((3,)),
        ],
        cost_estimate=SMALL,
        compiler_params=pltpu.CompilerParams(vmem_limit_bytes=16 * 1024 * 1024),
        name="experts",
    )(*groups, w_gate, w_up, w_down)


def on_device(
    latent_cache,
    rope_cache,
    q_latent,
    q_rope,
    new_latent,
    new_rope,
    branch_slot,
    moe_input,
    routes,
    route_gate,
    w_gate,
    w_up,
    w_down,
):
    tok_rows, step_count, head_count, width = q_latent.shape
    rope_width = new_rope.shape[-1]
    line = tok_rows // 2
    q_rows = step_count * head_count
    half = latent_cache.shape[1]
    rope_rows = rope_cache.shape[1]
    branch = lax.axis_index("branch")
    own = branch % tok_rows
    low = own % 2
    high = own // 2
    middle = jnp.logical_and(high > 0, high < line - 1)

    outer = [(i, i ^ 1) for i in range(line)]
    inner = [(i, i + 1) for i in range(1, line - 1, 2)]
    inner = inner + [(j, i) for i, j in inner]
    outward = [(i, i ^ 1) for i in range(1, line - 1)]
    own_cache = pack_cache(latent_cache[0], rope_cache[0])
    cache_a = line_hop(own_cache, tok_rows, outer)
    first_b = line_hop(own_cache, tok_rows, inner)
    first_c = line_hop(own_cache, tok_rows, [(i ^ 1, j) for i, j in inner])

    q_lat = q_latent.reshape(tok_rows, q_rows, width)
    rope_raw = q_rope.reshape(tok_rows, q_rows * rope_width // width, width)
    fresh = jnp.concatenate(
        [
            jnp.pad(new_latent, ((0, 0), (0, PAD - step_count), (0, 0))),
            jnp.pad(new_rope, ((0, 0), (0, PAD - step_count), (0, width - rope_width))),
        ],
        axis=1,
    )
    scalars = (branch_slot, own[None])
    sources = (q_lat, rope_raw, fresh)
    leave = pack_tokens(1, branch_slot, after(own[None], own_cache), *sources)
    guest = swapped(leave, "branch", 0)
    stay = pack_tokens(0, branch_slot, after(own[None], leave), *sources)
    attend = build_attend(head_count, step_count, width, half, rope_rows, 32, half // 2)
    model_width = moe_input.shape[-1]
    tok_total = tok_rows * step_count
    device = branch * lax.axis_size("expert") + lax.axis_index("expert")
    experts = lax.axis_size("branch") * lax.axis_size("expert") // SHARDS
    cores = lax.axis_size("expert")
    shard_branches = SHARDS // cores
    block = device // SHARDS
    *outgoing, share = dispatch(
        after(block[None], leave),
        routes.reshape(tok_total, -1),
        route_gate.reshape(tok_total, -1),
        moe_input.reshape(tok_total, model_width),
        experts,
    )

    around = shard_branches // 2

    def along(x, shift, flip):
        count = lax.axis_size("branch")
        there = [
            ((i // shard_branches + shift) % experts) * shard_branches
            + ((i % shard_branches) ^ (flip * 2))
            for i in range(count)
        ]
        return lax.ppermute(x, "branch", list(enumerate(there)))

    ways = [(k, m) for m in range(around) for k in range(experts)]
    pieces = outgoing[:1] + [along(outgoing[k], k, 0) for k in range(1, experts)]
    second_b = line_hop(first_b, tok_rows, outward)
    cache_a, stay, *pieces = lax.optimization_barrier((cache_a, stay, *pieces))

    def both_halves(cache):
        return cache, swapped(cache, "expert", 0)

    guest = after(guest, cache_a, first_b)
    given_0, placed = attend(scalars, 0, guest, stay, both_halves(own_cache), None)
    back_0 = swapped(given_0, "branch", 0)
    rows = stack_rows(*lax.optimization_barrier((given_0, *pieces))[1:])
    rows = [rows] + [along(rows, 0, m) for m in range(1, around)]
    given_1, placed = attend(scalars, 1, guest, stay, both_halves(cache_a), placed)
    back_1 = swapped(given_1, "branch", 0)

    first_c, given_1, back_0, first_b, *rows = lax.optimization_barrier(
        (first_c, given_1, back_0, first_b, *rows)
    )
    second_c = line_hop(first_c, tok_rows, outward)
    cache_b = jnp.where(middle, first_b, second_b)
    given_2, placed = attend(scalars, 2, guest, stay, both_halves(cache_b), placed)
    back_2 = swapped(given_2, "branch", 0)
    rows = stack_rows(*rows)

    def around_chip(x, i):
        pairs = []
        for there in range(lax.axis_size("branch") * cores):
            row, core = there // cores, there % cores
            pairs.append((there, (row ^ (i & 1)) * cores + (core ^ (i >> 1))))
        return lax.ppermute(x, ("branch", "expert"), pairs)

    groups = [rows] + [around_chip(rows, i) for i in range(1, 2 * cores)]
    groups = lax.optimization_barrier((given_2, *groups))[1:]
    parts, *others = run_experts(groups, w_gate, w_up, w_down)
    others = [around_chip(x, i + 1) for i, x in enumerate(others)]

    second_c, back_1, parts, *others = lax.optimization_barrier(
        (second_c, back_1, parts, *others)
    )
    for other in others:
        parts = parts + other.astype(jnp.float32)
    cache_c = both_halves(jnp.where(middle, first_c, second_c))
    homeward = [
        parts[w * CAP : (w + 1) * CAP].astype(jnp.float32 if way == (0, 0) else jnp.bfloat16)
        for w, way in enumerate(ways)
    ]
    homeward = [
        piece if (k, m) == (0, 0) else along(piece, -k, m)
        for (k, m), piece in zip(ways, homeward)
    ]
    guest, back_2 = lax.optimization_barrier((guest, back_2))
    (given_3,) = attend(scalars, 3, guest, None, cache_c, None)
    back_3 = swapped(given_3, "branch", 0)
    (placed,) = attend(scalars, 3, None, after(stay, given_3), cache_c, placed)
    homeward = [after(x, given_3).astype(jnp.float32) for x in homeward]
    placed = place(scalars, (back_0, back_1, back_2, back_3), placed)
    attended = placed.reshape(tok_rows, step_count, head_count, width)

    sums = [0.0] * experts
    for (k, _), piece in zip(ways, homeward):
        sums[k] = sums[k] + piece
    sums = jnp.concatenate(sums, axis=0)
    combined = jnp.sum(share[:, :, None] * sums[None, :, :], axis=1)
    moe_out = combined.astype(jnp.bfloat16).reshape(tok_rows, step_count, model_width)
    return (attended, moe_out)


def solution(mesh):
    return jax.shard_map(
        on_device,
        mesh=mesh,
        in_specs=(
            P(("group", "branch"), "expert", None),
            P(("group", "branch"), "expert", None),
            P(("group", "branch", "expert"), None, None, None),
            P(("group", "branch", "expert"), None, None),
            P(("group", "branch", "expert"), None, None),
            P(("group", "branch", "expert"), None, None),
            P(("group", "branch", "expert")),
            P(("group", "branch", "expert"), None, None),
            P(("group", "branch", "expert"), None, None),
            P(("group", "branch", "expert"), None, None),
            P(("branch", "expert"), None, None),
            P(("branch", "expert"), None, None),
            P(("branch", "expert"), None, None),
        ),
        out_specs=(
            P(("group", "branch", "expert"), None, None, None),
            P(("group", "branch", "expert"), None, None),
        ),
        check_vma=False,
    )
```

```python
import functools

import jax
import jax.numpy as jnp
from jax import lax
from jax.experimental import pallas as pl
from jax.experimental.pallas import tpu as pltpu
from jax.sharding import PartitionSpec as P

SHARDS = 8
CAP = 2
LANES = 128
PAD = 16

SMALL = pl.CostEstimate(flops=0, bytes_accessed=1024, transcendentals=0)

LARGE = 62 * 1024 * 1024

softmax_scale = 192.0 ** (-0.5)
log2e = 1.4426950408889634


def after(x, *earlier):
    return lax.optimization_barrier((x, *earlier))[0]


def swapped(x, axis, bit):
    return lax.ppermute(x, axis, [(i, i ^ 1 << bit) for i in range(lax.axis_size(axis))])


def line_hop(x, block, moves):
    pairs = []
    for base in range(0, lax.axis_size("branch"), block):
        for low in range(2):
            pairs += [(base + 2 * i + low, base + 2 * j + low) for i, j in moves]
    return lax.ppermute(x, "branch", pairs)


def pack_cache_kernel(lat_ref, rope_ref, out_ref, sems):
    rows = lat_ref.shape[0]
    copies = [
        pltpu.make_async_copy(lat_ref, out_ref.at[pl.ds(0, rows)], sems.at[0]),
        pltpu.make_async_copy(rope_ref, out_ref.at[pl.ds(rows, rope_ref.shape[0])], sems.at[1]),
    ]
    for copy in copies:
        copy.start()
    for copy in copies:
        copy.wait()


def pack_cache(lat, rope):
    return pl.pallas_call(
        pack_cache_kernel,
        out_shape=jax.ShapeDtypeStruct((lat.shape[0] + rope.shape[0], lat.shape[1]), lat.dtype),
        in_specs=[pl.BlockSpec(memory_space=pltpu.HBM)] * 2,
        out_specs=pl.BlockSpec(memory_space=pltpu.VMEM),
        scratch_shapes=[pltpu.SemaphoreType.DMA((2,))],
        cost_estimate=SMALL,
        compiler_params=pltpu.CompilerParams(vmem_limit_bytes=LARGE),
        name="pack_cache",
    )(lat, rope)


def row_for(slot, parity, slot_ref, own_ref):
    count = slot_ref.shape[0]
    line = count // 2
    own = own_ref[0]
    high = lax.div(own, 2)
    low = lax.rem(own, 2)
    mine = high
    pair = high + 1 - 2 * lax.rem(high, 2)
    first_half = high < line // 2
    nearer = jnp.where(first_half, line // 2, line // 2 - 1)
    farther = jnp.where(first_half, line - 1, 0)
    position = mine
    for number, place_there in ((1, pair), (2, nearer), (3, farther)):
        position = jnp.where(slot == number, place_there, position)
    wanted = 2 * position + (low if parity == 0 else 1 - low)
    row = jnp.int32(0)
    for r in range(1, count):
        row = row + jnp.where(slot_ref[r] == wanted, r, 0)
    return row


def pack_tokens_kernel(parity, slot_ref, own_ref, q_ref, rope_ref, new_ref, out_ref, sems):
    copies = []
    for slot in range(out_ref.shape[0]):
        row = row_for(slot, parity, slot_ref, own_ref)
        start = 0
        for part, source in enumerate((q_ref, rope_ref, new_ref)):
            count = source.shape[1]
            copy = pltpu.make_async_copy(
                source.at[row], out_ref.at[slot, pl.ds(start, count)], sems.at[slot, part]
            )
            copy.start()
            copies.append(copy)
            start += count
    for copy in copies:
        copy.wait()


def pack_tokens(parity, branch_slot, own, q_lat, q_rope, new):
    slots = branch_slot.shape[0] // 2
    sources = (q_lat, q_rope, new)
    rows = sum(x.shape[1] for x in sources)
    return pl.pallas_call(
        functools.partial(pack_tokens_kernel, parity),
        out_shape=jax.ShapeDtypeStruct((slots, rows, q_lat.shape[2]), q_lat.dtype),
        in_specs=[pl.BlockSpec(memory_space=pltpu.SMEM)] * 2
        + [pl.BlockSpec(memory_space=pl.ANY)] * 3,
        out_specs=pl.BlockSpec(memory_space=pltpu.VMEM),
        scratch_shapes=[pltpu.SemaphoreType.DMA((slots, 3))],
        cost_estimate=SMALL,
        compiler_params=pltpu.CompilerParams(vmem_limit_bytes=4 * 1024 * 1024),
        name="pack_tokens",
    )(branch_slot, own, *sources)


def spread_matrix(raw_rows, width):
    per_row = width // (LANES // 2)
    blocks = width // LANES
    shape = (raw_rows * per_row, raw_rows * blocks)
    row = lax.broadcasted_iota(jnp.int32, shape, 0)
    column = lax.broadcasted_iota(jnp.int32, shape, 1)
    wanted = ((row % per_row) // 2) * raw_rows + row // per_row
    return (column == wanted).astype(jnp.bfloat16)


def spread(matrix, raw):
    blocks = raw.shape[1] // LANES
    stacked = jnp.concatenate(
        [raw[:, b * LANES : (b + 1) * LANES] for b in range(blocks)], axis=0
    )
    rows = jnp.dot(matrix, stacked, preferred_element_type=jnp.float32)
    row = lax.broadcasted_iota(jnp.int32, rows.shape, 0)
    lane = lax.broadcasted_iota(jnp.int32, rows.shape, 1)
    return jnp.where(row % 2 == lane // (LANES // 2), rows, 0.0)


def build_attend(heads, steps, width, half, rope_rows, raw_group, chunk):
    q_rows = heads * steps
    token_rope = q_rows // 8

    factor = softmax_scale * log2e
    contract = (((1,), (1,)), ((), ()))

    def put_query_rope(rope_queries, number, raw_rope, matrix):
        grown = raw_group * width // (LANES // 2)
        for i, start in enumerate(range(0, token_rope, raw_group)):
            part = spread(matrix, raw_rope[start : start + raw_group, :])
            part = part + pltpu.roll(part, LANES // 2, 1)
            row = number * q_rows + i * grown
            rope_queries[row : row + grown, :] = part.astype(jnp.bfloat16)

    def merge_own(query, rope_query, fresh_all, peak, total, summed):
        fresh = fresh_all[0:PAD, :]
        fresh_rope = fresh_all[PAD : 2 * PAD, 0:LANES]
        own = lax.dot_general(
            query, fresh, contract, preferred_element_type=jnp.float32
        )
        own = own + lax.dot_general(
            rope_query, fresh_rope, contract, preferred_element_type=jnp.float32
        )
        row_step = lax.broadcasted_iota(jnp.int32, (q_rows, 1), 0) // heads
        columns = [jnp.where(row_step >= j, own[:, j : j + 1], -1e30) for j in range(steps)]
        top = peak
        for column in columns:
            top = jnp.maximum(top, column)
        share = jnp.exp2((peak - top) * factor)
        parts = [
            jnp.where(row_step >= j, jnp.exp2((column - top) * factor), 0.0)
            for j, column in enumerate(columns)
        ]
        denominator = total * share
        for part in parts:
            denominator = denominator + part
        inverse = 1.0 / denominator
        fresh32 = fresh.astype(jnp.float32)
        value = summed * (share * inverse)
        for j, part in enumerate(parts):
            value = value + (part * inverse) * fresh32[j : j + 1, :]
        return value.astype(jnp.bfloat16)

    def put_key_rope(rope_keys, first, raw_rope, matrix):
        grown = raw_group * width // (LANES // 2)
        for i, start in enumerate(range(0, rope_rows, raw_group)):
            part = spread(matrix, raw_rope[start : start + raw_group, :])
            row = first + i * grown
            rope_keys[row : row + grown, :] = part.astype(jnp.bfloat16)

    def kernel(slot, gives, keeps, has_placed, slot_ref, own_ref, *refs):
        refs = list(refs)
        tokens = [refs.pop(0).at[slot] for _ in range(gives + keeps)]
        own_half, other_half = refs.pop(0), refs.pop(0)
        if has_placed:
            refs.pop(0)
        give = refs.pop(0) if gives else None
        placed = refs.pop(0) if keeps else None
        rope_keys, query_rope, scores, summed, result, sem = refs
        matrix = spread_matrix(raw_group, width)
        middle = q_rows + token_rope
        for number, token in enumerate(tokens):
            put_query_rope(query_rope, number, token.at[pl.ds(q_rows, token_rope)], matrix)
        peak = None
        for i, cache in enumerate((own_half, other_half)):
            put_key_rope(rope_keys, 0, cache.at[pl.ds(half, rope_rows)], matrix)
            for first in range(0, half, chunk):
                highs = []
                for number, token in enumerate(tokens):
                    rows = slice(number * q_rows, (number + 1) * q_rows)
                    part = lax.dot_general(
                        token[0:q_rows, :],
                        cache[first : first + chunk, :],
                        contract,
                        preferred_element_type=jnp.float32,
                    )
                    part = part + lax.dot_general(
                        query_rope[rows, :],
                        rope_keys[first : first + chunk, :],
                        contract,
                        preferred_element_type=jnp.float32,
                    )
                    scores[rows, i * half + first : i * half + first + chunk] = part
                    highs.append(jnp.max(part, axis=1, keepdims=True))
                high = jnp.concatenate(highs, axis=0) if len(highs) > 1 else highs[0]
                peak = high if peak is None else jnp.maximum(peak, high)
        scaled = peak * factor
        total = None
        for first in range(0, 2 * half, chunk):
            cache = own_half if first < half else other_half
            weights = jnp.exp2(scores[:, first : first + chunk] * factor - scaled)
            part = jnp.sum(weights, axis=1, keepdims=True)
            value = jnp.dot(
                weights.astype(jnp.bfloat16),
                cache[first % half : first % half + chunk, :],
                preferred_element_type=jnp.float32,
            )
            if first == 0:
                total = part
                summed[...] = value
            else:
                total = total + part
                summed[...] += value
        for number, token in enumerate(tokens):
            rows = slice(number * q_rows, (number + 1) * q_rows)
            value = merge_own(
                token[0:q_rows, :],
                query_rope[rows, :],
                token[middle : middle + 2 * PAD, :],
                peak[rows],
                total[rows],
                summed[rows, :],
            )
            if number < gives:
                give[...] = value
            else:
                result[...] = value
        if keeps:
            row = row_for(slot, 0, slot_ref, own_ref)
            copy = pltpu.make_async_copy(result, placed.at[row], sem)
            copy.start()
            copy.wait()

    def call(scalars, slot, guest, stay, caches, placed):
        count = scalars[0].shape[0]
        vmem = pl.BlockSpec(memory_space=pltpu.VMEM)
        anywhere = pl.BlockSpec(memory_space=pl.ANY)
        gives, keeps = int(guest is not None), int(stay is not None)
        n_tok = gives + keeps
        caches = [pltpu.with_memory_space_constraint(x, pltpu.VMEM) for x in caches]
        operands = [x for x in (guest, stay) if x is not None] + [*caches]
        in_specs = [pl.BlockSpec(memory_space=pltpu.SMEM)] * 2 + [vmem] * len(operands)
        operands = [*scalars, *operands]
        out_shape, out_specs, alias = [], [], {}
        if gives:
            out_shape.append(jax.ShapeDtypeStruct((q_rows, width), jnp.bfloat16))
            out_specs.append(vmem)
        if keeps:
            out_shape.append(jax.ShapeDtypeStruct((count, q_rows, width), jnp.bfloat16))
            out_specs.append(anywhere)
        has_placed = bool(keeps and placed is not None)
        if has_placed:
            alias = {len(operands): gives}
            in_specs.append(anywhere)
            operands.append(placed)
        return pl.pallas_call(
            functools.partial(kernel, slot, gives, keeps, has_placed),
            out_shape=tuple(out_shape),
            in_specs=in_specs,
            out_specs=tuple(out_specs),
            scratch_shapes=[
                pltpu.VMEM((half, LANES), jnp.bfloat16),
                pltpu.VMEM((n_tok * q_rows, LANES), jnp.bfloat16),
                pltpu.VMEM((n_tok * q_rows, 2 * half), jnp.float32),
                pltpu.VMEM((n_tok * q_rows, width), jnp.float32),
                pltpu.VMEM((q_rows, width), jnp.bfloat16),
                pltpu.SemaphoreType.DMA,
            ],
            input_output_aliases=alias,
            cost_estimate=SMALL,
            compiler_params=pltpu.CompilerParams(vmem_limit_bytes=16 * 1024 * 1024),
            name="attend",
        )(*operands)

    return call


def place_kernel(slots, slot_ref, own_ref, *refs):
    sources, (before, placed_ref, sems) = refs[:-3], refs[-3:]
    copies = []
    for i, (slot, source) in enumerate(zip(slots, sources)):
        row = row_for(slot, 1, slot_ref, own_ref)
        copies.append(pltpu.make_async_copy(source, placed_ref.at[row], sems.at[i]))
    for copy in copies:
        copy.start()
    for copy in copies:
        copy.wait()


def place(scalars, slots, sources, placed):
    vmem = pl.BlockSpec(memory_space=pltpu.VMEM)
    return pl.pallas_call(
        functools.partial(place_kernel, slots),
        out_shape=jax.ShapeDtypeStruct(placed.shape, placed.dtype),
        in_specs=[pl.BlockSpec(memory_space=pltpu.SMEM)] * 2
        + [vmem] * len(sources)
        + [pl.BlockSpec(memory_space=pl.ANY)],
        out_specs=pl.BlockSpec(memory_space=pl.ANY),
        scratch_shapes=[pltpu.SemaphoreType.DMA((len(sources),))],
        input_output_aliases={2 + len(sources): 0},
        cost_estimate=SMALL,
        compiler_params=pltpu.CompilerParams(vmem_limit_bytes=4 * 1024 * 1024),
        name="place",
    )(*scalars, *sources, placed)


def dispatch_kernel(experts, block_ref, routes_ref, gate_ref, tokens_ref, *out_refs):
    block = block_ref[0]
    routes = routes_ref[...]
    gates = gate_ref[...]
    rows = routes.shape[0]
    down = lax.broadcasted_iota(jnp.int32, (rows, rows), 0)
    across = lax.broadcasted_iota(jnp.int32, (rows, rows), 1)
    same = (down == across).astype(jnp.float32)
    slots = experts * CAP
    slot_row = lax.broadcasted_iota(jnp.int32, (slots, rows), 0)
    slot_column = lax.broadcasted_iota(jnp.int32, (rows, slots), 1)
    placing = jnp.zeros((slots, rows), jnp.float32)
    share = jnp.zeros((rows, slots), jnp.float32)
    for k in range(experts):
        expert = lax.rem(block + k, experts)
        hit = routes == expert
        has = jnp.sum(hit.astype(jnp.float32), axis=1, keepdims=True)
        weight = jnp.sum(jnp.where(hit, gates, 0.0), axis=1, keepdims=True)
        has_row = jnp.sum(has * same, axis=0, keepdims=True)
        before_row = jnp.sum(jnp.where(down < across, has, 0.0), axis=0, keepdims=True)
        before = jnp.sum(jnp.where(across < down, has_row, 0.0), axis=1, keepdims=True)
        for c in range(CAP):
            slot = k * CAP + c
            placing += jnp.where((slot_row == slot) & (before_row == c), has_row, 0.0)
            share += jnp.where((slot_column == slot) & (before == c), weight, 0.0)
    for k in range(experts):
        out_refs[k][...] = jnp.dot(
            placing[k * CAP : (k + 1) * CAP].astype(jnp.bfloat16),
            tokens_ref[...],
            preferred_element_type=jnp.float32,
        ).astype(jnp.bfloat16)
    out_refs[experts][...] = share


def dispatch(block, routes, gates, tokens, experts):
    slots = experts * CAP
    return pl.pallas_call(
        functools.partial(dispatch_kernel, experts),
        out_shape=(
            *(jax.ShapeDtypeStruct((CAP, tokens.shape[1]), tokens.dtype) for _ in range(experts)),
            jax.ShapeDtypeStruct((tokens.shape[0], slots), jnp.float32),
        ),
        in_specs=[pl.BlockSpec(memory_space=pltpu.SMEM)]
        + [pl.BlockSpec(memory_space=pltpu.VMEM)] * 3,
        out_specs=(pl.BlockSpec(memory_space=pltpu.VMEM),) * (experts + 1),
        cost_estimate=SMALL,
        compiler_params=pltpu.CompilerParams(vmem_limit_bytes=8 * 1024 * 1024),
        name="dispatch",
    )(block, routes, gates, tokens)


def moved_rows(pieces, places, rows):
    total = None
    for piece, places_of_piece in zip(pieces, places):
        shape = (rows, piece.shape[0])
        row = lax.broadcasted_iota(jnp.int32, shape, 0)
        column = lax.broadcasted_iota(jnp.int32, shape, 1)
        chosen = jnp.zeros(shape, jnp.float32)
        for source, there in places_of_piece:
            chosen += ((row == there) & (column == source)).astype(jnp.float32)
        part = jnp.dot(
            chosen.astype(jnp.bfloat16), piece[...], preferred_element_type=jnp.float32
        )
        total = part if total is None else total + part
    return total.astype(jnp.bfloat16)


def stack_kernel(*refs):
    arrays, out_ref = refs[:-1], refs[-1]
    places, start = [], 0
    for array in arrays:
        places.append([(r, start + r) for r in range(array.shape[0])])
        start += array.shape[0]
    out_ref[...] = moved_rows(arrays, places, start)


def stack_rows(*arrays):
    rows = sum(array.shape[0] for array in arrays)
    return pl.pallas_call(
        stack_kernel,
        out_shape=jax.ShapeDtypeStruct((rows, arrays[0].shape[1]), arrays[0].dtype),
        in_specs=[pl.BlockSpec(memory_space=pltpu.VMEM)] * len(arrays),
        out_specs=pl.BlockSpec(memory_space=pltpu.VMEM),
        cost_estimate=SMALL,
        compiler_params=pltpu.CompilerParams(vmem_limit_bytes=8 * 1024 * 1024),
        name="stack_rows",
    )(*arrays)


def experts_kernel(count, *refs):
    row_refs, (gate_hbm, up_hbm, down_hbm) = refs[:count], refs[count : count + 3]
    out_refs = refs[count + 3 : 2 * count + 3]
    gate_ref, up_ref, down_ref, sems = refs[2 * count + 3 :]
    copies = [
        pltpu.make_async_copy(source.at[0], there, sems.at[i])
        for i, (source, there) in enumerate(
            ((gate_hbm, gate_ref), (up_hbm, up_ref), (down_hbm, down_ref))
        )
    ]
    for copy in copies:
        copy.start()
    rows = jnp.concatenate([ref[...].astype(jnp.float32) for ref in row_refs], axis=0)
    rows = rows.astype(jnp.bfloat16)
    copies[0].wait()
    gate = jnp.dot(rows, gate_ref[...], preferred_element_type=jnp.float32)
    copies[1].wait()
    lifted = jnp.dot(rows, up_ref[...], preferred_element_type=jnp.float32)
    hidden = (gate / (1.0 + jnp.exp(-gate)) * lifted).astype(jnp.bfloat16)
    copies[2].wait()
    parts = jnp.dot(hidden, down_ref[...], preferred_element_type=jnp.float32)
    for i, (row_ref, out_ref) in enumerate(zip(row_refs, out_refs)):
        size = row_ref.shape[0]
        out_ref[...] = parts[i * size : (i + 1) * size].astype(out_ref.dtype)


def run_experts(groups, w_gate, w_up, w_down):
    count = len(groups)
    vmem = pl.BlockSpec(memory_space=pltpu.VMEM)
    return pl.pallas_call(
        functools.partial(experts_kernel, count),
        out_shape=tuple(
            jax.ShapeDtypeStruct(x.shape, jnp.bfloat16 if i else jnp.float32)
            for i, x in enumerate(groups)
        ),
        in_specs=[vmem] * count + [pl.BlockSpec(memory_space=pltpu.HBM)] * 3,
        out_specs=(vmem,) * count,
        scratch_shapes=[
            pltpu.VMEM(w_gate.shape[1:], w_gate.dtype),
            pltpu.VMEM(w_up.shape[1:], w_up.dtype),
            pltpu.VMEM(w_down.shape[1:], w_down.dtype),
            pltpu.SemaphoreType.DMA((3,)),
        ],
        cost_estimate=SMALL,
        compiler_params=pltpu.CompilerParams(vmem_limit_bytes=16 * 1024 * 1024),
        name="experts",
    )(*groups, w_gate, w_up, w_down)


def on_device(
    latent_cache,
    rope_cache,
    q_latent,
    q_rope,
    new_latent,
    new_rope,
    branch_slot,
    moe_input,
    routes,
    route_gate,
    w_gate,
    w_up,
    w_down,
):
    tok_rows, step_count, head_count, width = q_latent.shape
    rope_width = new_rope.shape[-1]
    line = tok_rows // 2
    q_rows = step_count * head_count
    half = latent_cache.shape[1]
    rope_rows = rope_cache.shape[1]
    branch = lax.axis_index("branch")
    own = branch % tok_rows
    low = own % 2
    high = own // 2
    middle = jnp.logical_and(high > 0, high < line - 1)

    outer = [(i, i ^ 1) for i in range(line)]
    inner = [(i, i + 1) for i in range(1, line - 1, 2)]
    inner = inner + [(j, i) for i, j in inner]
    outward = [(i, i ^ 1) for i in range(1, line - 1)]
    own_cache = pack_cache(latent_cache[0], rope_cache[0])
    cache_a = line_hop(own_cache, tok_rows, outer)
    first_b = line_hop(own_cache, tok_rows, inner)

    q_lat = q_latent.reshape(tok_rows, q_rows, width)
    rope_raw = q_rope.reshape(tok_rows, q_rows * rope_width // width, width)
    fresh = jnp.concatenate(
        [
            jnp.pad(new_latent, ((0, 0), (0, PAD - step_count), (0, 0))),
            jnp.pad(new_rope, ((0, 0), (0, PAD - step_count), (0, width - rope_width))),
        ],
        axis=1,
    )
    scalars = (branch_slot, own[None])
    sources = (q_lat, rope_raw, fresh)
    leave = pack_tokens(1, branch_slot, after(own[None], own_cache), *sources)
    guest = swapped(leave, "branch", 0)
    stay = pack_tokens(0, branch_slot, after(own[None], leave), *sources)
    attend = build_attend(head_count, step_count, width, half, rope_rows, 32, half // 2)
    model_width = moe_input.shape[-1]
    tok_total = tok_rows * step_count
    device = branch * lax.axis_size("expert") + lax.axis_index("expert")
    experts = lax.axis_size("branch") * lax.axis_size("expert") // SHARDS
    cores = lax.axis_size("expert")
    shard_branches = SHARDS // cores
    block = device // SHARDS
    *outgoing, share = dispatch(
        after(block[None], leave),
        routes.reshape(tok_total, -1),
        route_gate.reshape(tok_total, -1),
        moe_input.reshape(tok_total, model_width),
        experts,
    )

    around = shard_branches // 2

    def along(x, shift, flip):
        count = lax.axis_size("branch")
        there = [
            ((i // shard_branches + shift) % experts) * shard_branches
            + ((i % shard_branches) ^ (flip * 2))
            for i in range(count)
        ]
        return lax.ppermute(x, "branch", list(enumerate(there)))

    ways = [(k, m) for m in range(around) for k in range(experts)]
    pieces = outgoing[:1] + [along(outgoing[k], k, 0) for k in range(1, experts)]
    cache_a, first_b, stay, *pieces = lax.optimization_barrier(
        (cache_a, first_b, stay, *pieces)
    )
    second_b = line_hop(first_b, tok_rows, outward)
    first_c = line_hop(cache_a, tok_rows, inner)

    def both_halves(cache):
        return cache, swapped(cache, "expert", 0)

    guest = after(guest, cache_a, first_b)
    given_0, placed = attend(scalars, 0, guest, stay, both_halves(own_cache), None)
    back_0 = swapped(given_0, "branch", 0)
    rows = stack_rows(*lax.optimization_barrier((given_0, *pieces))[1:])
    rows = [rows] + [along(rows, 0, m) for m in range(1, around)]
    given_1, placed = attend(scalars, 1, guest, stay, both_halves(cache_a), placed)
    back_1 = swapped(given_1, "branch", 0)

    first_c, given_1, back_0, first_b, *rows = lax.optimization_barrier(
        (first_c, given_1, back_0, first_b, *rows)
    )
    second_c = line_hop(first_c, tok_rows, outward)
    cache_b = jnp.where(middle, first_b, second_b)
    given_2, placed = attend(scalars, 2, guest, stay, both_halves(cache_b), placed)
    back_2 = swapped(given_2, "branch", 0)
    rows = stack_rows(*rows)

    def around_chip(x, i):
        pairs = []
        for there in range(lax.axis_size("branch") * cores):
            row, core = there // cores, there % cores
            pairs.append((there, (row ^ (i & 1)) * cores + (core ^ (i >> 1))))
        return lax.ppermute(x, ("branch", "expert"), pairs)

    groups = [rows] + [around_chip(rows, i) for i in range(1, 2 * cores)]
    groups = lax.optimization_barrier((given_2, *groups))[1:]
    parts, *others = run_experts(groups, w_gate, w_up, w_down)
    others = [around_chip(x, i + 1) for i, x in enumerate(others)]

    second_c, back_1, parts, *others = lax.optimization_barrier(
        (second_c, back_1, parts, *others)
    )
    for other in others:
        parts = parts + other.astype(jnp.float32)
    cache_c = both_halves(jnp.where(middle, first_c, second_c))
    homeward = [
        parts[w * CAP : (w + 1) * CAP].astype(jnp.float32 if way == (0, 0) else jnp.bfloat16)
        for w, way in enumerate(ways)
    ]
    homeward = [
        piece if (k, m) == (0, 0) else along(piece, -k, m)
        for (k, m), piece in zip(ways, homeward)
    ]
    guest, back_2 = lax.optimization_barrier((guest, back_2))
    placed = place(scalars, (0, 1, 2), (back_0, back_1, back_2), placed)
    (given_3,) = attend(scalars, 3, guest, None, cache_c, None)
    back_3 = swapped(given_3, "branch", 0)
    (placed,) = attend(scalars, 3, None, after(stay, given_3), cache_c, placed)
    homeward = [after(x, given_3).astype(jnp.float32) for x in homeward]
    placed = place(scalars, (3,), (back_3,), placed)
    attended = placed.reshape(tok_rows, step_count, head_count, width)

    sums = [0.0] * experts
    for (k, _), piece in zip(ways, homeward):
        sums[k] = sums[k] + piece
    sums = jnp.concatenate(sums, axis=0)
    combined = jnp.sum(share[:, :, None] * sums[None, :, :], axis=1)
    moe_out = combined.astype(jnp.bfloat16).reshape(tok_rows, step_count, model_width)
    return (attended, moe_out)


def solution(mesh):
    return jax.shard_map(
        on_device,
        mesh=mesh,
        in_specs=(
            P(("group", "branch"), "expert", None),
            P(("group", "branch"), "expert", None),
            P(("group", "branch", "expert"), None, None, None),
            P(("group", "branch", "expert"), None, None),
            P(("group", "branch", "expert"), None, None),
            P(("group", "branch", "expert"), None, None),
            P(("group", "branch", "expert")),
            P(("group", "branch", "expert"), None, None),
            P(("group", "branch", "expert"), None, None),
            P(("group", "branch", "expert"), None, None),
            P(("branch", "expert"), None, None),
            P(("branch", "expert"), None, None),
            P(("branch", "expert"), None, None),
        ),
        out_specs=(
            P(("group", "branch", "expert"), None, None, None),
            P(("group", "branch", "expert"), None, None),
        ),
        check_vma=False,
    )
```

```python
import functools

import jax
import jax.numpy as jnp
from jax import lax
from jax.experimental import pallas as pl
from jax.experimental.pallas import tpu as pltpu
from jax.sharding import PartitionSpec as P

SHARDS = 8
CAP = 2
LANES = 128
PAD = 16

SMALL = pl.CostEstimate(flops=0, bytes_accessed=1024, transcendentals=0)

LARGE = 62 * 1024 * 1024

softmax_scale = 192.0 ** (-0.5)
log2e = 1.4426950408889634


def after(x, *earlier):
    return lax.optimization_barrier((x, *earlier))[0]


def swapped(x, axis, bit):
    return lax.ppermute(x, axis, [(i, i ^ 1 << bit) for i in range(lax.axis_size(axis))])


def line_hop(x, block, moves):
    pairs = []
    for base in range(0, lax.axis_size("branch"), block):
        for low in range(2):
            pairs += [(base + 2 * i + low, base + 2 * j + low) for i, j in moves]
    return lax.ppermute(x, "branch", pairs)


def pack_cache_kernel(lat_ref, rope_ref, out_ref, sems):
    rows = lat_ref.shape[0]
    copies = [
        pltpu.make_async_copy(lat_ref, out_ref.at[pl.ds(0, rows)], sems.at[0]),
        pltpu.make_async_copy(rope_ref, out_ref.at[pl.ds(rows, rope_ref.shape[0])], sems.at[1]),
    ]
    for copy in copies:
        copy.start()
    for copy in copies:
        copy.wait()


def pack_cache(lat, rope):
    return pl.pallas_call(
        pack_cache_kernel,
        out_shape=jax.ShapeDtypeStruct((lat.shape[0] + rope.shape[0], lat.shape[1]), lat.dtype),
        in_specs=[pl.BlockSpec(memory_space=pltpu.HBM)] * 2,
        out_specs=pl.BlockSpec(memory_space=pltpu.VMEM),
        scratch_shapes=[pltpu.SemaphoreType.DMA((2,))],
        cost_estimate=SMALL,
        compiler_params=pltpu.CompilerParams(vmem_limit_bytes=LARGE),
        name="pack_cache",
    )(lat, rope)


def row_for(slot, parity, slot_ref, own_ref):
    count = slot_ref.shape[0]
    line = count // 2
    own = own_ref[0]
    high = lax.div(own, 2)
    low = lax.rem(own, 2)
    mine = high
    pair = high + 1 - 2 * lax.rem(high, 2)
    first_half = high < line // 2
    nearer = jnp.where(first_half, line // 2, line // 2 - 1)
    farther = jnp.where(first_half, line - 1, 0)
    position = mine
    for number, place_there in ((1, pair), (2, nearer), (3, farther)):
        position = jnp.where(slot == number, place_there, position)
    wanted = 2 * position + (low if parity == 0 else 1 - low)
    row = jnp.int32(0)
    for r in range(1, count):
        row = row + jnp.where(slot_ref[r] == wanted, r, 0)
    return row


def pack_tokens_kernel(parity, slot_ref, own_ref, q_ref, rope_ref, new_ref, out_ref, sems):
    copies = []
    for slot in range(out_ref.shape[0]):
        row = row_for(slot, parity, slot_ref, own_ref)
        start = 0
        for part, source in enumerate((q_ref, rope_ref, new_ref)):
            count = source.shape[1]
            copy = pltpu.make_async_copy(
                source.at[row], out_ref.at[slot, pl.ds(start, count)], sems.at[slot, part]
            )
            copy.start()
            copies.append(copy)
            start += count
    for copy in copies:
        copy.wait()


def pack_tokens(parity, branch_slot, own, q_lat, q_rope, new):
    slots = branch_slot.shape[0] // 2
    sources = (q_lat, q_rope, new)
    rows = sum(x.shape[1] for x in sources)
    return pl.pallas_call(
        functools.partial(pack_tokens_kernel, parity),
        out_shape=jax.ShapeDtypeStruct((slots, rows, q_lat.shape[2]), q_lat.dtype),
        in_specs=[pl.BlockSpec(memory_space=pltpu.SMEM)] * 2
        + [pl.BlockSpec(memory_space=pl.ANY)] * 3,
        out_specs=pl.BlockSpec(memory_space=pltpu.VMEM),
        scratch_shapes=[pltpu.SemaphoreType.DMA((slots, 3))],
        cost_estimate=SMALL,
        compiler_params=pltpu.CompilerParams(vmem_limit_bytes=4 * 1024 * 1024),
        name="pack_tokens",
    )(branch_slot, own, *sources)


def spread_matrix(raw_rows, width):
    per_row = width // (LANES // 2)
    blocks = width // LANES
    shape = (raw_rows * per_row, raw_rows * blocks)
    row = lax.broadcasted_iota(jnp.int32, shape, 0)
    column = lax.broadcasted_iota(jnp.int32, shape, 1)
    wanted = ((row % per_row) // 2) * raw_rows + row // per_row
    return (column == wanted).astype(jnp.bfloat16)


def spread(matrix, raw):
    blocks = raw.shape[1] // LANES
    stacked = jnp.concatenate(
        [raw[:, b * LANES : (b + 1) * LANES] for b in range(blocks)], axis=0
    )
    rows = jnp.dot(matrix, stacked, preferred_element_type=jnp.float32)
    row = lax.broadcasted_iota(jnp.int32, rows.shape, 0)
    lane = lax.broadcasted_iota(jnp.int32, rows.shape, 1)
    return jnp.where(row % 2 == lane // (LANES // 2), rows, 0.0)


def build_attend(heads, steps, width, half, rope_rows, raw_group, chunk):
    q_rows = heads * steps
    token_rope = q_rows // 8

    factor = softmax_scale * log2e
    contract = (((1,), (1,)), ((), ()))

    def put_query_rope(rope_queries, number, raw_rope, matrix):
        grown = raw_group * width // (LANES // 2)
        for i, start in enumerate(range(0, token_rope, raw_group)):
            part = spread(matrix, raw_rope[start : start + raw_group, :])
            part = part + pltpu.roll(part, LANES // 2, 1)
            row = number * q_rows + i * grown
            rope_queries[row : row + grown, :] = part.astype(jnp.bfloat16)

    def merge_own(query, rope_query, fresh_all, peak, total, summed):
        fresh = fresh_all[0:PAD, :]
        fresh_rope = fresh_all[PAD : 2 * PAD, 0:LANES]
        own = lax.dot_general(
            query, fresh, contract, preferred_element_type=jnp.float32
        )
        own = own + lax.dot_general(
            rope_query, fresh_rope, contract, preferred_element_type=jnp.float32
        )
        row_step = lax.broadcasted_iota(jnp.int32, (q_rows, 1), 0) // heads
        columns = [jnp.where(row_step >= j, own[:, j : j + 1], -1e30) for j in range(steps)]
        top = peak
        for column in columns:
            top = jnp.maximum(top, column)
        share = jnp.exp2((peak - top) * factor)
        parts = [
            jnp.where(row_step >= j, jnp.exp2((column - top) * factor), 0.0)
            for j, column in enumerate(columns)
        ]
        denominator = total * share
        for part in parts:
            denominator = denominator + part
        inverse = 1.0 / denominator
        fresh32 = fresh.astype(jnp.float32)
        value = summed * (share * inverse)
        for j, part in enumerate(parts):
            value = value + (part * inverse) * fresh32[j : j + 1, :]
        return value.astype(jnp.bfloat16)

    def put_key_rope(rope_keys, first, raw_rope, matrix):
        grown = raw_group * width // (LANES // 2)
        for i, start in enumerate(range(0, rope_rows, raw_group)):
            part = spread(matrix, raw_rope[start : start + raw_group, :])
            row = first + i * grown
            rope_keys[row : row + grown, :] = part.astype(jnp.bfloat16)

    def kernel(slot, gives, keeps, has_placed, slot_ref, own_ref, *refs):
        refs = list(refs)
        tokens = [refs.pop(0).at[slot] for _ in range(gives + keeps)]
        own_half, other_half = refs.pop(0), refs.pop(0)
        if has_placed:
            refs.pop(0)
        give = refs.pop(0) if gives else None
        placed = refs.pop(0) if keeps else None
        rope_keys, query_rope, scores, summed, result, sem = refs
        matrix = spread_matrix(raw_group, width)
        middle = q_rows + token_rope
        for number, token in enumerate(tokens):
            put_query_rope(query_rope, number, token.at[pl.ds(q_rows, token_rope)], matrix)
        peak = None
        for i, cache in enumerate((own_half, other_half)):
            put_key_rope(rope_keys, 0, cache.at[pl.ds(half, rope_rows)], matrix)
            for first in range(0, half, chunk):
                highs = []
                for number, token in enumerate(tokens):
                    rows = slice(number * q_rows, (number + 1) * q_rows)
                    part = lax.dot_general(
                        token[0:q_rows, :],
                        cache[first : first + chunk, :],
                        contract,
                        preferred_element_type=jnp.float32,
                    )
                    part = part + lax.dot_general(
                        query_rope[rows, :],
                        rope_keys[first : first + chunk, :],
                        contract,
                        preferred_element_type=jnp.float32,
                    )
                    scores[rows, i * half + first : i * half + first + chunk] = part
                    highs.append(jnp.max(part, axis=1, keepdims=True))
                high = jnp.concatenate(highs, axis=0) if len(highs) > 1 else highs[0]
                peak = high if peak is None else jnp.maximum(peak, high)
        scaled = peak * factor
        total = None
        for first in range(0, 2 * half, chunk):
            cache = own_half if first < half else other_half
            weights = jnp.exp2(scores[:, first : first + chunk] * factor - scaled)
            part = jnp.sum(weights, axis=1, keepdims=True)
            value = jnp.dot(
                weights.astype(jnp.bfloat16),
                cache[first % half : first % half + chunk, :],
                preferred_element_type=jnp.float32,
            )
            if first == 0:
                total = part
                summed[...] = value
            else:
                total = total + part
                summed[...] += value
        for number, token in enumerate(tokens):
            rows = slice(number * q_rows, (number + 1) * q_rows)
            value = merge_own(
                token[0:q_rows, :],
                query_rope[rows, :],
                token[middle : middle + 2 * PAD, :],
                peak[rows],
                total[rows],
                summed[rows, :],
            )
            if number < gives:
                give[...] = value
            else:
                result[...] = value
        if keeps:
            row = row_for(slot, 0, slot_ref, own_ref)
            copy = pltpu.make_async_copy(result, placed.at[row], sem)
            copy.start()
            copy.wait()

    def call(scalars, slot, guest, stay, caches, placed):
        count = scalars[0].shape[0]
        vmem = pl.BlockSpec(memory_space=pltpu.VMEM)
        anywhere = pl.BlockSpec(memory_space=pl.ANY)
        gives, keeps = int(guest is not None), int(stay is not None)
        n_tok = gives + keeps
        operands = [x for x in (guest, stay) if x is not None] + [*caches]
        in_specs = [pl.BlockSpec(memory_space=pltpu.SMEM)] * 2 + [vmem] * len(operands)
        operands = [*scalars, *operands]
        out_shape, out_specs, alias = [], [], {}
        if gives:
            out_shape.append(jax.ShapeDtypeStruct((q_rows, width), jnp.bfloat16))
            out_specs.append(vmem)
        if keeps:
            out_shape.append(jax.ShapeDtypeStruct((count, q_rows, width), jnp.bfloat16))
            out_specs.append(anywhere)
        has_placed = bool(keeps and placed is not None)
        if has_placed:
            alias = {len(operands): gives}
            in_specs.append(anywhere)
            operands.append(placed)
        return pl.pallas_call(
            functools.partial(kernel, slot, gives, keeps, has_placed),
            out_shape=tuple(out_shape),
            in_specs=in_specs,
            out_specs=tuple(out_specs),
            scratch_shapes=[
                pltpu.VMEM((half, LANES), jnp.bfloat16),
                pltpu.VMEM((n_tok * q_rows, LANES), jnp.bfloat16),
                pltpu.VMEM((n_tok * q_rows, 2 * half), jnp.float32),
                pltpu.VMEM((n_tok * q_rows, width), jnp.float32),
                pltpu.VMEM((q_rows, width), jnp.bfloat16),
                pltpu.SemaphoreType.DMA,
            ],
            input_output_aliases=alias,
            cost_estimate=SMALL,
            compiler_params=pltpu.CompilerParams(vmem_limit_bytes=16 * 1024 * 1024),
            name="attend",
        )(*operands)

    return call


def place_kernel(slot_ref, own_ref, *refs):
    sources, (before, placed_ref, sems) = refs[:-3], refs[-3:]
    copies = []
    for slot, source in enumerate(sources):
        row = row_for(slot, 1, slot_ref, own_ref)
        copies.append(pltpu.make_async_copy(source, placed_ref.at[row], sems.at[slot]))
    for copy in copies:
        copy.start()
    for copy in copies:
        copy.wait()


def place(scalars, sources, placed):
    vmem = pl.BlockSpec(memory_space=pltpu.VMEM)
    return pl.pallas_call(
        place_kernel,
        out_shape=jax.ShapeDtypeStruct(placed.shape, placed.dtype),
        in_specs=[pl.BlockSpec(memory_space=pltpu.SMEM)] * 2
        + [vmem] * len(sources)
        + [pl.BlockSpec(memory_space=pl.ANY)],
        out_specs=pl.BlockSpec(memory_space=pl.ANY),
        scratch_shapes=[pltpu.SemaphoreType.DMA((len(sources),))],
        input_output_aliases={2 + len(sources): 0},
        cost_estimate=SMALL,
        compiler_params=pltpu.CompilerParams(vmem_limit_bytes=4 * 1024 * 1024),
        name="place",
    )(*scalars, *sources, placed)


def dispatch_kernel(experts, block_ref, routes_ref, gate_ref, tokens_ref, *out_refs):
    block = block_ref[0]
    routes = routes_ref[...]
    gates = gate_ref[...]
    rows = routes.shape[0]
    down = lax.broadcasted_iota(jnp.int32, (rows, rows), 0)
    across = lax.broadcasted_iota(jnp.int32, (rows, rows), 1)
    same = (down == across).astype(jnp.float32)
    slots = experts * CAP
    slot_row = lax.broadcasted_iota(jnp.int32, (slots, rows), 0)
    slot_column = lax.broadcasted_iota(jnp.int32, (rows, slots), 1)
    placing = jnp.zeros((slots, rows), jnp.float32)
    share = jnp.zeros((rows, slots), jnp.float32)
    for k in range(experts):
        expert = lax.rem(block + k, experts)
        hit = routes == expert
        has = jnp.sum(hit.astype(jnp.float32), axis=1, keepdims=True)
        weight = jnp.sum(jnp.where(hit, gates, 0.0), axis=1, keepdims=True)
        has_row = jnp.sum(has * same, axis=0, keepdims=True)
        before_row = jnp.sum(jnp.where(down < across, has, 0.0), axis=0, keepdims=True)
        before = jnp.sum(jnp.where(across < down, has_row, 0.0), axis=1, keepdims=True)
        for c in range(CAP):
            slot = k * CAP + c
            placing += jnp.where((slot_row == slot) & (before_row == c), has_row, 0.0)
            share += jnp.where((slot_column == slot) & (before == c), weight, 0.0)
    for k in range(experts):
        out_refs[k][...] = jnp.dot(
            placing[k * CAP : (k + 1) * CAP].astype(jnp.bfloat16),
            tokens_ref[...],
            preferred_element_type=jnp.float32,
        ).astype(jnp.bfloat16)
    out_refs[experts][...] = share


def dispatch(block, routes, gates, tokens, experts):
    slots = experts * CAP
    return pl.pallas_call(
        functools.partial(dispatch_kernel, experts),
        out_shape=(
            *(jax.ShapeDtypeStruct((CAP, tokens.shape[1]), tokens.dtype) for _ in range(experts)),
            jax.ShapeDtypeStruct((tokens.shape[0], slots), jnp.float32),
        ),
        in_specs=[pl.BlockSpec(memory_space=pltpu.SMEM)]
        + [pl.BlockSpec(memory_space=pltpu.VMEM)] * 3,
        out_specs=(pl.BlockSpec(memory_space=pltpu.VMEM),) * (experts + 1),
        cost_estimate=SMALL,
        compiler_params=pltpu.CompilerParams(vmem_limit_bytes=8 * 1024 * 1024),
        name="dispatch",
    )(block, routes, gates, tokens)


def moved_rows(pieces, places, rows):
    total = None
    for piece, places_of_piece in zip(pieces, places):
        shape = (rows, piece.shape[0])
        row = lax.broadcasted_iota(jnp.int32, shape, 0)
        column = lax.broadcasted_iota(jnp.int32, shape, 1)
        chosen = jnp.zeros(shape, jnp.float32)
        for source, there in places_of_piece:
            chosen += ((row == there) & (column == source)).astype(jnp.float32)
        part = jnp.dot(
            chosen.astype(jnp.bfloat16), piece[...], preferred_element_type=jnp.float32
        )
        total = part if total is None else total + part
    return total.astype(jnp.bfloat16)


def stack_kernel(*refs):
    arrays, out_ref = refs[:-1], refs[-1]
    places, start = [], 0
    for array in arrays:
        places.append([(r, start + r) for r in range(array.shape[0])])
        start += array.shape[0]
    out_ref[...] = moved_rows(arrays, places, start)


def stack_rows(*arrays):
    rows = sum(array.shape[0] for array in arrays)
    return pl.pallas_call(
        stack_kernel,
        out_shape=jax.ShapeDtypeStruct((rows, arrays[0].shape[1]), arrays[0].dtype),
        in_specs=[pl.BlockSpec(memory_space=pltpu.VMEM)] * len(arrays),
        out_specs=pl.BlockSpec(memory_space=pltpu.VMEM),
        cost_estimate=SMALL,
        compiler_params=pltpu.CompilerParams(vmem_limit_bytes=8 * 1024 * 1024),
        name="stack_rows",
    )(*arrays)


def experts_kernel(count, *refs):
    row_refs, (gate_hbm, up_hbm, down_hbm) = refs[:count], refs[count : count + 3]
    out_refs = refs[count + 3 : 2 * count + 3]
    gate_ref, up_ref, down_ref, sems = refs[2 * count + 3 :]
    copies = [
        pltpu.make_async_copy(source.at[0], there, sems.at[i])
        for i, (source, there) in enumerate(
            ((gate_hbm, gate_ref), (up_hbm, up_ref), (down_hbm, down_ref))
        )
    ]
    for copy in copies:
        copy.start()
    rows = jnp.concatenate([ref[...].astype(jnp.float32) for ref in row_refs], axis=0)
    rows = rows.astype(jnp.bfloat16)
    copies[0].wait()
    gate = jnp.dot(rows, gate_ref[...], preferred_element_type=jnp.float32)
    copies[1].wait()
    lifted = jnp.dot(rows, up_ref[...], preferred_element_type=jnp.float32)
    hidden = (gate / (1.0 + jnp.exp(-gate)) * lifted).astype(jnp.bfloat16)
    copies[2].wait()
    parts = jnp.dot(hidden, down_ref[...], preferred_element_type=jnp.float32)
    for i, (row_ref, out_ref) in enumerate(zip(row_refs, out_refs)):
        size = row_ref.shape[0]
        out_ref[...] = parts[i * size : (i + 1) * size].astype(out_ref.dtype)


def run_experts(groups, w_gate, w_up, w_down):
    count = len(groups)
    vmem = pl.BlockSpec(memory_space=pltpu.VMEM)
    return pl.pallas_call(
        functools.partial(experts_kernel, count),
        out_shape=tuple(
            jax.ShapeDtypeStruct(x.shape, jnp.bfloat16 if i else jnp.float32)
            for i, x in enumerate(groups)
        ),
        in_specs=[vmem] * count + [pl.BlockSpec(memory_space=pltpu.HBM)] * 3,
        out_specs=(vmem,) * count,
        scratch_shapes=[
            pltpu.VMEM(w_gate.shape[1:], w_gate.dtype),
            pltpu.VMEM(w_up.shape[1:], w_up.dtype),
            pltpu.VMEM(w_down.shape[1:], w_down.dtype),
            pltpu.SemaphoreType.DMA((3,)),
        ],
        cost_estimate=SMALL,
        compiler_params=pltpu.CompilerParams(vmem_limit_bytes=16 * 1024 * 1024),
        name="experts",
    )(*groups, w_gate, w_up, w_down)


def combine_kernel(ways, share_ref, *refs):
    pieces, out_ref = refs[:-1], refs[-1]
    sums = {}
    for (k, _), piece in zip(ways, pieces):
        rows = piece[...].astype(jnp.float32)
        sums[k] = sums[k] + rows if k in sums else rows
    total = None
    for k, rows in sums.items():
        for c in range(CAP):
            slot = k * CAP + c
            part = share_ref[:, slot : slot + 1] * rows[c : c + 1, :]
            total = part if total is None else total + part
    out_ref[...] = total.astype(jnp.bfloat16)


def combine(ways, share, pieces):
    vmem = pl.BlockSpec(memory_space=pltpu.VMEM)
    return pl.pallas_call(
        functools.partial(combine_kernel, tuple(ways)),
        out_shape=jax.ShapeDtypeStruct((share.shape[0], pieces[0].shape[1]), jnp.bfloat16),
        in_specs=[vmem] * (1 + len(pieces)),
        out_specs=vmem,
        cost_estimate=SMALL,
        compiler_params=pltpu.CompilerParams(vmem_limit_bytes=8 * 1024 * 1024),
        name="combine",
    )(share, *pieces)


def on_device(
    latent_cache,
    rope_cache,
    q_latent,
    q_rope,
    new_latent,
    new_rope,
    branch_slot,
    moe_input,
    routes,
    route_gate,
    w_gate,
    w_up,
    w_down,
):
    tok_rows, step_count, head_count, width = q_latent.shape
    rope_width = new_rope.shape[-1]
    line = tok_rows // 2
    q_rows = step_count * head_count
    half = latent_cache.shape[1]
    rope_rows = rope_cache.shape[1]
    branch = lax.axis_index("branch")
    own = branch % tok_rows
    low = own % 2
    high = own // 2
    middle = jnp.logical_and(high > 0, high < line - 1)

    outer = [(i, i ^ 1) for i in range(line)]
    inner = [(i, i + 1) for i in range(1, line - 1, 2)]
    inner = inner + [(j, i) for i, j in inner]
    outward = [(i, i ^ 1) for i in range(1, line - 1)]
    own_cache = pack_cache(latent_cache[0], rope_cache[0])
    cache_a = line_hop(own_cache, tok_rows, outer)
    first_b = line_hop(own_cache, tok_rows, inner)

    q_lat = q_latent.reshape(tok_rows, q_rows, width)
    rope_raw = q_rope.reshape(tok_rows, q_rows * rope_width // width, width)
    fresh = jnp.concatenate(
        [
            jnp.pad(new_latent, ((0, 0), (0, PAD - step_count), (0, 0))),
            jnp.pad(new_rope, ((0, 0), (0, PAD - step_count), (0, width - rope_width))),
        ],
        axis=1,
    )
    scalars = (branch_slot, own[None])
    sources = (q_lat, rope_raw, fresh)
    leave = pack_tokens(1, branch_slot, after(own[None], own_cache), *sources)
    guest = swapped(leave, "branch", 0)
    stay = pack_tokens(0, branch_slot, after(own[None], leave), *sources)
    attend = build_attend(head_count, step_count, width, half, rope_rows, 32, half // 2)
    model_width = moe_input.shape[-1]
    tok_total = tok_rows * step_count
    device = branch * lax.axis_size("expert") + lax.axis_index("expert")
    experts = lax.axis_size("branch") * lax.axis_size("expert") // SHARDS
    cores = lax.axis_size("expert")
    shard_branches = SHARDS // cores
    block = device // SHARDS
    *outgoing, share = dispatch(
        after(block[None], leave),
        routes.reshape(tok_total, -1),
        route_gate.reshape(tok_total, -1),
        moe_input.reshape(tok_total, model_width),
        experts,
    )

    around = shard_branches // 2

    def along(x, shift, flip):
        count = lax.axis_size("branch")
        there = [
            ((i // shard_branches + shift) % experts) * shard_branches
            + ((i % shard_branches) ^ (flip * 2))
            for i in range(count)
        ]
        return lax.ppermute(x, "branch", list(enumerate(there)))

    ways = [(k, m) for m in range(around) for k in range(experts)]
    pieces = outgoing[:1] + [along(outgoing[k], k, 0) for k in range(1, experts)]
    cache_a, first_b, stay, *pieces = lax.optimization_barrier(
        (cache_a, first_b, stay, *pieces)
    )
    second_b = line_hop(first_b, tok_rows, outward)
    first_c = line_hop(cache_a, tok_rows, inner)

    def both_halves(cache):
        return cache, swapped(cache, "expert", 0)

    guest = after(guest, cache_a, first_b)
    given_0, placed = attend(scalars, 0, guest, stay, both_halves(own_cache), None)
    back_0 = swapped(given_0, "branch", 0)
    rows = stack_rows(*lax.optimization_barrier((given_0, *pieces))[1:])
    rows = [rows] + [along(rows, 0, m) for m in range(1, around)]
    given_1, placed = attend(scalars, 1, guest, stay, both_halves(cache_a), placed)
    back_1 = swapped(given_1, "branch", 0)

    first_c, given_1, back_0, first_b, *rows = lax.optimization_barrier(
        (first_c, given_1, back_0, first_b, *rows)
    )
    second_c = line_hop(first_c, tok_rows, outward)
    cache_b = jnp.where(middle, first_b, second_b)
    given_2, placed = attend(scalars, 2, guest, stay, both_halves(cache_b), placed)
    back_2 = swapped(given_2, "branch", 0)
    rows = stack_rows(*rows)

    def around_chip(x, i):
        pairs = []
        for there in range(lax.axis_size("branch") * cores):
            row, core = there // cores, there % cores
            pairs.append((there, (row ^ (i & 1)) * cores + (core ^ (i >> 1))))
        return lax.ppermute(x, ("branch", "expert"), pairs)

    groups = [rows] + [around_chip(rows, i) for i in range(1, 2 * cores)]
    groups = lax.optimization_barrier((given_2, *groups))[1:]
    parts, *others = run_experts(groups, w_gate, w_up, w_down)
    others = [around_chip(x, i + 1) for i, x in enumerate(others)]

    second_c, back_1, parts, *others = lax.optimization_barrier(
        (second_c, back_1, parts, *others)
    )
    for other in others:
        parts = parts + other.astype(jnp.float32)
    cache_c = both_halves(jnp.where(middle, first_c, second_c))
    homeward = [
        parts[w * CAP : (w + 1) * CAP].astype(jnp.float32 if way == (0, 0) else jnp.bfloat16)
        for w, way in enumerate(ways)
    ]
    homeward = [
        piece if (k, m) == (0, 0) else along(piece, -k, m)
        for (k, m), piece in zip(ways, homeward)
    ]
    guest, back_2 = lax.optimization_barrier((guest, back_2))
    (given_3,) = attend(scalars, 3, guest, None, cache_c, None)
    back_3 = swapped(given_3, "branch", 0)
    (placed,) = attend(scalars, 3, None, after(stay, given_3), cache_c, placed)
    placed, *homeward = lax.optimization_barrier((placed, *homeward))
    placed = place(scalars, (back_0, back_1, back_2, back_3), placed)
    attended = placed.reshape(tok_rows, step_count, head_count, width)

    combined = combine(ways, share, homeward)
    moe_out = combined.reshape(tok_rows, step_count, model_width)
    return (attended, moe_out)


def solution(mesh):
    return jax.shard_map(
        on_device,
        mesh=mesh,
        in_specs=(
            P(("group", "branch"), "expert", None),
            P(("group", "branch"), "expert", None),
            P(("group", "branch", "expert"), None, None, None),
            P(("group", "branch", "expert"), None, None),
            P(("group", "branch", "expert"), None, None),
            P(("group", "branch", "expert"), None, None),
            P(("group", "branch", "expert")),
            P(("group", "branch", "expert"), None, None),
            P(("group", "branch", "expert"), None, None),
            P(("group", "branch", "expert"), None, None),
            P(("branch", "expert"), None, None),
            P(("branch", "expert"), None, None),
            P(("branch", "expert"), None, None),
        ),
        out_specs=(
            P(("group", "branch", "expert"), None, None, None),
            P(("group", "branch", "expert"), None, None),
        ),
        check_vma=False,
    )
```
